32 devices in a mesh: group: 2 (over x), node: 8 (over z, y), head: 2 (over core).
Axes of the slice: x: 2, y: 2, z: 4, core: 2. Of those that a mesh axis runs over, the one named last changes fastest.
Arguments:
- queries_one: bfloat16 [16, 128, 64, 128], P(('group', 'node'), None, 'head'), parts along dimension 0, may hold values from -80 to 80
- keys_one: bfloat16 [16, 128, 8, 128], P(('group', 'node'), None, 'head'), parts along dimension 0, may hold values from -8 to 8
- values_one: bfloat16 [16, 128, 8, 128], P(('group', 'node'), None, 'head'), parts along dimension 0, may hold values from -6 to 6
- queries_two: bfloat16 [16, 128, 64, 128], P(('group', 'node'), None, 'head'), parts along dimension 0, may hold values from -80 to 80
- keys_two: bfloat16 [16, 128, 8, 128], P(('group', 'node'), None, 'head'), parts along dimension 0, may hold values from -8 to 8
- values_two: bfloat16 [16, 128, 8, 128], P(('group', 'node'), None, 'head'), parts along dimension 0, may hold values from -6 to 6
- cache_keys: bfloat16 [512, 128, 8, 128], P(('group', 'node'), None, 'head'), parts along dimension 0, may hold values from -8 to 8
- cache_values: bfloat16 [512, 128, 8, 128], P(('group', 'node'), None, 'head'), parts along dimension 0, may hold values from -6 to 6
- paths: int32 [16, 32], P('group'), parts along dimension 0, may hold values from 0 to 255, as said below
- parents: int32 [16], P('group'), parts along dimension 0, may hold values from 0 to 7
- positions: int32 [2, 16, 128], P(None, ('group', 'node')), parts along dimension 1, may hold values from 0 to 8446, as said below
Outputs:
- attended_one: bfloat16 [16, 128, 64, 128], P(('group', 'node'), None, 'head'), parts along dimension 0
- attended_two: bfloat16 [16, 128, 64, 128], P(('group', 'node'), None, 'head'), parts along dimension 0
The draws below stay inside these ranges and needn't reach their ends.
There are 2 independent parts, one for each index of `group`. The reference program is written for one: setup_inputs(seed, part) draws one part's arguments, and reference() takes and returns one part's arrays. A program takes and returns all parts, laid end to end along the dimension named above; each array names one. Nothing has to cross between parts.
Inputs may be any that keep to these rules, and one draw needn't show every extreme that they name: Each row paths[c] names 32 different cache blocks. Block b lies on device b // 32 of node, and each row names exactly 4 blocks of every device of node. positions[d, c, t] = s + (32 + d) * 128 + t, with one offset s of 0 to 4095 for a tree.
All inputs are finite; a program needn't handle non-finite values.
Results may differ from the reference program's by a relative error of at most 0.012.
The reference program's roundings to bfloat16 on the way (of `query_rot_one`, `key_rot_one`, `query_rot_two` and `key_rot_two`) count: a program that leaves them out, or rounds other values in their place, can miss the bound.
Values may be sent and summed in bfloat16 or wider, within the bound.
No kernel may reach another device: no remote copies, remote signals or barrier semaphores. Data moves between devices by JAX's collectives and lax.ppermute only.
A program may use at most 128 MiB of HBM per device.

```python
import jax
import jax.numpy as jnp
from jax import lax

QH = 64
KVH = 8
HD = 128
BLK = 128
ANC = 32
NEW = 8
NB = 256


def draw_queries_one(key, part):
    key = jax.random.fold_in(key, 1)
    array_shape = (NEW, BLK, QH, HD)
    return (2.0 * jax.random.truncated_normal(key, -4.0, 4.0, array_shape, jnp.float32)).astype(jnp.bfloat16)


def draw_queries_two(key, part):
    key = jax.random.fold_in(key, 2)
    array_shape = (NEW, BLK, QH, HD)
    return (2.0 * jax.random.truncated_normal(key, -4.0, 4.0, array_shape, jnp.float32)).astype(jnp.bfloat16)


def draw_keys_one(key, part):
    key = jax.random.fold_in(key, 3)
    array_shape = (NEW, BLK, KVH, HD)
    return (1.25 * jax.random.truncated_normal(key, -4.0, 4.0, array_shape, jnp.float32)).astype(jnp.bfloat16)


def draw_keys_two(key, part):
    key = jax.random.fold_in(key, 4)
    array_shape = (NEW, BLK, KVH, HD)
    return (1.25 * jax.random.truncated_normal(key, -4.0, 4.0, array_shape, jnp.float32)).astype(jnp.bfloat16)


def draw_cache_keys(key, part):
    key = jax.random.fold_in(key, 5)
    array_shape = (ANC * NEW, BLK, KVH, HD)
    return (1.25 * jax.random.truncated_normal(key, -4.0, 4.0, array_shape, jnp.float32)).astype(jnp.bfloat16)


def draw_paths(key, part):
    key = jax.random.fold_in(key, 6)
    key_levels, key_spans, key_slots = jax.random.split(key, 3)
    middle_order = (jax.random.permutation(key_levels, ANC - 2) + 1).astype(jnp.int32)
    level_order = jnp.concatenate([middle_order, jnp.zeros((1,), jnp.int32), jnp.full((1,), ANC - 1, jnp.int32)]).astype(jnp.int32)
    owner_device = level_order % NEW
    slot_rank = level_order // NEW
    span_order = jax.random.permutation(key_spans, NEW).astype(jnp.int32)
    levels = jnp.arange(ANC, dtype=jnp.int32)
    branch_count = jnp.minimum(NEW, 2 ** jnp.minimum(levels * 5 // ANC, 20))
    branch_width = NEW // branch_count
    branch = span_order[:, None] // branch_width[None, :]
    local_perms = jax.vmap(lambda slot_key: jax.random.permutation(slot_key, NEW).astype(jnp.int32))(jax.random.split(key_slots, NEW))
    local_block = slot_rank[None, :] * NEW + local_perms[owner_device[None, :], branch]
    block_ids = owner_device[None, :] * ANC + local_block
    return block_ids.astype(jnp.int32)


def draw_positions(key, part):
    key = jax.random.fold_in(key, 7)
    start_offset = jax.random.randint(key, (), 0, 4096, jnp.int32)
    depth_index = jnp.arange(2, dtype=jnp.int32)[:, None, None]
    token_index = jnp.arange(BLK, dtype=jnp.int32)[None, None, :]
    span_zero = jnp.zeros((1, NEW, 1), jnp.int32)
    return (start_offset + (ANC + depth_index) * BLK + token_index + span_zero).astype(jnp.int32)


def set_ends(values, key, least, top_value):
    place = [jax.random.randint(jax.random.fold_in(key, axis), (), 0, length) for axis, length in enumerate(values.shape)]
    widest = values.shape.index(max(values.shape))
    next_to = place[:widest] + [(place[widest] + 1) % values.shape[widest]] + place[widest + 1:]
    return values.at[tuple(place)].set(least).at[tuple(next_to)].set(top_value)


def shard_levels(key, dims, shards, low, largest):
    gain = 1.0
    for position, blocks in shards:
        heights = jax.random.uniform(jax.random.fold_in(jax.random.fold_in(key, 6), position), (blocks,), jnp.float32, low / len(shards), largest / len(shards))
        gain = gain * jnp.repeat(jnp.exp(heights), dims[position] // blocks).reshape((-1,) + (1,) * (len(dims) - 1 - position))
    return gain


def gaussian(key, extent, scale, reach, shards=(), kind=jnp.bfloat16):
    factor_of = shard_levels(key, extent, shards, -0.22, 0.18) if shards else 1.0
    entries = jax.random.normal(key, extent, jnp.float32) * scale * factor_of
    return jnp.minimum(jnp.maximum(entries, -reach), reach).astype(kind)


def setup_inputs(seed: int = 0, part: int = 0) -> dict:
    keys = jax.random.split(jax.random.key(seed), 12)
    part_splits = jax.random.split(jax.random.fold_in(keys[11], part), 12)
    return {
        "queries_one": draw_queries_one(jax.random.fold_in(jax.random.fold_in(keys[11], part), 71), part),
        "keys_one": draw_keys_one(jax.random.fold_in(jax.random.fold_in(keys[11], part), 71), part),
        "values_one": gaussian(part_splits[2], (NEW, BLK, KVH, HD), 1.0, 6.0, ((0, 8), (2, 2))),
        "queries_two": draw_queries_two(jax.random.fold_in(jax.random.fold_in(keys[11], part), 71), part),
        "keys_two": draw_keys_two(jax.random.fold_in(jax.random.fold_in(keys[11], part), 71), part),
        "values_two": gaussian(part_splits[5], (NEW, BLK, KVH, HD), 1.0, 6.0, ((0, 8), (2, 2))),
        "cache_keys": draw_cache_keys(jax.random.fold_in(jax.random.fold_in(keys[11], part), 71), part),
        "cache_values": gaussian(part_splits[7], (NB, BLK, KVH, HD), 1.0, 6.0, ((0, 8), (2, 2))),
        "paths": draw_paths(jax.random.fold_in(jax.random.fold_in(keys[11], part), 71), part),
        "parents": set_ends(jax.random.randint(part_splits[9], (NEW,), 0, NEW), jax.random.fold_in(part_splits[9], 1), 0, NEW - 1).astype(jnp.int32),
        "positions": draw_positions(jax.random.fold_in(jax.random.fold_in(keys[11], part), 71), part),
    }


rope_theta = 500000.0


def rotary(vector, position_row):
    head_width = vector.shape[-1]
    half_width = head_width // 2
    frequency = rope_theta ** (-(jnp.arange(half_width, dtype=jnp.float32) * 2.0) / head_width)
    angles = position_row.astype(jnp.float32)[:, None] * frequency[None, :]
    cosine = jnp.cos(angles)[:, None, :]
    sine_part = jnp.sin(angles)[:, None, :]
    widened = vector.astype(jnp.float32)
    first_half = widened[..., :half_width]
    second_half = widened[..., half_width:]
    turned = jnp.concatenate([first_half * cosine - second_half * sine_part, second_half * cosine + first_half * sine_part], -1)
    return turned.astype(jnp.bfloat16)


def attend(query, key_rows, value_rows, score_scale):
    row_count, head_count, head_width = query.shape
    key_count = key_rows.shape[0]
    kv_count = key_rows.shape[1]
    group_size = head_count // kv_count
    grouped = jnp.moveaxis(query.reshape(row_count, kv_count, group_size, head_width), 0, 2)
    key_heads = jnp.moveaxis(key_rows, 1, 0)
    value_heads = jnp.moveaxis(value_rows, 1, 0)
    token_index = lax.broadcasted_iota(jnp.int32, (row_count, key_count), 0)
    key_index = lax.broadcasted_iota(jnp.int32, (row_count, key_count), 1)
    visible = key_index - (key_count - row_count) <= token_index

    def one_head(operands):
        query_head, key_head, value_head = operands
        scores = jnp.einsum("gtd,sd->gts", query_head.astype(jnp.float32), key_head.astype(jnp.float32), precision=lax.Precision.HIGHEST) * score_scale
        scores = jnp.where(visible[None], scores, -1e30)
        row_max = jnp.max(scores, axis=-1, keepdims=True)
        weights = jnp.exp(scores - row_max)
        total_weight = jnp.sum(weights, axis=-1, keepdims=True)
        rounded = lax.optimization_barrier(weights.astype(jnp.bfloat16)).astype(jnp.float32)
        mixture = jnp.einsum("gts,sd->gtd", rounded, value_head.astype(jnp.float32), precision=lax.Precision.HIGHEST)
        return (mixture / total_weight).astype(jnp.bfloat16)

    result = lax.map(one_head, (grouped, key_heads, value_heads))
    return jnp.moveaxis(result, 2, 0).reshape(row_count, head_count, head_width)


def reference(queries_one, keys_one, values_one, queries_two, keys_two, values_two, cache_keys, cache_values, paths, parents, positions):
    score_scale = HD ** -0.5
    query_rot_one = jax.vmap(rotary)(queries_one, positions[0])
    key_rot_one = jax.vmap(rotary)(keys_one, positions[0])
    query_rot_two = jax.vmap(rotary)(queries_two, positions[1])
    key_rot_two = jax.vmap(rotary)(keys_two, positions[1])

    def path_blocks(cache, path_row):
        return cache[path_row].reshape(ANC * BLK, KVH, HD)

    def depth_one(span_index):
        path_row = paths[span_index]
        key_rows = jnp.concatenate([path_blocks(cache_keys, path_row), key_rot_one[span_index]], 0)
        value_rows = jnp.concatenate([path_blocks(cache_values, path_row), values_one[span_index]], 0)
        return attend(query_rot_one[span_index], key_rows, value_rows, score_scale)

    def depth_two(span_index):
        parent = parents[span_index]
        path_row = paths[parent]
        key_rows = jnp.concatenate([path_blocks(cache_keys, path_row), key_rot_one[parent], key_rot_two[span_index]], 0)
        value_rows = jnp.concatenate([path_blocks(cache_values, path_row), values_one[parent], values_two[span_index]], 0)
        return attend(query_rot_two[span_index], key_rows, value_rows, score_scale)

    span_ids = jnp.arange(NEW, dtype=jnp.int32)
    attended_one = lax.map(depth_one, span_ids)
    attended_two = lax.map(depth_two, span_ids)
    return attended_one, attended_two
```

```python
import functools

import jax
import jax.numpy as jnp
from jax import lax
from jax.experimental import pallas as pl
from jax.experimental.pallas import tpu as pltpu
from jax.sharding import PartitionSpec as P

rope_theta = 500000.0
log2_e = 1.4426950408889634
stat_rows = 32
row_tile = 256
vmem_bytes = 56 * 1024 * 1024


def rotary(vector, position_row):
    head_width = vector.shape[-1]
    half_width = head_width // 2
    frequency = rope_theta ** (-(jnp.arange(half_width, dtype=jnp.float32) * 2.0) / head_width)
    angles = position_row.astype(jnp.float32)[:, None] * frequency[None, :]
    cosine = jnp.cos(angles)[:, None, :]
    sine_part = jnp.sin(angles)[:, None, :]
    widened = vector.astype(jnp.float32)
    first_half = widened[..., :half_width]
    second_half = widened[..., half_width:]
    turned = jnp.concatenate(
        [
            first_half * cosine - second_half * sine_part,
            second_half * cosine + first_half * sine_part,
        ],
        -1,
    )
    return turned.astype(jnp.bfloat16)


def local_blocks(paths, here_index, per_owner, per_peer):
    is_local = paths // per_owner == here_index
    slot_rank = jnp.cumsum(is_local.astype(jnp.int32), axis=1) - 1
    slot_range = jnp.arange(per_peer, dtype=jnp.int32)
    selected = jnp.logical_and(
        is_local[:, :, None], slot_rank[:, :, None] == slot_range[None, None, :]
    )
    return jnp.sum(jnp.where(selected, (paths % per_owner)[:, :, None], 0), axis=1)


def pack_kernel(per_peer, head_count, token_count, with_new, index_ref, head_ref, *refs):
    key_refs = refs[:per_peer]
    value_refs = refs[per_peer : 2 * per_peer]
    refs = refs[2 * per_peer :]
    new_refs = ()
    if with_new:
        new_refs, refs = refs[:2], refs[2:]
    out_refs, wide = refs[:head_count], refs[head_count]
    step = pl.program_id(0)
    mine = head_ref[0]
    span_rows = 2 * per_peer * token_count

    def spread(rows, offset):
        wide[...] = rows.astype(jnp.float32)
        for far in range(head_count):
            head = lax.bitwise_xor(mine, far)
            picked = wide[pl.ds(head, token_count, stride=head_count), :]
            out_refs[far][pl.ds(offset, token_count), :] = picked.astype(jnp.bfloat16)

    for which, source_refs in enumerate((key_refs, value_refs)):
        for slot, source in enumerate(source_refs):
            offset = step * span_rows + (which * per_peer + slot) * token_count
            spread(source[0], pl.multiple_of(offset, token_count))
    if with_new:

        @pl.when(step == 0)
        def _():
            base = pl.num_programs(0) * span_rows
            for which, source in enumerate(new_refs):
                spread(source[...], pl.multiple_of(base + which * token_count, token_count))


def pack(cache_keys, cache_values, block_index, head_index, new_rows, per_peer):
    block_count, token_count, head_count, width = cache_keys.shape
    path_count = block_index.shape[0]
    flat_keys = cache_keys.reshape(block_count, token_count * head_count, width)
    flat_values = cache_values.reshape(block_count, token_count * head_count, width)
    span_rows = 2 * per_peer * token_count
    out_rows = path_count * span_rows + (2 * token_count if new_rows else 0)

    def block_spec(slot):
        return pl.BlockSpec(
            (1, token_count * head_count, width),
            lambda step, index, head: (index[step * per_peer + slot], 0, 0),
        )

    cache_specs = [block_spec(slot) for slot in range(per_peer)]
    new_spec = pl.BlockSpec((token_count * head_count, width), lambda step, index, head: (0, 0))
    operands = [flat_keys] * per_peer + [flat_values] * per_peer
    operands += [row.reshape(token_count * head_count, width) for row in new_rows]
    return pl.pallas_call(
        functools.partial(pack_kernel, per_peer, head_count, token_count, bool(new_rows)),
        grid_spec=pltpu.PrefetchScalarGridSpec(
            num_scalar_prefetch=2,
            grid=(path_count,),
            in_specs=cache_specs + cache_specs + [new_spec] * len(new_rows),
            out_specs=[pl.BlockSpec((out_rows, width), lambda step, index, head: (0, 0))]
            * head_count,
            scratch_shapes=[pltpu.VMEM((token_count * head_count, width), jnp.float32)],
        ),
        out_shape=[jax.ShapeDtypeStruct((out_rows, width), jnp.bfloat16)] * head_count,
        compiler_params=pltpu.CompilerParams(vmem_limit_bytes=vmem_bytes),
        cost_estimate=pl.CostEstimate(
            flops=0, bytes_accessed=4 * head_count * out_rows * width, transcendentals=0
        ),
        name="pack_rows",
    )(block_index.reshape(-1), head_index, *operands)


def eye(size):
    return lax.broadcasted_iota(jnp.int32, (size, size), 0) == lax.broadcasted_iota(
        jnp.int32, (size, size), 1
    )


def product(left, right):
    return lax.dot_general(
        left, right, (((1,), (1,)), ((), ())), preferred_element_type=jnp.float32
    )


def attend_rows(query, key_parts, value_parts, mask, score_scale):
    scores = [product(query, keys) for keys in key_parts]
    if mask is not None:
        scores[-1] = jnp.where(mask, scores[-1], -1e30)
    row_max = functools.reduce(
        jnp.maximum, [jnp.max(part, axis=-1, keepdims=True) for part in scores]
    )
    total = jnp.zeros_like(row_max)
    mixture = jnp.zeros((query.shape[0], value_parts[0].shape[-1]), jnp.float32)
    for part, values in zip(scores, value_parts):
        weights = jnp.exp2((part - row_max) * (score_scale * log2_e))
        total = total + jnp.sum(weights, axis=-1, keepdims=True)
        mixture = mixture + jnp.dot(
            weights.astype(jnp.bfloat16), values, preferred_element_type=jnp.float32
        )
    return mixture / total, row_max * score_scale + jnp.log(total)


def store_partial(out_ref, tile, mixture, level, lanes):
    rows = mixture.shape[0]
    out_ref[0, pl.ds(pl.multiple_of(tile * rows, rows), rows), :] = mixture.astype(jnp.bfloat16)
    picks = eye(lanes)
    flat = [
        jnp.sum(
            jnp.where(picks, level[part * lanes : (part + 1) * lanes], 0.0), axis=0, keepdims=True
        )
        for part in range(rows // lanes)
    ]
    return flat


def store_stats(out_ref, levels):
    row_count = out_ref.shape[1] - stat_rows
    high = levels.astype(jnp.bfloat16).astype(jnp.float32)
    middle = (levels - high).astype(jnp.bfloat16).astype(jnp.float32)
    low = levels - high - middle
    stats = jnp.concatenate([high, middle, low, jnp.zeros_like(levels)], 0)
    out_ref[0, pl.ds(row_count, stat_rows), :] = stats.astype(jnp.bfloat16)


def attend_task(query_ref, out_ref, level_ref, key_parts, value_parts, mask_of, score_scale):
    row_count = out_ref.shape[1] - stat_rows
    lanes = out_ref.shape[2]
    per_tile = row_tile // lanes

    def tile_step(tile, carry):
        query = query_ref[0, pl.ds(pl.multiple_of(tile * row_tile, row_tile), row_tile), :]
        mixture, level = attend_rows(
            query,
            [read() for read in key_parts],
            [read() for read in value_parts],
            None if mask_of is None else mask_of(tile),
            score_scale,
        )
        flat = store_partial(out_ref, tile, mixture, level, lanes)
        for part in range(per_tile):
            level_ref[pl.ds(tile * per_tile + part, 1), :] = flat[part]
        return carry

    lax.fori_loop(0, row_count // row_tile, tile_step, 0)
    store_stats(out_ref, level_ref[...])


def part_readers(refs, part_rows):
    keys = [functools.partial(lambda ref: ref[pl.ds(0, part_rows), :], ref) for ref in refs]
    values = [
        functools.partial(lambda ref: ref[pl.ds(part_rows, part_rows), :], ref) for ref in refs
    ]
    return keys, values


def first_kernel(source_count, part_rows, score_scale, has_base, query_ref, *refs):
    source_refs = refs[:source_count]
    out_ref, level_ref = refs[source_count + has_base :]
    keys, values = part_readers(source_refs, part_rows)
    attend_task(query_ref, out_ref, level_ref, keys, values, None, score_scale)


def attend_first(queries, sources, base, first_path, path_count, part_rows, score_scale):
    span_count, row_count, width = queries.shape
    span_rows = 2 * part_rows
    out_shape = jax.ShapeDtypeStruct((span_count, row_count + stat_rows, width), jnp.bfloat16)
    has_base = int(base is not None)
    operands = [queries, *sources] + ([base] if has_base else [])
    keys = len(sources) * part_rows
    return pl.pallas_call(
        functools.partial(first_kernel, len(sources), part_rows, score_scale, has_base),
        grid=(path_count,),
        in_specs=[pl.BlockSpec((1, row_count, width), lambda step: (first_path + step, 0, 0))]
        + [pl.BlockSpec((span_rows, width), lambda step: (step, 0))] * len(sources)
        + [pl.BlockSpec(memory_space=pl.ANY)] * has_base,
        out_specs=pl.BlockSpec(
            (1, row_count + stat_rows, width), lambda step: (first_path + step, 0, 0)
        ),
        out_shape=out_shape,
        scratch_shapes=[pltpu.VMEM((row_count // width, width), jnp.float32)],
        input_output_aliases={len(operands) - 1: 0} if has_base else {},
        compiler_params=pltpu.CompilerParams(vmem_limit_bytes=vmem_bytes),
        cost_estimate=pl.CostEstimate(
            flops=8 * path_count * row_count * keys * width,
            bytes_accessed=4 * path_count * (row_count + keys) * width,
            transcendentals=path_count * row_count * keys,
        ),
        name="attend_first",
    )(*operands)


def second_kernel(
    chunk_count, source_count, chunk_paths, part_rows, score_scale, parent_ref, group_ref, *refs
):
    query_ref = refs[0]
    source_refs = refs[1 : 1 + chunk_count * source_count]
    out_ref, level_ref, held, fresh, semaphores = refs[1 + chunk_count * source_count :]
    span_rows = 2 * part_rows
    token_count = fresh.shape[1] // 2
    step = pl.program_id(0)

    def copies():
        out = []
        for chunk in range(chunk_count):
            for source in range(source_count):
                ref = source_refs[chunk * source_count + source]
                for path in range(chunk_paths):
                    out.append(
                        pltpu.make_async_copy(
                            ref.at[pl.ds(path * span_rows, span_rows)],
                            held.at[source, chunk * chunk_paths + path],
                            semaphores.at[len(out)],
                        )
                    )
        for source in range(source_count):
            ref = source_refs[(chunk_count - 1) * source_count + source]
            out.append(
                pltpu.make_async_copy(
                    ref.at[pl.ds(chunk_paths * span_rows, 2 * token_count)],
                    fresh.at[source],
                    semaphores.at[len(out)],
                )
            )
        return out

    @pl.when(step == 0)
    def _():
        moves = copies()
        for move in moves:
            move.start()
        for move in moves:
            move.wait()

    parent = parent_ref[step]
    home = parent // source_count
    present = home == group_ref[0]
    slot = lax.bitwise_xor(parent % source_count, group_ref[1])
    keys = [
        functools.partial(lambda source: held[source, parent, pl.ds(0, part_rows), :], source)
        for source in range(source_count)
    ]
    values = [
        functools.partial(
            lambda source: held[source, parent, pl.ds(part_rows, part_rows), :], source
        )
        for source in range(source_count)
    ]
    keys.append(lambda: fresh[slot, pl.ds(0, token_count), :])
    values.append(lambda: fresh[slot, pl.ds(token_count, token_count), :])

    def mask_of(tile):
        return jnp.broadcast_to(present, (row_tile, token_count))

    attend_task(query_ref, out_ref, level_ref, keys, values, mask_of, score_scale)


def attend_second(queries, chunks, parents, group_index, chunk_paths, part_rows, score_scale):
    span_count, row_count, width = queries.shape
    source_count = len(chunks[0])
    chunk_count = len(chunks)
    span_rows = 2 * part_rows
    fresh_rows = chunks[-1][0].shape[0] - chunk_paths * span_rows
    operands = [ref for chunk in chunks for ref in chunk]
    keys = source_count * part_rows + fresh_rows // 2
    copy_count = chunk_count * source_count * chunk_paths + source_count
    return pl.pallas_call(
        functools.partial(
            second_kernel, chunk_count, source_count, chunk_paths, part_rows, score_scale
        ),
        grid_spec=pltpu.PrefetchScalarGridSpec(
            num_scalar_prefetch=2,
            grid=(span_count,),
            in_specs=[pl.BlockSpec((1, row_count, width), lambda step, parent, group: (step, 0, 0))]
            + [pl.BlockSpec(memory_space=pl.ANY)] * len(operands),
            out_specs=pl.BlockSpec(
                (1, row_count + stat_rows, width), lambda step, parent, group: (step, 0, 0)
            ),
            scratch_shapes=[
                pltpu.VMEM((row_count // width, width), jnp.float32),
                pltpu.VMEM(
                    (source_count, chunk_count * chunk_paths, span_rows, width), jnp.bfloat16
                ),
                pltpu.VMEM((source_count, fresh_rows, width), jnp.bfloat16),
                pltpu.SemaphoreType.DMA((copy_count,)),
            ],
        ),
        out_shape=jax.ShapeDtypeStruct((span_count, row_count + stat_rows, width), jnp.bfloat16),
        compiler_params=pltpu.CompilerParams(vmem_limit_bytes=vmem_bytes),
        cost_estimate=pl.CostEstimate(
            flops=8 * span_count * row_count * keys * width,
            bytes_accessed=4 * span_count * (row_count + keys) * width,
            transcendentals=span_count * row_count * keys,
        ),
        name="attend_second",
    )(parents, group_index, queries, *operands)


def own_kernel(group_size, score_scale, query_ref, key_ref, value_ref, out_ref, level_ref):
    token_count = key_ref.shape[1]

    def mask_of(tile):
        row = tile * row_tile + lax.broadcasted_iota(jnp.int32, (row_tile, token_count), 0)
        column = lax.broadcasted_iota(jnp.int32, (row_tile, token_count), 1)
        return column * group_size <= row

    attend_task(
        query_ref,
        out_ref,
        level_ref,
        [lambda: key_ref[0]],
        [lambda: value_ref[0]],
        mask_of,
        score_scale,
    )


def attend_own(queries, keys, values, score_scale):
    head_count, token_count, width = keys.shape
    row_count = queries.shape[1]
    return pl.pallas_call(
        functools.partial(own_kernel, row_count // token_count, score_scale),
        grid=(head_count,),
        in_specs=[
            pl.BlockSpec((1, row_count, width), lambda step: (step, 0, 0)),
            pl.BlockSpec((1, token_count, width), lambda step: (step, 0, 0)),
            pl.BlockSpec((1, token_count, width), lambda step: (step, 0, 0)),
        ],
        out_specs=pl.BlockSpec((1, row_count + stat_rows, width), lambda step: (step, 0, 0)),
        out_shape=jax.ShapeDtypeStruct((head_count, row_count + stat_rows, width), jnp.bfloat16),
        scratch_shapes=[pltpu.VMEM((row_count // width, width), jnp.float32)],
        compiler_params=pltpu.CompilerParams(vmem_limit_bytes=vmem_bytes),
        cost_estimate=pl.CostEstimate(
            flops=8 * head_count * row_count * token_count * width,
            bytes_accessed=4 * head_count * (row_count + token_count) * width,
            transcendentals=head_count * row_count * token_count,
        ),
        name="attend_own",
    )(queries, keys, values)


def merge_kernel(head_count, group_size, part_ref, own_ref, part_stat_ref, own_stat_ref, out_ref):
    token_tile, _, lanes = out_ref.shape[1:]
    rows = token_tile * group_size
    stat_tile = rows // lanes
    step = pl.program_id(0)
    group_count = part_ref.shape[0] // head_count
    picks = eye(lanes)

    def levels(ref, place):
        stats = ref[place].astype(jnp.float32)
        span = stat_rows // 4
        return stats[:span] + stats[span : 2 * span] + stats[2 * span : 3 * span]

    heads = []
    for head in range(head_count):
        places = [(part_ref, part_stat_ref, group * head_count + head) for group in range(group_count)]
        places.append((own_ref, own_stat_ref, head))
        level = [levels(stat, place) for _, stat, place in places]
        top = functools.reduce(jnp.maximum, level)
        shares = [jnp.exp(one - top) for one in level]
        total = functools.reduce(jnp.add, shares)
        shares = [one / total for one in shares]
        pieces = []
        for part in range(stat_tile):
            mixed = None
            for (ref, _, place), share in zip(places, shares):
                span = lax.broadcasted_iota(jnp.int32, share.shape, 0) == step * stat_tile + part
                line = jnp.sum(jnp.where(span, share, 0.0), axis=0, keepdims=True)
                column = jnp.sum(jnp.where(picks, line, 0.0), axis=1, keepdims=True)
                block = ref[place, pl.ds(part * lanes, lanes), :].astype(jnp.float32) * column
                mixed = block if mixed is None else mixed + block
            pieces.append(mixed.reshape(lanes // group_size, group_size, lanes))
        heads.append(jnp.concatenate(pieces, 0))
    out_ref[0] = jnp.concatenate(heads, 1).astype(out_ref.dtype)


def merge(parts, own, token_count):
    part_count, padded_rows, width = parts.shape
    head_count = own.shape[0]
    row_count = padded_rows - stat_rows
    group_size = row_count // token_count
    token_tile = 32
    rows = token_tile * group_size
    stat_block = row_count // stat_rows
    return pl.pallas_call(
        functools.partial(merge_kernel, head_count, group_size),
        grid=(token_count // token_tile,),
        in_specs=[
            pl.BlockSpec((part_count, rows, width), lambda step: (0, step, 0)),
            pl.BlockSpec((head_count, rows, width), lambda step: (0, step, 0)),
            pl.BlockSpec((part_count, stat_rows, width), lambda step: (0, stat_block, 0)),
            pl.BlockSpec((head_count, stat_rows, width), lambda step: (0, stat_block, 0)),
        ],
        out_specs=pl.BlockSpec(
            (1, token_tile, head_count * group_size, width), lambda step: (0, step, 0, 0)
        ),
        out_shape=jax.ShapeDtypeStruct(
            (1, token_count, head_count * group_size, width), jnp.bfloat16
        ),
        compiler_params=pltpu.CompilerParams(vmem_limit_bytes=vmem_bytes),
        cost_estimate=pl.CostEstimate(
            flops=4 * part_count * row_count * width,
            bytes_accessed=4 * part_count * row_count * width,
            transcendentals=0,
        ),
        name="merge_parts",
    )(parts, own, parts, own)


def local(
    chunk_count,
    queries_one,
    keys_one,
    values_one,
    queries_two,
    keys_two,
    values_two,
    cache_keys,
    cache_values,
    paths,
    parents,
    positions,
):
    here_index = lax.axis_index("node")
    peer_count = lax.axis_size("node")
    block_count, token_count, head_count, width = cache_keys.shape
    per_peer = paths.shape[1] // peer_count
    group_size = queries_one.shape[2] // head_count
    copies = peer_count // head_count
    score_scale = width ** (-0.5)
    my_head = here_index % head_count
    my_group = here_index // head_count

    def by_head(rotated):
        split = rotated.reshape(token_count, head_count, group_size, width)
        rows = jnp.moveaxis(split, 1, 0).reshape(head_count, token_count * group_size, width)
        return jnp.tile(rows, (copies, 1, 1))

    def exchange(rows):
        return lax.all_to_all(rows, "node", split_axis=0, concat_axis=0, tiled=True)

    send_one = by_head(rotary(queries_one[0], positions[0, 0]))
    got_one = exchange(send_one)
    key_rot_one = rotary(keys_one[0], positions[0, 0])
    key_rot_two = rotary(keys_two[0], positions[1, 0])

    block_index = local_blocks(paths, here_index, block_count, per_peer)
    chunk_paths = peer_count // chunk_count
    part_rows = per_peer * token_count
    chunks = []
    for chunk in range(chunk_count):
        last = chunk == chunk_count - 1
        packed = pack(
            cache_keys,
            cache_values,
            block_index[chunk * chunk_paths : (chunk + 1) * chunk_paths],
            my_head[None],
            (key_rot_one, values_one[0]) if last else (),
            per_peer,
        )
        arrived = [packed[0]]
        for far in range(1, head_count):
            pairs = [(node, node ^ far) for node in range(peer_count)]
            arrived.append(lax.ppermute(packed[far], "node", pairs))
        chunks.append(arrived)

    send_two = by_head(rotary(queries_two[0], positions[1, 0]))
    got_two = exchange(send_two)

    own_one = attend_own(
        send_one, jnp.moveaxis(key_rot_one, 1, 0), jnp.moveaxis(values_one[0], 1, 0), score_scale
    )
    own_two = attend_own(
        send_two, jnp.moveaxis(key_rot_two, 1, 0), jnp.moveaxis(values_two[0], 1, 0), score_scale
    )

    partial_one = None
    for chunk in range(chunk_count):
        partial_one = attend_first(
            got_one,
            chunks[chunk],
            partial_one,
            chunk * chunk_paths,
            chunk_paths,
            part_rows,
            score_scale,
        )
    parts_one = exchange(partial_one)
    partial_two = attend_second(
        got_two,
        chunks,
        parents,
        jnp.stack([my_group, my_head]),
        chunk_paths,
        part_rows,
        score_scale,
    )
    parts_two = exchange(partial_two)
    return merge(parts_one, own_one, token_count), merge(parts_two, own_two, token_count)


def solution(mesh):
    in_specs = (
        P(("group", "node"), None, "head", None),
        P(("group", "node"), None, "head", None),
        P(("group", "node"), None, "head", None),
        P(("group", "node"), None, "head", None),
        P(("group", "node"), None, "head", None),
        P(("group", "node"), None, "head", None),
        P(("group", "node"), None, "head", None),
        P(("group", "node"), None, "head", None),
        P("group", None),
        P("group"),
        P(None, ("group", "node"), None),
    )
    out_specs = (P(("group", "node"), None, "head", None), P(("group", "node"), None, "head", None))
    return jax.shard_map(
        functools.partial(local, 2),
        mesh=mesh,
        in_specs=in_specs,
        out_specs=out_specs,
        check_vma=False,
    )
```

```python
import functools

import jax
import jax.numpy as jnp
from jax import lax
from jax.experimental import pallas as pl
from jax.experimental.pallas import tpu as pltpu
from jax.sharding import PartitionSpec as P

rope_theta = 500000.0
log2_e = 1.4426950408889634
stat_rows = 32
row_tile = 256
vmem_bytes = 56 * 1024 * 1024


def rotary_tables(positions, head_width):
    half_width = head_width // 2
    frequency = rope_theta ** (-(jnp.arange(half_width, dtype=jnp.float32) * 2.0) / head_width)
    angles = positions.astype(jnp.float32)[..., None] * frequency
    cosine = jnp.cos(angles)
    sine_part = jnp.sin(angles)
    return jnp.concatenate([cosine, cosine], -1), jnp.concatenate([-sine_part, sine_part], -1)


def rotary(vector, cosine, signed_sine):
    widened = vector.astype(jnp.float32)
    swapped = jnp.roll(widened, widened.shape[-1] // 2, axis=-1)
    turned = widened * cosine[:, None, :] + swapped * signed_sine[:, None, :]
    return turned.astype(jnp.bfloat16)


def turn_kernel(head_count, copies, first_ref, second_ref, cosine_ref, sine_ref, out_ref):
    token_tile, query_heads, width = first_ref.shape[1:]
    group_size = query_heads // head_count
    rows = token_tile * group_size
    for depth, query_ref in enumerate((first_ref, second_ref)):
        widened = query_ref[0].astype(jnp.float32)
        swapped = pltpu.roll(widened.reshape(token_tile * query_heads, width), width // 2, 1)
        swapped = swapped.reshape(token_tile, query_heads, width)
        turned = widened * cosine_ref[depth][:, None, :] + swapped * sine_ref[depth][:, None, :]
        for head in range(head_count):
            turned_head = turned[:, head * group_size : (head + 1) * group_size, :]
            turned_head = turned_head.reshape(rows, width).astype(jnp.bfloat16)
            for copy in range(copies):
                out_ref[copy * head_count + head, depth] = turned_head


def turn_queries(queries_one, queries_two, cosine, sine_part, head_count, copies):
    _, token_count, query_heads, width = queries_one.shape
    token_tile = 32
    rows = token_tile * query_heads // head_count
    query_spec = pl.BlockSpec((1, token_tile, query_heads, width), lambda step: (0, step, 0, 0))
    table_spec = pl.BlockSpec((2, token_tile, width), lambda step: (0, step, 0))
    return pl.pallas_call(
        functools.partial(turn_kernel, head_count, copies),
        grid=(token_count // token_tile,),
        in_specs=[query_spec, query_spec, table_spec, table_spec],
        out_specs=pl.BlockSpec(
            (head_count * copies, 2, rows, width), lambda step: (0, 0, step, 0)
        ),
        out_shape=jax.ShapeDtypeStruct(
            (head_count * copies, 2, token_count * query_heads // head_count, width), jnp.bfloat16
        ),
        compiler_params=pltpu.CompilerParams(vmem_limit_bytes=vmem_bytes),
        cost_estimate=pl.CostEstimate(
            flops=8 * queries_one.size, bytes_accessed=12 * queries_one.size, transcendentals=0
        ),
        name="turn_queries",
    )(queries_one, queries_two, cosine, sine_part)


def local_blocks(paths, here_index, per_owner, per_peer):
    is_local = paths // per_owner == here_index
    slot_rank = jnp.cumsum(is_local.astype(jnp.int32), axis=1) - 1
    slot_range = jnp.arange(per_peer, dtype=jnp.int32)
    selected = jnp.logical_and(
        is_local[:, :, None], slot_rank[:, :, None] == slot_range[None, None, :]
    )
    return jnp.sum(jnp.where(selected, (paths % per_owner)[:, :, None], 0), axis=1)


def pack_kernel(per_peer, head_count, token_count, with_new, index_ref, head_ref, *refs):
    key_refs = refs[:per_peer]
    value_refs = refs[per_peer : 2 * per_peer]
    refs = refs[2 * per_peer :]
    new_refs = ()
    if with_new:
        new_refs = refs[:2]
    out_refs, wide = refs[-1 - head_count : -1], refs[-1]
    step = pl.program_id(0)
    mine = head_ref[0]
    span_rows = 2 * per_peer * token_count

    def spread(rows, offset):
        wide[...] = rows.astype(jnp.float32)
        for far in range(head_count):
            head = lax.bitwise_xor(mine, far)
            picked = wide[pl.ds(head, token_count, stride=head_count), :]
            out_refs[far][pl.ds(offset, token_count), :] = picked.astype(jnp.bfloat16)

    for which, source_refs in enumerate((key_refs, value_refs)):
        for slot, source in enumerate(source_refs):
            offset = step * span_rows + (which * per_peer + slot) * token_count
            spread(source[0], pl.multiple_of(offset, token_count))
    if with_new:

        @pl.when(step == 0)
        def _():
            base = pl.num_programs(0) * span_rows
            for which, source in enumerate(new_refs):
                spread(source[...], pl.multiple_of(base + which * token_count, token_count))


def pack(cache_keys, cache_values, block_index, head_index, new_rows, per_peer, before=()):
    block_count, token_count, head_count, width = cache_keys.shape
    path_count = block_index.shape[0]
    flat_keys = cache_keys.reshape(block_count, token_count * head_count, width)
    flat_values = cache_values.reshape(block_count, token_count * head_count, width)
    span_rows = 2 * per_peer * token_count
    out_rows = path_count * span_rows + (2 * token_count if new_rows else 0)

    def block_spec(slot):
        return pl.BlockSpec(
            (1, token_count * head_count, width),
            lambda step, index, head: (index[step * per_peer + slot], 0, 0),
        )

    cache_specs = [block_spec(slot) for slot in range(per_peer)]
    new_spec = pl.BlockSpec((token_count * head_count, width), lambda step, index, head: (0, 0))
    operands = [flat_keys] * per_peer + [flat_values] * per_peer
    operands += [row.reshape(token_count * head_count, width) for row in new_rows]
    return pl.pallas_call(
        functools.partial(pack_kernel, per_peer, head_count, token_count, bool(new_rows)),
        grid_spec=pltpu.PrefetchScalarGridSpec(
            num_scalar_prefetch=2,
            grid=(path_count,),
            in_specs=cache_specs
            + cache_specs
            + [new_spec] * len(new_rows)
            + [pl.BlockSpec(memory_space=pl.ANY)] * len(before),
            out_specs=[pl.BlockSpec((out_rows, width), lambda step, index, head: (0, 0))]
            * head_count,
            scratch_shapes=[pltpu.VMEM((token_count * head_count, width), jnp.float32)],
        ),
        out_shape=[jax.ShapeDtypeStruct((out_rows, width), jnp.bfloat16)] * head_count,
        compiler_params=pltpu.CompilerParams(vmem_limit_bytes=vmem_bytes),
        cost_estimate=pl.CostEstimate(
            flops=0, bytes_accessed=4 * head_count * out_rows * width, transcendentals=0
        ),
        name="pack_rows",
    )(block_index.reshape(-1), head_index, *operands, *before)


def eye(size):
    return lax.broadcasted_iota(jnp.int32, (size, size), 0) == lax.broadcasted_iota(
        jnp.int32, (size, size), 1
    )


def product(left, right):
    return lax.dot_general(
        left, right, (((1,), (1,)), ((), ())), preferred_element_type=jnp.float32
    )


def attend_rows(query, key_parts, value_parts, mask, score_scale):
    scores = [product(query, keys) for keys in key_parts]
    if mask is not None:
        scores[-1] = jnp.where(mask, scores[-1], -1e30)
    row_max = functools.reduce(
        jnp.maximum, [jnp.max(part, axis=-1, keepdims=True) for part in scores]
    )
    total = jnp.zeros_like(row_max)
    mixture = jnp.zeros((query.shape[0], value_parts[0].shape[-1]), jnp.float32)
    for part, values in zip(scores, value_parts):
        weights = jnp.exp2((part - row_max) * (score_scale * log2_e))
        total = total + jnp.sum(weights, axis=-1, keepdims=True)
        mixture = mixture + jnp.dot(
            weights.astype(jnp.bfloat16), values, preferred_element_type=jnp.float32
        )
    return mixture / total, row_max * score_scale + jnp.log(total)


def store_partial(out_ref, tile, mixture, level, lanes):
    rows = mixture.shape[0]
    out_ref[0, pl.ds(pl.multiple_of(tile * rows, rows), rows), :] = mixture.astype(jnp.bfloat16)
    picks = eye(lanes)
    flat = [
        jnp.sum(
            jnp.where(picks, level[part * lanes : (part + 1) * lanes], 0.0), axis=0, keepdims=True
        )
        for part in range(rows // lanes)
    ]
    return flat


def store_stats(out_ref, levels):
    row_count = out_ref.shape[1] - stat_rows
    high = levels.astype(jnp.bfloat16).astype(jnp.float32)
    middle = (levels - high).astype(jnp.bfloat16).astype(jnp.float32)
    low = levels - high - middle
    stats = jnp.concatenate([high, middle, low, jnp.zeros_like(levels)], 0)
    out_ref[0, pl.ds(row_count, stat_rows), :] = stats.astype(jnp.bfloat16)


def attend_task(query_ref, out_ref, level_ref, key_parts, value_parts, mask_of, score_scale):
    row_count = out_ref.shape[1] - stat_rows
    lanes = out_ref.shape[2]
    per_tile = row_tile // lanes

    def tile_step(tile, carry):
        query = query_ref[0, pl.ds(pl.multiple_of(tile * row_tile, row_tile), row_tile), :]
        mixture, level = attend_rows(
            query,
            [read() for read in key_parts],
            [read() for read in value_parts],
            None if mask_of is None else mask_of(tile),
            score_scale,
        )
        flat = store_partial(out_ref, tile, mixture, level, lanes)
        for part in range(per_tile):
            level_ref[pl.ds(tile * per_tile + part, 1), :] = flat[part]
        return carry

    lax.fori_loop(0, row_count // row_tile, tile_step, 0)
    store_stats(out_ref, level_ref[...])


def part_readers(refs, part_rows):
    keys = [functools.partial(lambda ref: ref[pl.ds(0, part_rows), :], ref) for ref in refs]
    values = [
        functools.partial(lambda ref: ref[pl.ds(part_rows, part_rows), :], ref) for ref in refs
    ]
    return keys, values


def first_kernel(source_count, part_rows, score_scale, query_ref, *refs):
    source_refs = refs[:source_count]
    out_ref, mark_ref, level_ref = refs[-3:]
    mark_ref[...] = jnp.zeros_like(mark_ref)
    keys, values = part_readers(source_refs, part_rows)
    attend_task(query_ref, out_ref, level_ref, keys, values, None, score_scale)


def attend_first(queries, sources, base, first_path, path_count, part_rows, score_scale, before):
    span_count, _, row_count, width = queries.shape
    span_rows = 2 * part_rows
    out_shape = jax.ShapeDtypeStruct((span_count, row_count + stat_rows, width), jnp.bfloat16)
    has_base = int(base is not None)
    operands = [queries, *sources, *before] + ([base] if has_base else [])
    keys = len(sources) * part_rows
    return pl.pallas_call(
        functools.partial(first_kernel, len(sources), part_rows, score_scale),
        grid=(path_count,),
        in_specs=[
            pl.BlockSpec((1, None, row_count, width), lambda step: (first_path + step, 0, 0, 0))
        ]
        + [pl.BlockSpec((span_rows, width), lambda step: (step, 0))] * len(sources)
        + [pl.BlockSpec(memory_space=pl.ANY)] * (len(before) + has_base),
        out_specs=[
            pl.BlockSpec((1, row_count + stat_rows, width), lambda step: (first_path + step, 0, 0)),
            pl.BlockSpec((8, width), lambda step: (0, 0)),
        ],
        out_shape=[out_shape, jax.ShapeDtypeStruct((8, width), jnp.float32)],
        scratch_shapes=[pltpu.VMEM((row_count // width, width), jnp.float32)],
        input_output_aliases={len(operands) - 1: 0} if has_base else {},
        compiler_params=pltpu.CompilerParams(vmem_limit_bytes=vmem_bytes),
        cost_estimate=pl.CostEstimate(
            flops=8 * path_count * row_count * keys * width,
            bytes_accessed=4 * path_count * (row_count + keys) * width,
            transcendentals=path_count * row_count * keys,
        ),
        name="attend_first",
    )(*operands)


def second_kernel(
    chunk_count, source_count, chunk_paths, part_rows, score_scale, parent_ref, group_ref, *refs
):
    query_ref = refs[0]
    source_refs = refs[1 : 1 + chunk_count * source_count]
    out_ref, level_ref, held, fresh, semaphores = refs[-5:]
    span_rows = 2 * part_rows
    token_count = fresh.shape[1] // 2
    step = pl.program_id(0)

    def copies():
        out = []
        for chunk in range(chunk_count):
            for source in range(source_count):
                ref = source_refs[chunk * source_count + source]
                for path in range(chunk_paths):
                    out.append(
                        pltpu.make_async_copy(
                            ref.at[pl.ds(path * span_rows, span_rows)],
                            held.at[source, chunk * chunk_paths + path],
                            semaphores.at[len(out)],
                        )
                    )
        for source in range(source_count):
            ref = source_refs[(chunk_count - 1) * source_count + source]
            out.append(
                pltpu.make_async_copy(
                    ref.at[pl.ds(chunk_paths * span_rows, 2 * token_count)],
                    fresh.at[source],
                    semaphores.at[len(out)],
                )
            )
        return out

    @pl.when(step == 0)
    def _():
        moves = copies()
        for move in moves:
            move.start()
        for move in moves:
            move.wait()

    parent = parent_ref[step]
    home = parent // source_count
    present = home == group_ref[0]
    slot = lax.bitwise_xor(parent % source_count, group_ref[1])
    keys = [
        functools.partial(lambda source: held[source, parent, pl.ds(0, part_rows), :], source)
        for source in range(source_count)
    ]
    values = [
        functools.partial(
            lambda source: held[source, parent, pl.ds(part_rows, part_rows), :], source
        )
        for source in range(source_count)
    ]
    keys.append(lambda: fresh[slot, pl.ds(0, token_count), :])
    values.append(lambda: fresh[slot, pl.ds(token_count, token_count), :])

    def mask_of(tile):
        return jnp.broadcast_to(present, (row_tile, token_count))

    attend_task(query_ref, out_ref, level_ref, keys, values, mask_of, score_scale)


def attend_second(
    queries, chunks, parents, group_index, chunk_paths, part_rows, score_scale, before
):
    span_count, _, row_count, width = queries.shape
    source_count = len(chunks[0])
    chunk_count = len(chunks)
    span_rows = 2 * part_rows
    fresh_rows = chunks[-1][0].shape[0] - chunk_paths * span_rows
    operands = [ref for chunk in chunks for ref in chunk]
    keys = source_count * part_rows + fresh_rows // 2
    copy_count = chunk_count * source_count * chunk_paths + source_count
    return pl.pallas_call(
        functools.partial(
            second_kernel, chunk_count, source_count, chunk_paths, part_rows, score_scale
        ),
        grid_spec=pltpu.PrefetchScalarGridSpec(
            num_scalar_prefetch=2,
            grid=(span_count,),
            in_specs=[
                pl.BlockSpec(
                    (1, None, row_count, width), lambda step, parent, group: (step, 1, 0, 0)
                )
            ]
            + [pl.BlockSpec(memory_space=pl.ANY)] * (len(operands) + len(before)),
            out_specs=pl.BlockSpec(
                (1, row_count + stat_rows, width), lambda step, parent, group: (step, 0, 0)
            ),
            scratch_shapes=[
                pltpu.VMEM((row_count // width, width), jnp.float32),
                pltpu.VMEM(
                    (source_count, chunk_count * chunk_paths, span_rows, width), jnp.bfloat16
                ),
                pltpu.VMEM((source_count, fresh_rows, width), jnp.bfloat16),
                pltpu.SemaphoreType.DMA((copy_count,)),
            ],
        ),
        out_shape=jax.ShapeDtypeStruct((span_count, row_count + stat_rows, width), jnp.bfloat16),
        compiler_params=pltpu.CompilerParams(vmem_limit_bytes=vmem_bytes),
        cost_estimate=pl.CostEstimate(
            flops=8 * span_count * row_count * keys * width,
            bytes_accessed=4 * span_count * (row_count + keys) * width,
            transcendentals=span_count * row_count * keys,
        ),
        name="attend_second",
    )(parents, group_index, queries, *operands, *before)


def own_kernel(group_size, score_scale, query_ref, key_ref, value_ref, out_ref, level_ref):
    token_count = key_ref.shape[1]

    def mask_of(tile):
        row = tile * row_tile + lax.broadcasted_iota(jnp.int32, (row_tile, token_count), 0)
        column = lax.broadcasted_iota(jnp.int32, (row_tile, token_count), 1)
        return column * group_size <= row

    attend_task(
        query_ref,
        out_ref,
        level_ref,
        [lambda: key_ref[0]],
        [lambda: value_ref[0]],
        mask_of,
        score_scale,
    )


def attend_own(queries, depth, keys, values, score_scale):
    head_count, token_count, width = keys.shape
    row_count = queries.shape[2]
    return pl.pallas_call(
        functools.partial(own_kernel, row_count // token_count, score_scale),
        grid=(head_count,),
        in_specs=[
            pl.BlockSpec((1, None, row_count, width), lambda step: (step, depth, 0, 0)),
            pl.BlockSpec((1, token_count, width), lambda step: (step, 0, 0)),
            pl.BlockSpec((1, token_count, width), lambda step: (step, 0, 0)),
        ],
        out_specs=pl.BlockSpec((1, row_count + stat_rows, width), lambda step: (step, 0, 0)),
        out_shape=jax.ShapeDtypeStruct((head_count, row_count + stat_rows, width), jnp.bfloat16),
        scratch_shapes=[pltpu.VMEM((row_count // width, width), jnp.float32)],
        compiler_params=pltpu.CompilerParams(vmem_limit_bytes=vmem_bytes),
        cost_estimate=pl.CostEstimate(
            flops=8 * head_count * row_count * token_count * width,
            bytes_accessed=4 * head_count * (row_count + token_count) * width,
            transcendentals=head_count * row_count * token_count,
        ),
        name="attend_own",
    )(queries, keys, values)


def merge_kernel(head_count, group_size, part_ref, own_ref, part_stat_ref, own_stat_ref, out_ref):
    token_tile, _, lanes = out_ref.shape[1:]
    rows = token_tile * group_size
    stat_tile = rows // lanes
    step = pl.program_id(0)
    group_count = part_ref.shape[0] // head_count
    picks = eye(lanes)

    def levels(ref, place):
        stats = ref[place].astype(jnp.float32)
        span = stat_rows // 4
        return stats[:span] + stats[span : 2 * span] + stats[2 * span : 3 * span]

    heads = []
    for head in range(head_count):
        places = [(part_ref, part_stat_ref, group * head_count + head) for group in range(group_count)]
        places.append((own_ref, own_stat_ref, head))
        level = [levels(stat, place) for _, stat, place in places]
        top = functools.reduce(jnp.maximum, level)
        shares = [jnp.exp(one - top) for one in level]
        total = functools.reduce(jnp.add, shares)
        shares = [one / total for one in shares]
        pieces = []
        for part in range(stat_tile):
            mixed = None
            for (ref, _, place), share in zip(places, shares):
                span = lax.broadcasted_iota(jnp.int32, share.shape, 0) == step * stat_tile + part
                line = jnp.sum(jnp.where(span, share, 0.0), axis=0, keepdims=True)
                column = jnp.sum(jnp.where(picks, line, 0.0), axis=1, keepdims=True)
                block = ref[place, pl.ds(part * lanes, lanes), :].astype(jnp.float32) * column
                mixed = block if mixed is None else mixed + block
            pieces.append(mixed.reshape(lanes // group_size, group_size, lanes))
        heads.append(jnp.concatenate(pieces, 0))
    out_ref[0] = jnp.concatenate(heads, 1).astype(out_ref.dtype)


def merge(parts, own, token_count):
    part_count, padded_rows, width = parts.shape
    head_count = own.shape[0]
    row_count = padded_rows - stat_rows
    group_size = row_count // token_count
    token_tile = 32
    rows = token_tile * group_size
    stat_block = row_count // stat_rows
    return pl.pallas_call(
        functools.partial(merge_kernel, head_count, group_size),
        grid=(token_count // token_tile,),
        in_specs=[
            pl.BlockSpec((part_count, rows, width), lambda step: (0, step, 0)),
            pl.BlockSpec((head_count, rows, width), lambda step: (0, step, 0)),
            pl.BlockSpec((part_count, stat_rows, width), lambda step: (0, stat_block, 0)),
            pl.BlockSpec((head_count, stat_rows, width), lambda step: (0, stat_block, 0)),
        ],
        out_specs=pl.BlockSpec(
            (1, token_tile, head_count * group_size, width), lambda step: (0, step, 0, 0)
        ),
        out_shape=jax.ShapeDtypeStruct(
            (1, token_count, head_count * group_size, width), jnp.bfloat16
        ),
        compiler_params=pltpu.CompilerParams(vmem_limit_bytes=vmem_bytes),
        cost_estimate=pl.CostEstimate(
            flops=4 * part_count * row_count * width,
            bytes_accessed=4 * part_count * row_count * width,
            transcendentals=0,
        ),
        name="merge_parts",
    )(parts, own, parts, own)


def local(
    chunk_count,
    queries_one,
    keys_one,
    values_one,
    queries_two,
    keys_two,
    values_two,
    cache_keys,
    cache_values,
    paths,
    parents,
    positions,
):
    here_index = lax.axis_index("node")
    peer_count = lax.axis_size("node")
    block_count, token_count, head_count, width = cache_keys.shape
    per_peer = paths.shape[1] // peer_count
    group_size = queries_one.shape[2] // head_count
    copies = peer_count // head_count
    score_scale = width ** (-0.5)
    my_head = here_index % head_count
    my_group = here_index // head_count

    def exchange(rows):
        return lax.all_to_all(rows, "node", split_axis=0, concat_axis=0, tiled=True)

    cosine, sine_part = rotary_tables(positions[:, 0], width)
    send = turn_queries(queries_one, queries_two, cosine, sine_part, head_count, copies)
    got = exchange(send)
    key_rot_one = rotary(keys_one[0], cosine[0], sine_part[0])
    key_rot_two = rotary(keys_two[0], cosine[1], sine_part[1])

    block_index = local_blocks(paths, here_index, block_count, per_peer)
    chunk_paths = peer_count // chunk_count
    part_rows = per_peer * token_count
    chunks = []
    for chunk in range(chunk_count):
        last = chunk == chunk_count - 1
        packed = pack(
            cache_keys,
            cache_values,
            block_index[chunk * chunk_paths : (chunk + 1) * chunk_paths],
            my_head[None],
            (key_rot_one, values_one[0]) if last else (),
            per_peer,
            (send,) if chunk == 0 else (packed[0],),
        )
        arrived = [packed[0]]
        for far in range(1, head_count):
            pairs = [(node, node ^ far) for node in range(peer_count)]
            arrived.append(lax.ppermute(packed[far], "node", pairs))
        chunks.append(arrived)

    own_one = attend_own(
        send, 0, jnp.moveaxis(key_rot_one, 1, 0), jnp.moveaxis(values_one[0], 1, 0), score_scale
    )
    own_two = attend_own(
        send, 1, jnp.moveaxis(key_rot_two, 1, 0), jnp.moveaxis(values_two[0], 1, 0), score_scale
    )

    partial_one = None
    for chunk in range(chunk_count):
        partial_one, mark = attend_first(
            got,
            chunks[chunk],
            partial_one,
            chunk * chunk_paths,
            chunk_paths,
            part_rows,
            score_scale,
            (own_one, own_two) if chunk == 0 else (),
        )
    parts_one = exchange(partial_one)
    partial_two = attend_second(
        got,
        chunks,
        parents,
        jnp.stack([my_group, my_head]),
        chunk_paths,
        part_rows,
        score_scale,
        (mark,),
    )
    parts_two = exchange(partial_two)
    return merge(parts_one, own_one, token_count), merge(parts_two, own_two, token_count)


def solution(mesh):
    in_specs = (
        P(("group", "node"), None, "head", None),
        P(("group", "node"), None, "head", None),
        P(("group", "node"), None, "head", None),
        P(("group", "node"), None, "head", None),
        P(("group", "node"), None, "head", None),
        P(("group", "node"), None, "head", None),
        P(("group", "node"), None, "head", None),
        P(("group", "node"), None, "head", None),
        P("group", None),
        P("group"),
        P(None, ("group", "node"), None),
    )
    out_specs = (P(("group", "node"), None, "head", None), P(("group", "node"), None, "head", None))
    return jax.shard_map(
        functools.partial(local, 2),
        mesh=mesh,
        in_specs=in_specs,
        out_specs=out_specs,
        check_vma=False,
    )
```

```python
import functools

import jax
import jax.numpy as jnp
from jax import lax
from jax.experimental import pallas as pl
from jax.experimental.pallas import tpu as pltpu
from jax.sharding import PartitionSpec as P

rope_theta = 500000.0
log2_e = 1.4426950408889634
stat_rows = 32
row_tile = 256
vmem_bytes = 56 * 1024 * 1024


def rotary_tables(positions, head_width):
    half_width = head_width // 2
    frequency = rope_theta ** (-(jnp.arange(half_width, dtype=jnp.float32) * 2.0) / head_width)
    angles = positions.astype(jnp.float32)[..., None] * frequency
    cosine = jnp.cos(angles)
    sine_part = jnp.sin(angles)
    return jnp.concatenate([cosine, cosine], -1), jnp.concatenate([-sine_part, sine_part], -1)


def rotary(vector, cosine, signed_sine):
    widened = vector.astype(jnp.float32)
    swapped = jnp.roll(widened, widened.shape[-1] // 2, axis=-1)
    turned = widened * cosine[:, None, :] + swapped * signed_sine[:, None, :]
    return turned.astype(jnp.bfloat16)


def turn_kernel(head_count, copies, first_ref, second_ref, cosine_ref, sine_ref, out_ref):
    token_tile, query_heads, width = first_ref.shape[1:]
    group_size = query_heads // head_count
    rows = token_tile * group_size
    for depth, query_ref in enumerate((first_ref, second_ref)):
        widened = query_ref[0].astype(jnp.float32)
        swapped = pltpu.roll(widened.reshape(token_tile * query_heads, width), width // 2, 1)
        swapped = swapped.reshape(token_tile, query_heads, width)
        turned = widened * cosine_ref[depth][:, None, :] + swapped * sine_ref[depth][:, None, :]
        for head in range(head_count):
            turned_head = turned[:, head * group_size : (head + 1) * group_size, :]
            turned_head = turned_head.reshape(rows, width).astype(jnp.bfloat16)
            for copy in range(copies):
                out_ref[copy * head_count + head, depth] = turned_head


def turn_queries(queries_one, queries_two, cosine, sine_part, head_count, copies):
    _, token_count, query_heads, width = queries_one.shape
    token_tile = 32
    rows = token_tile * query_heads // head_count
    query_spec = pl.BlockSpec((1, token_tile, query_heads, width), lambda step: (0, step, 0, 0))
    table_spec = pl.BlockSpec((2, token_tile, width), lambda step: (0, step, 0))
    return pl.pallas_call(
        functools.partial(turn_kernel, head_count, copies),
        grid=(token_count // token_tile,),
        in_specs=[query_spec, query_spec, table_spec, table_spec],
        out_specs=pl.BlockSpec(
            (head_count * copies, 2, rows, width), lambda step: (0, 0, step, 0)
        ),
        out_shape=jax.ShapeDtypeStruct(
            (head_count * copies, 2, token_count * query_heads // head_count, width), jnp.bfloat16
        ),
        compiler_params=pltpu.CompilerParams(vmem_limit_bytes=vmem_bytes),
        cost_estimate=pl.CostEstimate(
            flops=8 * queries_one.size, bytes_accessed=12 * queries_one.size, transcendentals=0
        ),
        name="turn_queries",
    )(queries_one, queries_two, cosine, sine_part)


def local_blocks(paths, here_index, per_owner, per_peer):
    is_local = paths // per_owner == here_index
    slot_rank = jnp.cumsum(is_local.astype(jnp.int32), axis=1) - 1
    slot_range = jnp.arange(per_peer, dtype=jnp.int32)
    selected = jnp.logical_and(
        is_local[:, :, None], slot_rank[:, :, None] == slot_range[None, None, :]
    )
    return jnp.sum(jnp.where(selected, (paths % per_owner)[:, :, None], 0), axis=1)


def pack_kernel(per_peer, head_count, token_count, with_new, index_ref, place_ref, *refs):
    key_refs = refs[:per_peer]
    value_refs = refs[per_peer : 2 * per_peer]
    refs = refs[2 * per_peer :]
    new_refs = ()
    if with_new:
        new_refs = refs[:2]
    out_refs, wide = refs[-1 - head_count : -1], refs[-1]
    step = pl.program_id(0)
    mine = place_ref[0]
    span_rows = 2 * per_peer * token_count

    def spread(rows, offset):
        wide[...] = rows.astype(jnp.float32)
        for far in range(head_count):
            head = lax.bitwise_xor(mine, far)
            picked = wide[pl.ds(head, token_count, stride=head_count), :]
            out_refs[far][pl.ds(offset, token_count), :] = picked.astype(jnp.bfloat16)

    for which, source_refs in enumerate((key_refs, value_refs)):
        for slot, source in enumerate(source_refs):
            offset = step * span_rows + (which * per_peer + slot) * token_count
            spread(source[0], pl.multiple_of(offset, token_count))
    if with_new:

        @pl.when(step == 0)
        def _():
            base = pl.num_programs(0) * span_rows
            for which, source in enumerate(new_refs):
                spread(source[...], pl.multiple_of(base + which * token_count, token_count))


def pack(cache_keys, cache_values, block_index, place, new_rows, per_peer, before=()):
    block_count, token_count, head_count, width = cache_keys.shape
    flat_keys = cache_keys.reshape(block_count, token_count * head_count, width)
    flat_values = cache_values.reshape(block_count, token_count * head_count, width)
    span_rows = 2 * per_peer * token_count
    out_rows = head_count * span_rows + (2 * token_count if new_rows else 0)

    def block_spec(slot):
        return pl.BlockSpec(
            (1, token_count * head_count, width),
            lambda step, index, place: (
                index[(place[1] * head_count + step) * per_peer + slot],
                0,
                0,
            ),
        )

    cache_specs = [block_spec(slot) for slot in range(per_peer)]
    new_spec = pl.BlockSpec((token_count * head_count, width), lambda step, index, place: (0, 0))
    operands = [flat_keys] * per_peer + [flat_values] * per_peer
    operands += [row.reshape(token_count * head_count, width) for row in new_rows]
    return pl.pallas_call(
        functools.partial(pack_kernel, per_peer, head_count, token_count, bool(new_rows)),
        grid_spec=pltpu.PrefetchScalarGridSpec(
            num_scalar_prefetch=2,
            grid=(head_count,),
            in_specs=cache_specs
            + cache_specs
            + [new_spec] * len(new_rows)
            + [pl.BlockSpec(memory_space=pl.ANY)] * len(before),
            out_specs=[pl.BlockSpec((out_rows, width), lambda step, index, place: (0, 0))]
            * head_count,
            scratch_shapes=[pltpu.VMEM((token_count * head_count, width), jnp.float32)],
        ),
        out_shape=[jax.ShapeDtypeStruct((out_rows, width), jnp.bfloat16)] * head_count,
        compiler_params=pltpu.CompilerParams(vmem_limit_bytes=vmem_bytes),
        cost_estimate=pl.CostEstimate(
            flops=0, bytes_accessed=4 * head_count * out_rows * width, transcendentals=0
        ),
        name="pack_rows",
    )(block_index, place, *operands, *before)


def eye(size):
    return lax.broadcasted_iota(jnp.int32, (size, size), 0) == lax.broadcasted_iota(
        jnp.int32, (size, size), 1
    )


def product(left, right):
    return lax.dot_general(
        left, right, (((1,), (1,)), ((), ())), preferred_element_type=jnp.float32
    )


def fold_lanes(array, width, operation):
    pieces = [array[:, start : start + width] for start in range(0, array.shape[1], width)]
    while len(pieces) > 1:
        pieces = [
            operation(*pieces[start : start + 2]) if start + 1 < len(pieces) else pieces[start]
            for start in range(0, len(pieces), 2)
        ]
    return pieces[0]


def attend_task(query_of, put, row_count, width, parts, mask_of, level_ref, score_ref, score_scale):
    tile_count = row_count // row_tile

    def make_scores(tile):
        query = query_of(tile)
        top, start = None, 0
        for place, (keys, _) in enumerate(parts):
            scores = product(query, keys())
            if mask_of is not None and place == len(parts) - 1:
                scores = jnp.where(mask_of(tile), scores, -1e30)
            size = scores.shape[1]
            score_ref[tile % 2, :, start : start + size] = scores
            start += size
            folded = fold_lanes(scores, width, jnp.maximum)
            top = folded if top is None else jnp.maximum(top, folded)
        return jnp.max(top, axis=-1, keepdims=True)

    picks = eye(width)
    row_max = make_scores(0)
    for tile in range(tile_count):
        next_max = make_scores(tile + 1) if tile + 1 < tile_count else None
        total, mixture, start = None, None, 0
        for _, values in parts:
            value_rows = values()
            size = value_rows.shape[0]
            scores = score_ref[tile % 2, :, start : start + size]
            start += size
            weights = jnp.exp2((scores - row_max) * (score_scale * log2_e))
            folded = fold_lanes(weights, width, jnp.add)
            total = folded if total is None else total + folded
            mixed = jnp.dot(
                weights.astype(jnp.bfloat16), value_rows, preferred_element_type=jnp.float32
            )
            mixture = mixed if mixture is None else mixture + mixed
        total = jnp.sum(total, axis=-1, keepdims=True)
        put(tile * row_tile, (mixture / total).astype(jnp.bfloat16))
        level = row_max * score_scale + jnp.log(total)
        for piece in range(row_tile // width):
            line = jnp.where(picks, level[piece * width : (piece + 1) * width], 0.0)
            row = tile * (row_tile // width) + piece
            level_ref[row : row + 1, :] = jnp.sum(line, axis=0, keepdims=True)
        row_max = next_max
    levels = level_ref[...]
    high = levels.astype(jnp.bfloat16).astype(jnp.float32)
    middle = (levels - high).astype(jnp.bfloat16).astype(jnp.float32)
    low = levels - high - middle
    stats = jnp.concatenate([high, middle, low, jnp.zeros_like(levels)], 0)
    put(row_count, stats.astype(jnp.bfloat16))


def putter(out_ref):
    def put(start, rows):
        out_ref[start : start + rows.shape[0], :] = rows

    return put


def hand_out(stage_ref, out_refs):
    for far, out_ref in enumerate(out_refs):

        @pl.when(pl.program_id(0) == far)
        def _():
            out_ref[...] = stage_ref[...]


def tile_reader(query_ref):
    return lambda tile: query_ref[0, tile * row_tile : (tile + 1) * row_tile, :]


def task_scratch(row_count, width, key_count):
    return [
        pltpu.VMEM((row_count // width, width), jnp.float32),
        pltpu.VMEM((2, row_tile, key_count), jnp.float32),
    ]


def task_cost(task_count, row_count, key_count, width):
    return pl.CostEstimate(
        flops=4 * task_count * row_count * key_count * width,
        bytes_accessed=4 * task_count * (row_count + key_count) * width,
        transcendentals=task_count * row_count * key_count,
    )


def first_kernel(
    source_count, task_count, part_rows, score_scale, stacked, place_ref, query_ref, *refs
):
    source_refs = refs[:source_count]
    out_refs = refs[-4 - (1 if stacked else task_count) : -4]
    mark_ref, level_ref, score_ref, stage_ref = refs[-4:]
    _, row_count, width = query_ref.shape
    mark_ref[...] = jnp.zeros_like(mark_ref)
    parts = [
        (
            functools.partial(lambda ref: ref[0:part_rows, :], ref),
            functools.partial(lambda ref: ref[part_rows : 2 * part_rows, :], ref),
        )
        for ref in source_refs
    ]

    attend_task(
        tile_reader(query_ref),
        putter(out_refs[0].at[0] if stacked else stage_ref),
        row_count,
        width,
        parts,
        None,
        level_ref,
        score_ref,
        score_scale,
    )
    if not stacked:
        hand_out(stage_ref, out_refs)


def result_arrays(task_count, out_rows, width, stacked):
    if stacked:
        specs = [
            pl.BlockSpec(
                (1, out_rows, width),
                lambda step, *prefetched: (lax.bitwise_xor(prefetched[-1][0], step), 0, 0),
            )
        ]
        shapes = [jax.ShapeDtypeStruct((task_count, out_rows, width), jnp.bfloat16)]
    else:
        specs = [pl.BlockSpec((out_rows, width), lambda step, *prefetched: (0, 0))] * task_count
        shapes = [jax.ShapeDtypeStruct((out_rows, width), jnp.bfloat16)] * task_count
    specs.append(pl.BlockSpec((8, width), lambda step, *prefetched: (0, 0)))
    shapes.append(jax.ShapeDtypeStruct((8, width), jnp.float32))
    return specs, shapes


def attend_first(
    queries, sources, place, first_far, task_count, part_rows, score_scale, stacked, before
):
    _, _, row_count, width = queries.shape
    source_count = len(sources)
    out_rows = row_count + stat_rows
    out_specs, out_shape = result_arrays(task_count, out_rows, width, stacked)
    outs = pl.pallas_call(
        functools.partial(
            first_kernel, source_count, task_count, part_rows, score_scale, stacked
        ),
        grid_spec=pltpu.PrefetchScalarGridSpec(
            num_scalar_prefetch=1,
            grid=(task_count,),
            in_specs=[
                pl.BlockSpec(
                    (1, None, row_count, width),
                    lambda step, place: (
                        place[1] * source_count + lax.bitwise_xor(place[0], first_far + step),
                        0,
                        0,
                        0,
                    ),
                )
            ]
            + [
                pl.BlockSpec(
                    (2 * part_rows, width),
                    lambda step, place: (lax.bitwise_xor(place[0], first_far + step), 0),
                )
            ]
            * source_count
            + [pl.BlockSpec(memory_space=pl.ANY)] * len(before),
            out_specs=out_specs,
            scratch_shapes=task_scratch(row_count, width, source_count * part_rows)
            + [pltpu.VMEM((out_rows, width), jnp.bfloat16)],
        ),
        out_shape=out_shape,
        compiler_params=pltpu.CompilerParams(vmem_limit_bytes=vmem_bytes),
        cost_estimate=task_cost(task_count, row_count, source_count * part_rows, width),
        name="attend_first",
    )(place, queries, *sources, *before)
    return outs[:-1], outs[-1]


def second_kernel(
    chunk_count,
    source_count,
    first_far,
    task_count,
    part_rows,
    score_scale,
    stacked,
    parent_ref,
    place_ref,
    *refs,
):
    query_ref = refs[0]
    source_refs = refs[1 : 1 + chunk_count * source_count]
    out_refs = refs[-8 - (1 if stacked else task_count) : -8]
    mark_ref, level_ref, score_ref, stage_ref, held, fresh = refs[-8:-2]
    semaphores, fresh_semaphores = refs[-2:]
    _, row_count, width = query_ref.shape
    span_rows = 2 * part_rows
    token_count = fresh.shape[1] // 2
    step = pl.program_id(0)
    mine, group, home = place_ref[0], place_ref[1], place_ref[2]
    mark_ref[...] = jnp.zeros_like(mark_ref)

    def parent_at(task):
        return parent_ref[group * source_count + lax.bitwise_xor(mine, first_far + task)]

    def fetch(task):
        parent = parent_at(task)
        path = parent % source_count
        chunk_of = lax.bitwise_xor(parent // source_count, home)
        for chunk in range(chunk_count):

            @pl.when(chunk_of == chunk)
            def _():
                for source in range(source_count):
                    pltpu.make_async_copy(
                        source_refs[chunk * source_count + source].at[
                            pl.ds(pl.multiple_of(path * span_rows, span_rows), span_rows)
                        ],
                        held.at[task % 2, source],
                        semaphores.at[task % 2, source],
                    ).start()

    fresh_copies = [
        pltpu.make_async_copy(
            source_refs[source].at[pl.ds(source_count * span_rows, 2 * token_count)],
            fresh.at[source],
            fresh_semaphores.at[source],
        )
        for source in range(source_count)
    ]

    @pl.when(step == 0)
    def _():
        fetch(0)
        for copy in fresh_copies:
            copy.start()
        for copy in fresh_copies:
            copy.wait()

    @pl.when(step + 1 < task_count)
    def _():
        fetch(step + 1)

    slot = step % 2
    for source in range(source_count):
        pltpu.make_async_copy(
            source_refs[source].at[pl.ds(0, span_rows)],
            held.at[slot, source],
            semaphores.at[slot, source],
        ).wait()

    parent = parent_at(step)
    present = parent // source_count == home
    fresh_place = lax.bitwise_xor(parent % source_count, mine)
    parts = [
        (
            functools.partial(lambda source: held[slot, source, 0:part_rows, :], source),
            functools.partial(lambda source: held[slot, source, part_rows:span_rows, :], source),
        )
        for source in range(source_count)
    ]
    parts.append(
        (
            lambda: fresh[fresh_place, 0:token_count, :],
            lambda: fresh[fresh_place, token_count : 2 * token_count, :],
        )
    )

    def mask_of(tile):
        return jnp.broadcast_to(present, (row_tile, token_count))

    attend_task(
        tile_reader(query_ref),
        putter(out_refs[0].at[0] if stacked else stage_ref),
        row_count,
        width,
        parts,
        mask_of,
        level_ref,
        score_ref,
        score_scale,
    )
    if not stacked:
        hand_out(stage_ref, out_refs)


def attend_second(
    queries, chunks, parents, place, first_far, task_count, part_rows, score_scale, stacked, before
):
    _, _, row_count, width = queries.shape
    source_count = len(chunks[0])
    chunk_count = len(chunks)
    span_rows = 2 * part_rows
    fresh_rows = chunks[0][0].shape[0] - source_count * span_rows
    operands = [ref for chunk in chunks for ref in chunk]
    keys = source_count * part_rows + fresh_rows // 2
    out_rows = row_count + stat_rows
    out_specs, out_shape = result_arrays(task_count, out_rows, width, stacked)
    outs = pl.pallas_call(
        functools.partial(
            second_kernel,
            chunk_count,
            source_count,
            first_far,
            task_count,
            part_rows,
            score_scale,
            stacked,
        ),
        grid_spec=pltpu.PrefetchScalarGridSpec(
            num_scalar_prefetch=2,
            grid=(task_count,),
            in_specs=[
                pl.BlockSpec(
                    (1, None, row_count, width),
                    lambda step, parent, place: (
                        place[1] * source_count + lax.bitwise_xor(place[0], first_far + step),
                        1,
                        0,
                        0,
                    ),
                )
            ]
            + [pl.BlockSpec(memory_space=pl.ANY)] * (len(operands) + len(before)),
            out_specs=out_specs,
            scratch_shapes=task_scratch(row_count, width, keys)
            + [
                pltpu.VMEM((out_rows, width), jnp.bfloat16),
                pltpu.VMEM((2, source_count, span_rows, width), jnp.bfloat16),
                pltpu.VMEM((source_count, fresh_rows, width), jnp.bfloat16),
                pltpu.SemaphoreType.DMA((2, source_count)),
                pltpu.SemaphoreType.DMA((source_count,)),
            ],
        ),
        out_shape=out_shape,
        compiler_params=pltpu.CompilerParams(vmem_limit_bytes=vmem_bytes),
        cost_estimate=task_cost(task_count, row_count, keys, width),
        name="attend_second",
    )(parents, place, queries, *operands, *before)
    return outs[:-1], outs[-1]


def own_kernel(
    group_size, score_scale, place_ref, query_ref, key_ref, value_ref, out_ref, level_ref, score_ref
):
    token_count = key_ref.shape[1]
    _, row_count, width = query_ref.shape

    def mask_of(tile):
        row = tile * row_tile + lax.broadcasted_iota(jnp.int32, (row_tile, token_count), 0)
        column = lax.broadcasted_iota(jnp.int32, (row_tile, token_count), 1)
        return column * group_size <= row

    attend_task(
        tile_reader(query_ref),
        putter(out_ref.at[0]),
        row_count,
        width,
        [(lambda: key_ref[0], lambda: value_ref[0])],
        mask_of,
        level_ref,
        score_ref,
        score_scale,
    )


def attend_own(queries, depth, keys, values, place, score_scale):
    head_count, token_count, width = keys.shape
    row_count = queries.shape[2]

    def head_spec(rows):
        return pl.BlockSpec(
            (1, rows, width), lambda step, place: (lax.bitwise_xor(place[0], step), 0, 0)
        )

    return pl.pallas_call(
        functools.partial(own_kernel, row_count // token_count, score_scale),
        grid_spec=pltpu.PrefetchScalarGridSpec(
            num_scalar_prefetch=1,
            grid=(head_count,),
            in_specs=[
                pl.BlockSpec(
                    (1, None, row_count, width),
                    lambda step, place: (lax.bitwise_xor(place[0], step), depth, 0, 0),
                ),
                head_spec(token_count),
                head_spec(token_count),
            ],
            out_specs=pl.BlockSpec(
                (1, row_count + stat_rows, width), lambda step, place: (step, 0, 0)
            ),
            scratch_shapes=task_scratch(row_count, width, token_count),
        ),
        out_shape=jax.ShapeDtypeStruct((head_count, row_count + stat_rows, width), jnp.bfloat16),
        compiler_params=pltpu.CompilerParams(vmem_limit_bytes=vmem_bytes),
        cost_estimate=task_cost(head_count, row_count, token_count, width),
        name="attend_own",
    )(place, queries, keys, values)


def merge_kernel(head_count, group_size, part_count, place_ref, *refs):
    part_refs, own_ref = refs[:part_count], refs[part_count]
    refs = refs[part_count + 1 :]
    stat_refs, own_stat_ref = refs[:part_count], refs[part_count]
    out_ref, mixed_ref = refs[-2:]
    token_tile, _, lanes = out_ref.shape[1:]
    stat_tile = token_tile * group_size // lanes
    step = pl.program_id(0)
    picks = eye(lanes)
    ones = jnp.ones((2 * lanes, lanes), jnp.bfloat16)
    span = stat_rows // 4

    for far in range(head_count):
        head = lax.bitwise_xor(place_ref[0], far)
        sources = [part_refs[place] for place in range(far, part_count, head_count)]
        sources.append(own_ref.at[far])
        stats = [stat_refs[place][...] for place in range(far, part_count, head_count)]
        stats.append(own_stat_ref[far])
        stats = [stat.astype(jnp.float32) for stat in stats]
        level = [
            stat[:span] + stat[span : 2 * span] + stat[2 * span : 3 * span] for stat in stats
        ]
        top = functools.reduce(jnp.maximum, level)
        shares = [jnp.exp(one - top) for one in level]
        total = functools.reduce(jnp.add, shares)
        shares = [one / total for one in shares]
        lines = []
        for share in shares:
            for piece in range(stat_tile):
                chosen = (
                    lax.broadcasted_iota(jnp.int32, share.shape, 0) == step * stat_tile + piece
                )
                lines.append(jnp.sum(jnp.where(chosen, share, 0.0), axis=0, keepdims=True))
        scales = []
        for line in lines:
            high = line.astype(jnp.bfloat16).astype(jnp.float32)
            scales.append(
                jnp.concatenate(
                    [
                        jnp.where(picks, portion, 0.0).astype(jnp.bfloat16)
                        for portion in (high, line - high)
                    ],
                    1,
                )
            )
        columns = jnp.dot(
            jnp.concatenate(scales, 0), ones, preferred_element_type=jnp.float32
        )
        mixed = None
        rows = stat_tile * lanes
        for place, source in enumerate(sources):
            block = source[...].astype(jnp.float32) * columns[place * rows : (place + 1) * rows]
            mixed = block if mixed is None else mixed + block
        mixed_ref[
            :, pl.ds(pl.multiple_of(head * group_size, group_size), group_size), :
        ] = mixed.reshape(token_tile, group_size, lanes)
    out_ref[0] = mixed_ref[...].astype(out_ref.dtype)


def merge(parts, own, place, token_count, before=()):
    head_count, out_rows, width = own.shape
    row_count = out_rows - stat_rows
    group_size = row_count // token_count
    token_tile = 64
    rows = token_tile * group_size
    stat_block = row_count // stat_rows
    query_heads = head_count * group_size

    def specs(size, index):
        flat = pl.BlockSpec((size, width), lambda step, place: (index(step), 0))
        whole = pl.BlockSpec((head_count, size, width), lambda step, place: (0, index(step), 0))
        return [flat] * len(parts) + [whole]

    return pl.pallas_call(
        functools.partial(merge_kernel, head_count, group_size, len(parts)),
        grid_spec=pltpu.PrefetchScalarGridSpec(
            num_scalar_prefetch=1,
            grid=(token_count // token_tile,),
            in_specs=specs(rows, lambda step: step)
            + specs(stat_rows, lambda step: stat_block)
            + [pl.BlockSpec(memory_space=pl.ANY)] * len(before),
            out_specs=pl.BlockSpec(
                (1, token_tile, query_heads, width), lambda step, place: (0, step, 0, 0)
            ),
            scratch_shapes=[pltpu.VMEM((token_tile, query_heads, width), jnp.float32)],
        ),
        out_shape=jax.ShapeDtypeStruct((1, token_count, query_heads, width), jnp.bfloat16),
        compiler_params=pltpu.CompilerParams(vmem_limit_bytes=vmem_bytes),
        cost_estimate=pl.CostEstimate(
            flops=4 * (len(parts) + head_count) * row_count * width,
            bytes_accessed=4 * (len(parts) + head_count) * row_count * width,
            transcendentals=0,
        ),
        name="merge_parts",
    )(place, *parts, own, *parts, own, *before)


def local(
    queries_one,
    keys_one,
    values_one,
    queries_two,
    keys_two,
    values_two,
    cache_keys,
    cache_values,
    paths,
    parents,
    positions,
):
    here_index = lax.axis_index("node")
    peer_count = lax.axis_size("node")
    block_count, token_count, head_count, width = cache_keys.shape
    per_peer = paths.shape[1] // peer_count
    copies = peer_count // head_count
    score_scale = width ** (-0.5)
    my_head = here_index % head_count
    my_group = here_index // head_count
    part_rows = per_peer * token_count
    places = [
        jnp.stack([my_head, lax.bitwise_xor(my_group, apart), my_group]) for apart in range(copies)
    ]

    def swap(array, apart):
        return lax.ppermute(array, "node", [(node, node ^ apart) for node in range(peer_count)])

    cosine, sine_part = rotary_tables(positions[:, 0], width)
    send = turn_queries(queries_one, queries_two, cosine, sine_part, head_count, copies)
    got = lax.all_to_all(send, "node", split_axis=0, concat_axis=0, tiled=True)
    key_rot_one = rotary(keys_one[0], cosine[0], sine_part[0])
    key_rot_two = rotary(keys_two[0], cosine[1], sine_part[1])

    block_index = local_blocks(paths, here_index, block_count, per_peer).reshape(-1)
    order = list(range(1, copies)) + [0]
    chunks = [None] * copies
    before = (send,)
    for apart in order:
        packed = pack(
            cache_keys,
            cache_values,
            block_index,
            places[apart],
            () if apart else (key_rot_one, values_one[0]),
            per_peer,
            before,
        )
        chunks[apart] = [packed[0]] + [swap(packed[far], far) for far in range(1, head_count)]
        before = (packed[0],)

    own_one = attend_own(
        send,
        0,
        jnp.moveaxis(key_rot_one, 1, 0),
        jnp.moveaxis(values_one[0], 1, 0),
        places[0],
        score_scale,
    )
    own_two = attend_own(
        send,
        1,
        jnp.moveaxis(key_rot_two, 1, 0),
        jnp.moveaxis(values_two[0], 1, 0),
        places[0],
        score_scale,
    )

    def send_home(apart, first_far, rows):
        base = apart * head_count + first_far
        return [swap(row, base + far) for far, row in enumerate(rows)]

    def first(apart, first_far, task_count, stacked, before):
        rows, mark = attend_first(
            got,
            chunks[apart],
            places[apart],
            first_far,
            task_count,
            part_rows,
            score_scale,
            stacked,
            before,
        )
        return rows, (mark,)

    def second(apart, first_far, task_count, stacked, before):
        rows, mark = attend_second(
            got,
            chunks,
            parents,
            places[apart],
            first_far,
            task_count,
            part_rows,
            score_scale,
            stacked,
            before,
        )
        return rows, (mark,)

    far_one, far_two = [], []
    before = (own_one, own_two)
    for apart in order[:-1]:
        rows, before = first(apart, 0, 1, False, before)
        far_one += send_home(apart, 0, rows)
        rows, before = first(apart, 1, head_count - 1, False, before)
        far_one += send_home(apart, 1, rows)
    for number, apart in enumerate(order[:-1]):
        rows, before = second(apart, 0, 1, False, before)
        far_two += send_home(apart, 0, rows)
        arrived = far_one[number * head_count : (number + 1) * head_count]
        rows, before = second(apart, 1, head_count - 1, False, (*before, *arrived[:2]))
        far_two += send_home(apart, 1, rows)
        before = (*before, *arrived[2:])
    rows, before = first(0, 1, head_count - 1, False, before)
    near_one = send_home(0, 1, rows)
    rows, before = second(0, 1, head_count - 1, False, (*before, *far_two[:2]))
    near_two = send_home(0, 1, rows)
    rows, before = first(0, 0, 1, False, before)
    near_one = [*rows, *near_one]
    rows, before = second(0, 0, 1, False, before)
    near_two = [*rows, *near_two]
    before = (*before, far_two[2])
    return (
        merge(far_one + near_one, own_one, places[0], token_count, before),
        merge(far_two + near_two, own_two, places[0], token_count),
    )


def solution(mesh):
    in_specs = (
        P(("group", "node"), None, "head", None),
        P(("group", "node"), None, "head", None),
        P(("group", "node"), None, "head", None),
        P(("group", "node"), None, "head", None),
        P(("group", "node"), None, "head", None),
        P(("group", "node"), None, "head", None),
        P(("group", "node"), None, "head", None),
        P(("group", "node"), None, "head", None),
        P("group", None),
        P("group"),
        P(None, ("group", "node"), None),
    )
    out_specs = (P(("group", "node"), None, "head", None), P(("group", "node"), None, "head", None))
    return jax.shard_map(
        local,
        mesh=mesh,
        in_specs=in_specs,
        out_specs=out_specs,
        check_vma=False,
    )
```

```python
import functools

import jax
import jax.numpy as jnp
from jax import lax
from jax.experimental import pallas as pl
from jax.experimental.pallas import tpu as pltpu
from jax.sharding import PartitionSpec as P

rope_theta = 500000.0
log2_e = 1.4426950408889634
stat_rows = 32
row_tile = 256
vmem_bytes = 56 * 1024 * 1024


def rotary_tables(positions, head_width):
    half_width = head_width // 2
    frequency = rope_theta ** (-(jnp.arange(half_width, dtype=jnp.float32) * 2.0) / head_width)
    angles = positions.astype(jnp.float32)[..., None] * frequency
    cosine = jnp.cos(angles)
    sine_part = jnp.sin(angles)
    return jnp.concatenate([cosine, cosine], -1), jnp.concatenate([-sine_part, sine_part], -1)


def rotary(vector, cosine, signed_sine):
    widened = vector.astype(jnp.float32)
    swapped = jnp.roll(widened, widened.shape[-1] // 2, axis=-1)
    turned = widened * cosine[:, None, :] + swapped * signed_sine[:, None, :]
    return turned.astype(jnp.bfloat16)


def turn_kernel(head_count, copies, first_ref, second_ref, cosine_ref, sine_ref, out_ref):
    token_tile, query_heads, width = first_ref.shape[1:]
    group_size = query_heads // head_count
    rows = token_tile * group_size
    for depth, query_ref in enumerate((first_ref, second_ref)):
        widened = query_ref[0].astype(jnp.float32)
        swapped = pltpu.roll(widened.reshape(token_tile * query_heads, width), width // 2, 1)
        swapped = swapped.reshape(token_tile, query_heads, width)
        turned = widened * cosine_ref[depth][:, None, :] + swapped * sine_ref[depth][:, None, :]
        for head in range(head_count):
            turned_head = turned[:, head * group_size : (head + 1) * group_size, :]
            turned_head = turned_head.reshape(rows, width).astype(jnp.bfloat16)
            for copy in range(copies):
                out_ref[copy * head_count + head, depth] = turned_head


def turn_queries(queries_one, queries_two, cosine, sine_part, head_count, copies):
    _, token_count, query_heads, width = queries_one.shape
    token_tile = 32
    rows = token_tile * query_heads // head_count
    query_spec = pl.BlockSpec((1, token_tile, query_heads, width), lambda step: (0, step, 0, 0))
    table_spec = pl.BlockSpec((2, token_tile, width), lambda step: (0, step, 0))
    return pl.pallas_call(
        functools.partial(turn_kernel, head_count, copies),
        grid=(token_count // token_tile,),
        in_specs=[query_spec, query_spec, table_spec, table_spec],
        out_specs=pl.BlockSpec(
            (head_count * copies, 2, rows, width), lambda step: (0, 0, step, 0)
        ),
        out_shape=jax.ShapeDtypeStruct(
            (head_count * copies, 2, token_count * query_heads // head_count, width), jnp.bfloat16
        ),
        compiler_params=pltpu.CompilerParams(vmem_limit_bytes=vmem_bytes),
        cost_estimate=pl.CostEstimate(
            flops=8 * queries_one.size, bytes_accessed=12 * queries_one.size, transcendentals=0
        ),
        name="turn_queries",
    )(queries_one, queries_two, cosine, sine_part)


def local_blocks(paths, here_index, per_owner, per_peer):
    is_local = paths // per_owner == here_index
    slot_rank = jnp.cumsum(is_local.astype(jnp.int32), axis=1) - 1
    slot_range = jnp.arange(per_peer, dtype=jnp.int32)
    selected = jnp.logical_and(
        is_local[:, :, None], slot_rank[:, :, None] == slot_range[None, None, :]
    )
    return jnp.sum(jnp.where(selected, (paths % per_owner)[:, :, None], 0), axis=1)


def pack_kernel(per_peer, head_count, token_count, near, index_ref, place_ref, *refs):
    key_refs = refs[:per_peer]
    value_refs = refs[per_peer : 2 * per_peer]
    new_refs = refs[2 * per_peer : 2 * per_peer + 2] if near else ()
    out_refs, wide = refs[-1 - head_count * (2 if near else 1) : -1], refs[-1]
    step = pl.program_id(0)
    mine = place_ref[0]
    span_rows = 2 * per_peer * token_count
    half = head_count // 2

    def spread(rows, put):
        wide[...] = rows.astype(jnp.float32)
        for far in range(head_count):
            head = lax.bitwise_xor(mine, far)
            picked = wide[pl.ds(head, token_count, stride=head_count), :]
            put(far, head, picked.astype(jnp.bfloat16))

    for which, source_refs in enumerate((key_refs, value_refs)):
        for slot, source in enumerate(source_refs):
            offset = (which * per_peer + slot) * token_count

            def put(far, head, rows):
                if not near:
                    start = pl.multiple_of(step * span_rows + offset, token_count)
                    out_refs[far][pl.ds(start, token_count), :] = rows
                    return
                apart = lax.bitwise_xor(step, head)
                start = pl.multiple_of((apart % half) * span_rows + offset, token_count)

                @pl.when(apart >= half)
                def _():
                    out_refs[far][pl.ds(start, token_count), :] = rows

                @pl.when(apart < half)
                def _():
                    out_refs[head_count + far][pl.ds(start, token_count), :] = rows

            spread(source[0], put)
    if near:

        @pl.when(step == 0)
        def _():
            for which, source in enumerate(new_refs):
                start = half * span_rows + which * token_count

                def put(far, head, rows):
                    out_refs[far][start : start + token_count, :] = rows

                spread(source[...], put)


def pack(cache_keys, cache_values, block_index, place, new_rows, per_peer, before=()):
    block_count, token_count, head_count, width = cache_keys.shape
    flat_keys = cache_keys.reshape(block_count, token_count * head_count, width)
    flat_values = cache_values.reshape(block_count, token_count * head_count, width)
    span_rows = 2 * per_peer * token_count
    near = bool(new_rows)
    half_rows = head_count // 2 * span_rows
    out_rows = half_rows + 2 * token_count if near else head_count * span_rows
    shapes = [(out_rows, width)] * head_count
    if near:
        shapes += [(half_rows, width)] * head_count

    def block_spec(slot):
        return pl.BlockSpec(
            (1, token_count * head_count, width),
            lambda step, index, place: (
                index[(place[1] * head_count + step) * per_peer + slot],
                0,
                0,
            ),
        )

    def whole_spec(shape):
        return pl.BlockSpec(shape, lambda step, index, place: (0,) * len(shape))

    cache_specs = [block_spec(slot) for slot in range(per_peer)]
    new_spec = pl.BlockSpec((token_count * head_count, width), lambda step, index, place: (0, 0))
    operands = [flat_keys] * per_peer + [flat_values] * per_peer
    operands += [row.reshape(token_count * head_count, width) for row in new_rows]
    return pl.pallas_call(
        functools.partial(pack_kernel, per_peer, head_count, token_count, near),
        grid_spec=pltpu.PrefetchScalarGridSpec(
            num_scalar_prefetch=2,
            grid=(head_count,),
            in_specs=cache_specs
            + cache_specs
            + [new_spec] * len(new_rows)
            + [pl.BlockSpec(memory_space=pl.ANY)] * len(before),
            out_specs=[whole_spec(shape) for shape in shapes],
            scratch_shapes=[pltpu.VMEM((token_count * head_count, width), jnp.float32)],
        ),
        out_shape=[jax.ShapeDtypeStruct(shape, jnp.bfloat16) for shape in shapes],
        compiler_params=pltpu.CompilerParams(vmem_limit_bytes=vmem_bytes),
        cost_estimate=pl.CostEstimate(
            flops=0, bytes_accessed=4 * head_count * out_rows * width, transcendentals=0
        ),
        name="pack_rows",
    )(block_index, place, *operands, *before)


def eye(size):
    return lax.broadcasted_iota(jnp.int32, (size, size), 0) == lax.broadcasted_iota(
        jnp.int32, (size, size), 1
    )


def product(left, right):
    return lax.dot_general(
        left, right, (((1,), (1,)), ((), ())), preferred_element_type=jnp.float32
    )


def fold_lanes(array, width, operation):
    pieces = [array[:, start : start + width] for start in range(0, array.shape[1], width)]
    while len(pieces) > 1:
        pieces = [
            operation(*pieces[start : start + 2]) if start + 1 < len(pieces) else pieces[start]
            for start in range(0, len(pieces), 2)
        ]
    return pieces[0]


def attend_task(query_of, put, row_count, width, parts, mask_of, level_ref, score_ref, score_scale):
    tile_count = row_count // row_tile

    def make_scores(tile):
        query = query_of(tile)
        top, start = None, 0
        for place, (keys, _) in enumerate(parts):
            scores = product(query, keys())
            if mask_of is not None and place == len(parts) - 1:
                scores = jnp.where(mask_of(tile), scores, -1e30)
            size = scores.shape[1]
            score_ref[tile % 2, :, start : start + size] = scores
            start += size
            folded = fold_lanes(scores, width, jnp.maximum)
            top = folded if top is None else jnp.maximum(top, folded)
        return jnp.max(top, axis=-1, keepdims=True)

    picks = eye(width)
    row_max = make_scores(0)
    for tile in range(tile_count):
        next_max = make_scores(tile + 1) if tile + 1 < tile_count else None
        total, mixture, start = None, None, 0
        for _, values in parts:
            value_rows = values()
            size = value_rows.shape[0]
            scores = score_ref[tile % 2, :, start : start + size]
            start += size
            weights = jnp.exp2((scores - row_max) * (score_scale * log2_e))
            folded = fold_lanes(weights, width, jnp.add)
            total = folded if total is None else total + folded
            mixed = jnp.dot(
                weights.astype(jnp.bfloat16), value_rows, preferred_element_type=jnp.float32
            )
            mixture = mixed if mixture is None else mixture + mixed
        total = jnp.sum(total, axis=-1, keepdims=True)
        put(tile * row_tile, (mixture / total).astype(jnp.bfloat16))
        level = row_max * score_scale + jnp.log(total)
        for piece in range(row_tile // width):
            line = jnp.where(picks, level[piece * width : (piece + 1) * width], 0.0)
            row = tile * (row_tile // width) + piece
            level_ref[row : row + 1, :] = jnp.sum(line, axis=0, keepdims=True)
        row_max = next_max
    levels = level_ref[...]
    high = levels.astype(jnp.bfloat16).astype(jnp.float32)
    middle = (levels - high).astype(jnp.bfloat16).astype(jnp.float32)
    low = levels - high - middle
    stats = jnp.concatenate([high, middle, low, jnp.zeros_like(levels)], 0)
    put(row_count, stats.astype(jnp.bfloat16))


def putter(out_ref):
    def put(start, rows):
        out_ref[start : start + rows.shape[0], :] = rows

    return put


def hand_out(stage_ref, out_refs):
    for far, out_ref in enumerate(out_refs):

        @pl.when(pl.program_id(0) == far)
        def _():
            out_ref[...] = stage_ref[...]


def tile_reader(query_ref):
    return lambda tile: query_ref[0, tile * row_tile : (tile + 1) * row_tile, :]


def task_scratch(row_count, width, key_count):
    return [
        pltpu.VMEM((row_count // width, width), jnp.float32),
        pltpu.VMEM((2, row_tile, key_count), jnp.float32),
    ]


def task_cost(task_count, row_count, key_count, width):
    return pl.CostEstimate(
        flops=4 * task_count * row_count * key_count * width,
        bytes_accessed=4 * task_count * (row_count + key_count) * width,
        transcendentals=task_count * row_count * key_count,
    )


def first_kernel(source_count, task_count, part_rows, score_scale, place_ref, query_ref, *refs):
    source_refs = refs[:source_count]
    out_refs = refs[-4 - task_count : -4]
    mark_ref, level_ref, score_ref, stage_ref = refs[-4:]
    _, row_count, width = query_ref.shape
    mark_ref[...] = jnp.zeros_like(mark_ref)
    parts = [
        (
            functools.partial(lambda ref: ref[0:part_rows, :], ref),
            functools.partial(lambda ref: ref[part_rows : 2 * part_rows, :], ref),
        )
        for ref in source_refs
    ]
    attend_task(
        tile_reader(query_ref),
        putter(stage_ref),
        row_count,
        width,
        parts,
        None,
        level_ref,
        score_ref,
        score_scale,
    )
    hand_out(stage_ref, out_refs)


def attend_first(queries, sources, place, task_of, slot_of, task_count, part_rows, score_scale, before):
    _, _, row_count, width = queries.shape
    out_rows = row_count + stat_rows
    span_rows = 2 * part_rows
    source_spec = pl.BlockSpec(
        (span_rows, width), lambda step, place: (slot_of(task_of(step), place), 0)
    )
    outs = pl.pallas_call(
        functools.partial(first_kernel, len(sources), task_count, part_rows, score_scale),
        grid_spec=pltpu.PrefetchScalarGridSpec(
            num_scalar_prefetch=1,
            grid=(task_count,),
            in_specs=[
                pl.BlockSpec(
                    (1, None, row_count, width),
                    lambda step, place: (lax.bitwise_xor(place[2], task_of(step)), 0, 0, 0),
                )
            ]
            + [source_spec] * len(sources)
            + [pl.BlockSpec(memory_space=pl.ANY)] * len(before),
            out_specs=[pl.BlockSpec((out_rows, width), lambda step, place: (0, 0))] * task_count
            + [pl.BlockSpec((8, width), lambda step, place: (0, 0))],
            scratch_shapes=task_scratch(row_count, width, len(sources) * part_rows)
            + [pltpu.VMEM((out_rows, width), jnp.bfloat16)],
        ),
        out_shape=[jax.ShapeDtypeStruct((out_rows, width), jnp.bfloat16)] * task_count
        + [jax.ShapeDtypeStruct((8, width), jnp.float32)],
        compiler_params=pltpu.CompilerParams(vmem_limit_bytes=vmem_bytes),
        cost_estimate=task_cost(task_count, row_count, len(sources) * part_rows, width),
        name="attend_first",
    )(place, queries, *sources, *before)
    return outs[:-1], (outs[-1],)


def second_kernel(
    head_count, far_chunks, task_of, task_count, part_rows, score_scale, parent_ref, place_ref, query_ref, *refs
):
    further_refs = refs[:head_count]
    nearer_refs = refs[head_count : 2 * head_count]
    far_refs = refs[2 * head_count : (2 + far_chunks) * head_count]
    out_refs = refs[-8 - task_count : -8]
    mark_ref, level_ref, score_ref, stage_ref, held, fresh = refs[-8:-2]
    semaphores, fresh_semaphores = refs[-2:]
    _, row_count, width = query_ref.shape
    span_rows = 2 * part_rows
    token_count = fresh.shape[1] // 2
    half = head_count // 2
    step = pl.program_id(0)
    node = place_ref[2]
    mark_ref[...] = jnp.zeros_like(mark_ref)

    def parent_at(number):
        return parent_ref[lax.bitwise_xor(node, task_of(number))]

    def fetch(number):
        parent = parent_at(number)
        apart = lax.bitwise_xor(parent, node)

        def bring(chosen, source_refs, slot):
            @pl.when(chosen)
            def _():
                rows = pl.ds(pl.multiple_of(slot * span_rows, span_rows), span_rows)
                for source in range(head_count):
                    pltpu.make_async_copy(
                        source_refs[source].at[rows],
                        held.at[number % 2, source],
                        semaphores.at[number % 2, source],
                    ).start()

        bring(apart < half, nearer_refs, apart)
        bring(jnp.logical_and(apart >= half, apart < head_count), further_refs, apart - half)
        for chunk in range(far_chunks):
            bring(
                apart // head_count == chunk + 1,
                far_refs[chunk * head_count : (chunk + 1) * head_count],
                parent % head_count,
            )

    @pl.when(step == 0)
    def _():
        fetch(0)
        fresh_copies = [
            pltpu.make_async_copy(
                further_refs[source].at[pl.ds(half * span_rows, 2 * token_count)],
                fresh.at[source],
                fresh_semaphores.at[source],
            )
            for source in range(head_count)
        ]
        for copy in fresh_copies:
            copy.start()
        for copy in fresh_copies:
            copy.wait()

    @pl.when(step + 1 < task_count)
    def _():
        fetch(step + 1)

    slot = step % 2
    for source in range(head_count):
        pltpu.make_async_copy(
            further_refs[source].at[pl.ds(0, span_rows)],
            held.at[slot, source],
            semaphores.at[slot, source],
        ).wait()
    apart = lax.bitwise_xor(parent_at(step), node)
    place = jnp.where(apart < head_count, apart, 0)
    parts = [
        (
            functools.partial(lambda source: held[slot, source, 0:part_rows, :], source),
            functools.partial(lambda source: held[slot, source, part_rows:span_rows, :], source),
        )
        for source in range(head_count)
    ]
    parts.append(
        (
            lambda: fresh[place, 0:token_count, :],
            lambda: fresh[place, token_count : 2 * token_count, :],
        )
    )

    def mask_of(tile):
        return jnp.broadcast_to(apart < head_count, (row_tile, token_count))

    attend_task(
        tile_reader(query_ref),
        putter(stage_ref),
        row_count,
        width,
        parts,
        mask_of,
        level_ref,
        score_ref,
        score_scale,
    )
    hand_out(stage_ref, out_refs)


def attend_second(
    queries, further, nearer, far, parents, place, task_of, task_count, part_rows, score_scale, before
):
    _, _, row_count, width = queries.shape
    head_count = len(further)
    span_rows = 2 * part_rows
    fresh_rows = further[0].shape[0] - head_count // 2 * span_rows
    keys = head_count * part_rows + fresh_rows // 2
    out_rows = row_count + stat_rows
    operands = [row for rows in (further, nearer, *far) for row in rows] + [*before]
    outs = pl.pallas_call(
        functools.partial(
            second_kernel, head_count, len(far), task_of, task_count, part_rows, score_scale
        ),
        grid_spec=pltpu.PrefetchScalarGridSpec(
            num_scalar_prefetch=2,
            grid=(task_count,),
            in_specs=[
                pl.BlockSpec(
                    (1, None, row_count, width),
                    lambda step, parent, place: (lax.bitwise_xor(place[2], task_of(step)), 1, 0, 0),
                )
            ]
            + [pl.BlockSpec(memory_space=pl.ANY)] * len(operands),
            out_specs=[pl.BlockSpec((out_rows, width), lambda step, parent, place: (0, 0))]
            * task_count
            + [pl.BlockSpec((8, width), lambda step, parent, place: (0, 0))],
            scratch_shapes=task_scratch(row_count, width, keys)
            + [
                pltpu.VMEM((out_rows, width), jnp.bfloat16),
                pltpu.VMEM((2, head_count, span_rows, width), jnp.bfloat16),
                pltpu.VMEM((head_count, fresh_rows, width), jnp.bfloat16),
                pltpu.SemaphoreType.DMA((2, head_count)),
                pltpu.SemaphoreType.DMA((head_count,)),
            ],
        ),
        out_shape=[jax.ShapeDtypeStruct((out_rows, width), jnp.bfloat16)] * task_count
        + [jax.ShapeDtypeStruct((8, width), jnp.float32)],
        compiler_params=pltpu.CompilerParams(vmem_limit_bytes=vmem_bytes),
        cost_estimate=task_cost(task_count, row_count, keys, width),
        name="attend_second",
    )(parents, place, queries, *operands)
    return outs[:-1], (outs[-1],)


def own_kernel(
    group_size, score_scale, place_ref, query_ref, key_ref, value_ref, out_ref, level_ref, score_ref
):
    token_count = key_ref.shape[1]
    _, row_count, width = query_ref.shape

    def mask_of(tile):
        row = tile * row_tile + lax.broadcasted_iota(jnp.int32, (row_tile, token_count), 0)
        column = lax.broadcasted_iota(jnp.int32, (row_tile, token_count), 1)
        return column * group_size <= row

    attend_task(
        tile_reader(query_ref),
        putter(out_ref.at[0]),
        row_count,
        width,
        [(lambda: key_ref[0], lambda: value_ref[0])],
        mask_of,
        level_ref,
        score_ref,
        score_scale,
    )


def attend_own(queries, depth, keys, values, place, score_scale):
    head_count, token_count, width = keys.shape
    row_count = queries.shape[2]

    def head_spec(rows):
        return pl.BlockSpec(
            (1, rows, width), lambda step, place: (lax.bitwise_xor(place[0], step), 0, 0)
        )

    return pl.pallas_call(
        functools.partial(own_kernel, row_count // token_count, score_scale),
        grid_spec=pltpu.PrefetchScalarGridSpec(
            num_scalar_prefetch=1,
            grid=(head_count,),
            in_specs=[
                pl.BlockSpec(
                    (1, None, row_count, width),
                    lambda step, place: (lax.bitwise_xor(place[0], step), depth, 0, 0),
                ),
                head_spec(token_count),
                head_spec(token_count),
            ],
            out_specs=pl.BlockSpec(
                (1, row_count + stat_rows, width), lambda step, place: (step, 0, 0)
            ),
            scratch_shapes=task_scratch(row_count, width, token_count),
        ),
        out_shape=jax.ShapeDtypeStruct((head_count, row_count + stat_rows, width), jnp.bfloat16),
        compiler_params=pltpu.CompilerParams(vmem_limit_bytes=vmem_bytes),
        cost_estimate=task_cost(head_count, row_count, token_count, width),
        name="attend_own",
    )(place, queries, keys, values)


def merge_kernel(head_count, group_size, part_count, place_ref, *refs):
    part_refs, own_ref = refs[:part_count], refs[part_count]
    refs = refs[part_count + 1 :]
    stat_refs, own_stat_ref = refs[:part_count], refs[part_count]
    out_ref, mixed_ref = refs[-2:]
    token_tile, _, lanes = out_ref.shape[1:]
    stat_tile = token_tile * group_size // lanes
    step = pl.program_id(0)
    picks = eye(lanes)
    ones = jnp.ones((2 * lanes, lanes), jnp.bfloat16)
    span = stat_rows // 4

    for far in range(head_count):
        head = lax.bitwise_xor(place_ref[0], far)
        sources = [part_refs[place] for place in range(far, part_count, head_count)]
        sources.append(own_ref.at[far])
        stats = [stat_refs[place][...] for place in range(far, part_count, head_count)]
        stats.append(own_stat_ref[far])
        stats = [stat.astype(jnp.float32) for stat in stats]
        level = [
            stat[:span] + stat[span : 2 * span] + stat[2 * span : 3 * span] for stat in stats
        ]
        top = functools.reduce(jnp.maximum, level)
        shares = [jnp.exp(one - top) for one in level]
        total = functools.reduce(jnp.add, shares)
        shares = [one / total for one in shares]
        lines = []
        for share in shares:
            for piece in range(stat_tile):
                chosen = (
                    lax.broadcasted_iota(jnp.int32, share.shape, 0) == step * stat_tile + piece
                )
                lines.append(jnp.sum(jnp.where(chosen, share, 0.0), axis=0, keepdims=True))
        scales = []
        for line in lines:
            high = line.astype(jnp.bfloat16).astype(jnp.float32)
            scales.append(
                jnp.concatenate(
                    [
                        jnp.where(picks, portion, 0.0).astype(jnp.bfloat16)
                        for portion in (high, line - high)
                    ],
                    1,
                )
            )
        columns = jnp.dot(
            jnp.concatenate(scales, 0), ones, preferred_element_type=jnp.float32
        )
        mixed = None
        rows = stat_tile * lanes
        for place, source in enumerate(sources):
            block = source[...].astype(jnp.float32) * columns[place * rows : (place + 1) * rows]
            mixed = block if mixed is None else mixed + block
        mixed_ref[
            :, pl.ds(pl.multiple_of(head * group_size, group_size), group_size), :
        ] = mixed.reshape(token_tile, group_size, lanes)
    out_ref[0] = mixed_ref[...].astype(out_ref.dtype)


def merge(parts, own, place, token_count, before=()):
    head_count, out_rows, width = own.shape
    row_count = out_rows - stat_rows
    group_size = row_count // token_count
    token_tile = 64
    rows = token_tile * group_size
    stat_block = row_count // stat_rows
    query_heads = head_count * group_size

    def specs(size, index):
        flat = pl.BlockSpec((size, width), lambda step, place: (index(step), 0))
        whole = pl.BlockSpec((head_count, size, width), lambda step, place: (0, index(step), 0))
        return [flat] * len(parts) + [whole]

    return pl.pallas_call(
        functools.partial(merge_kernel, head_count, group_size, len(parts)),
        grid_spec=pltpu.PrefetchScalarGridSpec(
            num_scalar_prefetch=1,
            grid=(token_count // token_tile,),
            in_specs=specs(rows, lambda step: step)
            + specs(stat_rows, lambda step: stat_block)
            + [pl.BlockSpec(memory_space=pl.ANY)] * len(before),
            out_specs=pl.BlockSpec(
                (1, token_tile, query_heads, width), lambda step, place: (0, step, 0, 0)
            ),
            scratch_shapes=[pltpu.VMEM((token_tile, query_heads, width), jnp.float32)],
        ),
        out_shape=jax.ShapeDtypeStruct((1, token_count, query_heads, width), jnp.bfloat16),
        compiler_params=pltpu.CompilerParams(vmem_limit_bytes=vmem_bytes),
        cost_estimate=pl.CostEstimate(
            flops=4 * (len(parts) + head_count) * row_count * width,
            bytes_accessed=4 * (len(parts) + head_count) * row_count * width,
            transcendentals=0,
        ),
        name="merge_parts",
    )(place, *parts, own, *parts, own, *before)


def local(
    queries_one,
    keys_one,
    values_one,
    queries_two,
    keys_two,
    values_two,
    cache_keys,
    cache_values,
    paths,
    parents,
    positions,
):
    here_index = lax.axis_index("node")
    peer_count = lax.axis_size("node")
    block_count, token_count, head_count, width = cache_keys.shape
    per_peer = paths.shape[1] // peer_count
    copies = peer_count // head_count
    score_scale = width ** (-0.5)
    my_head = here_index % head_count
    my_group = here_index // head_count
    part_rows = per_peer * token_count
    places = [
        jnp.stack([my_head, lax.bitwise_xor(my_group, apart), here_index])
        for apart in range(copies)
    ]

    def swap(array, apart):
        return lax.ppermute(array, "node", [(node, node ^ apart) for node in range(peer_count)])

    cosine, sine_part = rotary_tables(positions[:, 0], width)
    send = turn_queries(queries_one, queries_two, cosine, sine_part, head_count, copies)
    got = lax.all_to_all(send, "node", split_axis=0, concat_axis=0, tiled=True)
    key_rot_one = rotary(keys_one[0], cosine[0], sine_part[0])
    key_rot_two = rotary(keys_two[0], cosine[1], sine_part[1])

    block_index = local_blocks(paths, here_index, block_count, per_peer).reshape(-1)
    chunks = []
    before = (send,)
    for apart in range(1, copies):
        packed = pack(
            cache_keys, cache_values, block_index, places[apart], (), per_peer, before
        )
        chunks.append([packed[0]] + [swap(packed[far], far) for far in range(1, head_count)])
        before = (packed[0],)
    packed = pack(
        cache_keys,
        cache_values,
        block_index,
        places[0],
        (key_rot_one, values_one[0]),
        per_peer,
        before,
    )
    further = [packed[0]] + [swap(packed[far], far) for far in range(1, head_count)]
    nearer = [packed[head_count]] + [
        swap(packed[head_count + far], far) for far in range(1, head_count)
    ]

    own_one = attend_own(
        send,
        0,
        jnp.moveaxis(key_rot_one, 1, 0),
        jnp.moveaxis(values_one[0], 1, 0),
        places[0],
        score_scale,
    )
    own_two = attend_own(
        send,
        1,
        jnp.moveaxis(key_rot_two, 1, 0),
        jnp.moveaxis(values_two[0], 1, 0),
        places[0],
        score_scale,
    )

    half = head_count // 2
    parts_one, parts_two = [None] * peer_count, [None] * peer_count

    def send_home(parts, tasks, rows):
        for task, row in zip(tasks, rows):
            parts[task] = swap(row, task) if task else row

    def first(sources, tasks, task_of, slot_of, before):
        rows, before = attend_first(
            got,
            sources,
            places[0],
            task_of,
            slot_of,
            len(tasks),
            part_rows,
            score_scale,
            before,
        )
        send_home(parts_one, tasks, rows)
        return before

    def second(tasks, task_of, before):
        rows, before = attend_second(
            got,
            further,
            nearer,
            chunks,
            parents,
            places[0],
            task_of,
            len(tasks),
            part_rows,
            score_scale,
            before,
        )
        send_home(parts_two, tasks, rows)
        return before

    def far_slot(task, place):
        return lax.bitwise_xor(task % head_count, place[0])

    before = (own_one, own_two)
    for apart in range(1, copies):
        base = apart * head_count
        before = first(chunks[apart - 1], [base], lambda step: base, far_slot, before)
        before = first(
            chunks[apart - 1],
            list(range(base + 1, base + head_count)),
            lambda step: base + 1 + step,
            far_slot,
            before,
        )
    before = first(
        further,
        list(range(half, head_count)),
        lambda step: half + step,
        lambda task, place: task - half,
        before,
    )
    for apart in range(1, copies):
        base = apart * head_count
        before = second([base], lambda step: base, before)
        before = (*before, *parts_one[base : base + 2])
        before = second(
            list(range(base + 1, base + head_count)), lambda step: base + 1 + step, before
        )
        before = (*before, *parts_one[base + 2 : base + head_count])
    before = first(
        nearer,
        list(range(1, half)) + [0],
        lambda step: (step + 1) % half,
        lambda task, place: task,
        (*before, *parts_one[half:head_count]),
    )
    before = second(
        list(range(1, head_count)),
        lambda step: step + 1,
        before,
    )
    before = second([0], lambda step: 0, before)
    before = (*before, *parts_two[head_count : head_count + 3])
    return (
        merge(parts_one, own_one, places[0], token_count, before),
        merge(parts_two, own_two, places[0], token_count),
    )


def solution(mesh):
    in_specs = (
        P(("group", "node"), None, "head", None),
        P(("group", "node"), None, "head", None),
        P(("group", "node"), None, "head", None),
        P(("group", "node"), None, "head", None),
        P(("group", "node"), None, "head", None),
        P(("group", "node"), None, "head", None),
        P(("group", "node"), None, "head", None),
        P(("group", "node"), None, "head", None),
        P("group", None),
        P("group"),
        P(None, ("group", "node"), None),
    )
    out_specs = (P(("group", "node"), None, "head", None), P(("group", "node"), None, "head", None))
    return jax.shard_map(
        local,
        mesh=mesh,
        in_specs=in_specs,
        out_specs=out_specs,
        check_vma=False,
    )
```

```python
import functools

import jax
import jax.numpy as jnp
from jax import lax
from jax.experimental import pallas as pl
from jax.experimental.pallas import tpu as pltpu
from jax.sharding import PartitionSpec as P

rope_theta = 500000.0
log2_e = 1.4426950408889634
stat_rows = 32
row_tile = 256
vmem_bytes = 56 * 1024 * 1024


def rotary_tables(positions, head_width):
    half_width = head_width // 2
    place = jnp.arange(head_width, dtype=jnp.int32)
    pair = (place % half_width).astype(jnp.float32)
    frequency = rope_theta ** (-(pair * 2.0) / head_width)
    angles = positions.astype(jnp.float32)[..., None] * frequency
    return jnp.cos(angles), jnp.where(place < half_width, -1.0, 1.0) * jnp.sin(angles)


def rotary(vector, cosine, signed_sine):
    widened = vector.astype(jnp.float32)
    swapped = jnp.roll(widened, widened.shape[-1] // 2, axis=-1)
    turned = widened * cosine[:, None, :] + swapped * signed_sine[:, None, :]
    return turned.astype(jnp.bfloat16)


def turn_kernel(head_count, copies, first_ref, second_ref, cosine_ref, sine_ref, out_ref):
    token_tile, query_heads, width = first_ref.shape[1:]
    group_size = query_heads // head_count
    rows = token_tile * group_size
    for depth, query_ref in enumerate((first_ref, second_ref)):
        widened = query_ref[0].astype(jnp.float32)
        swapped = pltpu.roll(widened.reshape(token_tile * query_heads, width), width // 2, 1)
        swapped = swapped.reshape(token_tile, query_heads, width)
        turned = widened * cosine_ref[depth][:, None, :] + swapped * sine_ref[depth][:, None, :]
        for head in range(head_count):
            turned_head = turned[:, head * group_size : (head + 1) * group_size, :]
            turned_head = turned_head.reshape(rows, width).astype(jnp.bfloat16)
            for copy in range(copies):
                out_ref[copy * head_count + head, depth] = turned_head


def turn_queries(queries_one, queries_two, cosine, sine_part, head_count, copies):
    _, token_count, query_heads, width = queries_one.shape
    token_tile = 64
    rows = token_tile * query_heads // head_count
    query_spec = pl.BlockSpec((1, token_tile, query_heads, width), lambda step: (0, step, 0, 0))
    table_spec = pl.BlockSpec((2, token_tile, width), lambda step: (0, step, 0))
    return pl.pallas_call(
        functools.partial(turn_kernel, head_count, copies),
        grid=(token_count // token_tile,),
        in_specs=[query_spec, query_spec, table_spec, table_spec],
        out_specs=pl.BlockSpec(
            (head_count * copies, 2, rows, width), lambda step: (0, 0, step, 0)
        ),
        out_shape=jax.ShapeDtypeStruct(
            (head_count * copies, 2, token_count * query_heads // head_count, width), jnp.bfloat16
        ),
        compiler_params=pltpu.CompilerParams(vmem_limit_bytes=vmem_bytes),
        cost_estimate=pl.CostEstimate(
            flops=8 * queries_one.size, bytes_accessed=12 * queries_one.size, transcendentals=0
        ),
        name="turn_queries",
    )(queries_one, queries_two, cosine, sine_part)


def local_blocks(paths, here_index, per_owner, per_peer):
    is_local = paths // per_owner == here_index
    slot_rank = jnp.cumsum(is_local.astype(jnp.int32), axis=1) - 1
    slot_range = jnp.arange(per_peer, dtype=jnp.int32)
    selected = jnp.logical_and(
        is_local[:, :, None], slot_rank[:, :, None] == slot_range[None, None, :]
    )
    return jnp.sum(jnp.where(selected, (paths % per_owner)[:, :, None], 0), axis=1)


def pack_kernel(per_peer, head_count, token_count, near, index_ref, place_ref, *refs):
    key_refs = refs[:per_peer]
    value_refs = refs[per_peer : 2 * per_peer]
    new_refs = refs[2 * per_peer : 2 * per_peer + 2] if near else ()
    out_refs, wide = refs[-1 - head_count * (2 if near else 1) : -1], refs[-1]
    step = pl.program_id(0)
    mine = place_ref[0]
    span_rows = 2 * per_peer * token_count
    half = head_count // 2

    def spread(rows, put):
        wide[...] = rows.astype(jnp.float32)
        for far in range(head_count):
            head = lax.bitwise_xor(mine, far)
            picked = wide[pl.ds(head, token_count, stride=head_count), :]
            put(far, head, picked.astype(jnp.bfloat16))

    for which, source_refs in enumerate((key_refs, value_refs)):
        for slot, source in enumerate(source_refs):
            offset = (which * per_peer + slot) * token_count

            def put(far, head, rows):
                if not near:
                    start = pl.multiple_of(step * span_rows + offset, token_count)
                    out_refs[far][pl.ds(start, token_count), :] = rows
                    return
                apart = lax.bitwise_xor(step, head)
                start = pl.multiple_of((apart % half) * span_rows + offset, token_count)

                @pl.when(apart >= half)
                def _():
                    out_refs[far][pl.ds(start, token_count), :] = rows

                @pl.when(apart < half)
                def _():
                    out_refs[head_count + far][pl.ds(start, token_count), :] = rows

            spread(source[0], put)
    if near:

        @pl.when(step == 0)
        def _():
            for which, source in enumerate(new_refs):
                start = half * span_rows + which * token_count

                def put(far, head, rows):
                    out_refs[far][start : start + token_count, :] = rows

                spread(source[...], put)


def pack(cache_keys, cache_values, block_index, place, new_rows, per_peer, before=()):
    block_count, token_count, head_count, width = cache_keys.shape
    flat_keys = cache_keys.reshape(block_count, token_count * head_count, width)
    flat_values = cache_values.reshape(block_count, token_count * head_count, width)
    span_rows = 2 * per_peer * token_count
    near = bool(new_rows)
    half_rows = head_count // 2 * span_rows
    out_rows = half_rows + 2 * token_count if near else head_count * span_rows
    shapes = [(out_rows, width)] * head_count
    if near:
        shapes += [(half_rows, width)] * head_count

    def block_spec(slot):
        return pl.BlockSpec(
            (1, token_count * head_count, width),
            lambda step, index, place: (
                index[(place[1] * head_count + step) * per_peer + slot],
                0,
                0,
            ),
        )

    def whole_spec(shape):
        return pl.BlockSpec(shape, lambda step, index, place: (0,) * len(shape))

    cache_specs = [block_spec(slot) for slot in range(per_peer)]
    new_spec = pl.BlockSpec((token_count * head_count, width), lambda step, index, place: (0, 0))
    operands = [flat_keys] * per_peer + [flat_values] * per_peer
    operands += [row.reshape(token_count * head_count, width) for row in new_rows]
    return pl.pallas_call(
        functools.partial(pack_kernel, per_peer, head_count, token_count, near),
        grid_spec=pltpu.PrefetchScalarGridSpec(
            num_scalar_prefetch=2,
            grid=(head_count,),
            in_specs=cache_specs
            + cache_specs
            + [new_spec] * len(new_rows)
            + [pl.BlockSpec(memory_space=pl.ANY)] * len(before),
            out_specs=[whole_spec(shape) for shape in shapes],
            scratch_shapes=[pltpu.VMEM((token_count * head_count, width), jnp.float32)],
        ),
        out_shape=[jax.ShapeDtypeStruct(shape, jnp.bfloat16) for shape in shapes],
        compiler_params=pltpu.CompilerParams(vmem_limit_bytes=vmem_bytes),
        cost_estimate=pl.CostEstimate(
            flops=0, bytes_accessed=4 * head_count * out_rows * width, transcendentals=0
        ),
        name="pack_rows",
    )(block_index, place, *operands, *before)


def eye(size):
    return lax.broadcasted_iota(jnp.int32, (size, size), 0) == lax.broadcasted_iota(
        jnp.int32, (size, size), 1
    )


def product(left, right):
    return lax.dot_general(
        left, right, (((1,), (1,)), ((), ())), preferred_element_type=jnp.float32
    )


def fold_lanes(array, width, operation):
    pieces = [array[:, start : start + width] for start in range(0, array.shape[1], width)]
    while len(pieces) > 1:
        pieces = [
            operation(*pieces[start : start + 2]) if start + 1 < len(pieces) else pieces[start]
            for start in range(0, len(pieces), 2)
        ]
    return pieces[0]


def attend_task(query_of, put, row_count, width, parts, mask_of, level_ref, score_ref, score_scale):
    tile_count = row_count // row_tile

    def make_scores(tile):
        query = query_of(tile)
        top, start = None, 0
        for place, (keys, _) in enumerate(parts):
            scores = product(query, keys())
            if mask_of is not None and place == len(parts) - 1:
                scores = jnp.where(mask_of(tile), scores, -1e30)
            size = scores.shape[1]
            score_ref[tile % 2, :, start : start + size] = scores
            start += size
            folded = fold_lanes(scores, width, jnp.maximum)
            top = folded if top is None else jnp.maximum(top, folded)
        return jnp.max(top, axis=-1, keepdims=True)

    picks = eye(width)
    row_max = make_scores(0)
    for tile in range(tile_count):
        next_max = make_scores(tile + 1) if tile + 1 < tile_count else None
        total, mixture, start = None, None, 0
        for _, values in parts:
            value_rows = values()
            size = value_rows.shape[0]
            scores = score_ref[tile % 2, :, start : start + size]
            start += size
            weights = jnp.exp2((scores - row_max) * (score_scale * log2_e))
            folded = fold_lanes(weights, width, jnp.add)
            total = folded if total is None else total + folded
            mixed = jnp.dot(
                weights.astype(jnp.bfloat16), value_rows, preferred_element_type=jnp.float32
            )
            mixture = mixed if mixture is None else mixture + mixed
        total = jnp.sum(total, axis=-1, keepdims=True)
        put(tile * row_tile, (mixture / total).astype(jnp.bfloat16))
        level = row_max * score_scale + jnp.log(total)
        for piece in range(row_tile // width):
            line = jnp.where(picks, level[piece * width : (piece + 1) * width], 0.0)
            row = tile * (row_tile // width) + piece
            level_ref[row : row + 1, :] = jnp.sum(line, axis=0, keepdims=True)
        row_max = next_max
    levels = level_ref[...]
    high = levels.astype(jnp.bfloat16).astype(jnp.float32)
    middle = (levels - high).astype(jnp.bfloat16).astype(jnp.float32)
    low = levels - high - middle
    stats = jnp.concatenate([high, middle, low, jnp.zeros_like(levels)], 0)
    put(row_count, stats.astype(jnp.bfloat16))


def putter(out_ref):
    def put(start, rows):
        out_ref[start : start + rows.shape[0], :] = rows

    return put


def hand_out(stage_ref, out_refs):
    for far, out_ref in enumerate(out_refs):

        @pl.when(pl.program_id(0) == far)
        def _():
            out_ref[...] = stage_ref[...]


def tile_reader(query_ref):
    return lambda tile: query_ref[0, tile * row_tile : (tile + 1) * row_tile, :]


def task_scratch(row_count, width, key_count):
    return [
        pltpu.VMEM((row_count // width, width), jnp.float32),
        pltpu.VMEM((2, row_tile, key_count), jnp.float32),
    ]


def task_cost(task_count, row_count, key_count, width):
    return pl.CostEstimate(
        flops=4 * task_count * row_count * key_count * width,
        bytes_accessed=4 * task_count * (row_count + key_count) * width,
        transcendentals=task_count * row_count * key_count,
    )


def first_kernel(source_count, task_count, part_rows, score_scale, place_ref, query_ref, *refs):
    source_refs = refs[:source_count]
    out_refs = refs[-4 - task_count : -4]
    mark_ref, level_ref, score_ref, stage_ref = refs[-4:]
    _, row_count, width = query_ref.shape
    mark_ref[...] = jnp.zeros_like(mark_ref)
    parts = [
        (
            functools.partial(lambda ref: ref[0:part_rows, :], ref),
            functools.partial(lambda ref: ref[part_rows : 2 * part_rows, :], ref),
        )
        for ref in source_refs
    ]
    attend_task(
        tile_reader(query_ref),
        putter(stage_ref),
        row_count,
        width,
        parts,
        None,
        level_ref,
        score_ref,
        score_scale,
    )
    hand_out(stage_ref, out_refs)


def attend_first(queries, sources, place, task_of, slot_of, task_count, part_rows, score_scale, before):
    _, _, row_count, width = queries.shape
    out_rows = row_count + stat_rows
    span_rows = 2 * part_rows
    source_spec = pl.BlockSpec(
        (span_rows, width), lambda step, place: (slot_of(task_of(step), place), 0)
    )
    outs = pl.pallas_call(
        functools.partial(first_kernel, len(sources), task_count, part_rows, score_scale),
        grid_spec=pltpu.PrefetchScalarGridSpec(
            num_scalar_prefetch=1,
            grid=(task_count,),
            in_specs=[
                pl.BlockSpec(
                    (1, None, row_count, width),
                    lambda step, place: (lax.bitwise_xor(place[2], task_of(step)), 0, 0, 0),
                )
            ]
            + [source_spec] * len(sources)
            + [pl.BlockSpec(memory_space=pl.ANY)] * len(before),
            out_specs=[pl.BlockSpec((out_rows, width), lambda step, place: (0, 0))] * task_count
            + [pl.BlockSpec((8, width), lambda step, place: (0, 0))],
            scratch_shapes=task_scratch(row_count, width, len(sources) * part_rows)
            + [pltpu.VMEM((out_rows, width), jnp.bfloat16)],
        ),
        out_shape=[jax.ShapeDtypeStruct((out_rows, width), jnp.bfloat16)] * task_count
        + [jax.ShapeDtypeStruct((8, width), jnp.float32)],
        compiler_params=pltpu.CompilerParams(vmem_limit_bytes=vmem_bytes),
        cost_estimate=task_cost(task_count, row_count, len(sources) * part_rows, width),
        name="attend_first",
    )(place, queries, *sources, *before)
    return outs[:-1], (outs[-1],)


def second_kernel(
    head_count, far_chunks, task_of, task_count, part_rows, score_scale, parent_ref, place_ref, query_ref, *refs
):
    further_refs = refs[:head_count]
    nearer_refs = refs[head_count : 2 * head_count]
    far_refs = refs[2 * head_count : (2 + far_chunks) * head_count]
    out_refs = refs[-8 - task_count : -8]
    mark_ref, level_ref, score_ref, stage_ref, held, fresh = refs[-8:-2]
    semaphores, fresh_semaphores = refs[-2:]
    _, row_count, width = query_ref.shape
    span_rows = 2 * part_rows
    token_count = fresh.shape[1] // 2
    half = head_count // 2
    step = pl.program_id(0)
    node = place_ref[2]
    mark_ref[...] = jnp.zeros_like(mark_ref)

    def parent_at(number):
        return parent_ref[lax.bitwise_xor(node, task_of(number))]

    def fetch(number):
        parent = parent_at(number)
        apart = lax.bitwise_xor(parent, node)

        def bring(chosen, source_refs, slot):
            @pl.when(chosen)
            def _():
                rows = pl.ds(pl.multiple_of(slot * span_rows, span_rows), span_rows)
                for source in range(head_count):
                    pltpu.make_async_copy(
                        source_refs[source].at[rows],
                        held.at[number % 2, source],
                        semaphores.at[number % 2, source],
                    ).start()

        bring(apart < half, nearer_refs, apart)
        bring(jnp.logical_and(apart >= half, apart < head_count), further_refs, apart - half)
        for chunk in range(far_chunks):
            bring(
                apart // head_count == chunk + 1,
                far_refs[chunk * head_count : (chunk + 1) * head_count],
                parent % head_count,
            )

    @pl.when(step == 0)
    def _():
        fetch(0)
        fresh_copies = [
            pltpu.make_async_copy(
                further_refs[source].at[pl.ds(half * span_rows, 2 * token_count)],
                fresh.at[source],
                fresh_semaphores.at[source],
            )
            for source in range(head_count)
        ]
        for copy in fresh_copies:
            copy.start()
        for copy in fresh_copies:
            copy.wait()

    @pl.when(step + 1 < task_count)
    def _():
        fetch(step + 1)

    slot = step % 2
    for source in range(head_count):
        pltpu.make_async_copy(
            further_refs[source].at[pl.ds(0, span_rows)],
            held.at[slot, source],
            semaphores.at[slot, source],
        ).wait()
    apart = lax.bitwise_xor(parent_at(step), node)
    place = jnp.where(apart < head_count, apart, 0)
    parts = [
        (
            functools.partial(lambda source: held[slot, source, 0:part_rows, :], source),
            functools.partial(lambda source: held[slot, source, part_rows:span_rows, :], source),
        )
        for source in range(head_count)
    ]
    parts.append(
        (
            lambda: fresh[place, 0:token_count, :],
            lambda: fresh[place, token_count : 2 * token_count, :],
        )
    )

    def mask_of(tile):
        return jnp.broadcast_to(apart < head_count, (row_tile, token_count))

    attend_task(
        tile_reader(query_ref),
        putter(stage_ref),
        row_count,
        width,
        parts,
        mask_of,
        level_ref,
        score_ref,
        score_scale,
    )
    hand_out(stage_ref, out_refs)


def attend_second(
    queries, further, nearer, far, parents, place, task_of, task_count, part_rows, score_scale, before
):
    _, _, row_count, width = queries.shape
    head_count = len(further)
    span_rows = 2 * part_rows
    fresh_rows = further[0].shape[0] - head_count // 2 * span_rows
    keys = head_count * part_rows + fresh_rows // 2
    out_rows = row_count + stat_rows
    operands = [row for rows in (further, nearer, *far) for row in rows] + [*before]
    outs = pl.pallas_call(
        functools.partial(
            second_kernel, head_count, len(far), task_of, task_count, part_rows, score_scale
        ),
        grid_spec=pltpu.PrefetchScalarGridSpec(
            num_scalar_prefetch=2,
            grid=(task_count,),
            in_specs=[
                pl.BlockSpec(
                    (1, None, row_count, width),
                    lambda step, parent, place: (lax.bitwise_xor(place[2], task_of(step)), 1, 0, 0),
                )
            ]
            + [pl.BlockSpec(memory_space=pl.ANY)] * len(operands),
            out_specs=[pl.BlockSpec((out_rows, width), lambda step, parent, place: (0, 0))]
            * task_count
            + [pl.BlockSpec((8, width), lambda step, parent, place: (0, 0))],
            scratch_shapes=task_scratch(row_count, width, keys)
            + [
                pltpu.VMEM((out_rows, width), jnp.bfloat16),
                pltpu.VMEM((2, head_count, span_rows, width), jnp.bfloat16),
                pltpu.VMEM((head_count, fresh_rows, width), jnp.bfloat16),
                pltpu.SemaphoreType.DMA((2, head_count)),
                pltpu.SemaphoreType.DMA((head_count,)),
            ],
        ),
        out_shape=[jax.ShapeDtypeStruct((out_rows, width), jnp.bfloat16)] * task_count
        + [jax.ShapeDtypeStruct((8, width), jnp.float32)],
        compiler_params=pltpu.CompilerParams(vmem_limit_bytes=vmem_bytes),
        cost_estimate=task_cost(task_count, row_count, keys, width),
        name="attend_second",
    )(parents, place, queries, *operands)
    return outs[:-1], (outs[-1],)


def own_kernel(
    group_size, score_scale, place_ref, query_ref, key_ref, value_ref, out_ref, level_ref, score_ref
):
    token_count = key_ref.shape[1]
    _, row_count, width = query_ref.shape

    def mask_of(tile):
        row = tile * row_tile + lax.broadcasted_iota(jnp.int32, (row_tile, token_count), 0)
        column = lax.broadcasted_iota(jnp.int32, (row_tile, token_count), 1)
        return column * group_size <= row

    attend_task(
        tile_reader(query_ref),
        putter(out_ref.at[0]),
        row_count,
        width,
        [(lambda: key_ref[0], lambda: value_ref[0])],
        mask_of,
        level_ref,
        score_ref,
        score_scale,
    )


def attend_own(queries, depth, keys, values, place, score_scale):
    head_count, token_count, width = keys.shape
    row_count = queries.shape[2]

    def head_spec(rows):
        return pl.BlockSpec(
            (1, rows, width), lambda step, place: (lax.bitwise_xor(place[0], step), 0, 0)
        )

    return pl.pallas_call(
        functools.partial(own_kernel, row_count // token_count, score_scale),
        grid_spec=pltpu.PrefetchScalarGridSpec(
            num_scalar_prefetch=1,
            grid=(head_count,),
            in_specs=[
                pl.BlockSpec(
                    (1, None, row_count, width),
                    lambda step, place: (lax.bitwise_xor(place[0], step), depth, 0, 0),
                ),
                head_spec(token_count),
                head_spec(token_count),
            ],
            out_specs=pl.BlockSpec(
                (1, row_count + stat_rows, width), lambda step, place: (step, 0, 0)
            ),
            scratch_shapes=task_scratch(row_count, width, token_count),
        ),
        out_shape=jax.ShapeDtypeStruct((head_count, row_count + stat_rows, width), jnp.bfloat16),
        compiler_params=pltpu.CompilerParams(vmem_limit_bytes=vmem_bytes),
        cost_estimate=task_cost(head_count, row_count, token_count, width),
        name="attend_own",
    )(place, queries, keys, values)


def merge_kernel(head_count, group_size, part_count, place_ref, *refs):
    part_refs, own_ref = refs[:part_count], refs[part_count]
    refs = refs[part_count + 1 :]
    stat_refs, own_stat_ref = refs[:part_count], refs[part_count]
    out_ref, mixed_ref = refs[-2:]
    token_tile, _, lanes = out_ref.shape[1:]
    stat_tile = token_tile * group_size // lanes
    step = pl.program_id(0)
    picks = eye(lanes)
    ones = jnp.ones((2 * lanes, lanes), jnp.bfloat16)
    span = stat_rows // 4

    for far in range(head_count):
        head = lax.bitwise_xor(place_ref[0], far)
        sources = [part_refs[place] for place in range(far, part_count, head_count)]
        sources.append(own_ref.at[far])
        stats = [stat_refs[place][...] for place in range(far, part_count, head_count)]
        stats.append(own_stat_ref[far])
        stats = [stat.astype(jnp.float32) for stat in stats]
        level = [
            stat[:span] + stat[span : 2 * span] + stat[2 * span : 3 * span] for stat in stats
        ]
        top = functools.reduce(jnp.maximum, level)
        shares = [jnp.exp(one - top) for one in level]
        total = functools.reduce(jnp.add, shares)
        shares = [one / total for one in shares]
        lines = []
        for share in shares:
            for piece in range(stat_tile):
                chosen = (
                    lax.broadcasted_iota(jnp.int32, share.shape, 0) == step * stat_tile + piece
                )
                lines.append(jnp.sum(jnp.where(chosen, share, 0.0), axis=0, keepdims=True))
        scales = []
        for line in lines:
            high = line.astype(jnp.bfloat16).astype(jnp.float32)
            scales.append(
                jnp.concatenate(
                    [
                        jnp.where(picks, portion, 0.0).astype(jnp.bfloat16)
                        for portion in (high, line - high)
                    ],
                    1,
                )
            )
        columns = jnp.dot(
            jnp.concatenate(scales, 0), ones, preferred_element_type=jnp.float32
        )
        mixed = None
        rows = stat_tile * lanes
        for place, source in enumerate(sources):
            block = source[...].astype(jnp.float32) * columns[place * rows : (place + 1) * rows]
            mixed = block if mixed is None else mixed + block
        mixed_ref[
            :, pl.ds(pl.multiple_of(head * group_size, group_size), group_size), :
        ] = mixed.reshape(token_tile, group_size, lanes)
    out_ref[0] = mixed_ref[...].astype(out_ref.dtype)


def merge(parts, own, place, token_count, before=()):
    head_count, out_rows, width = own.shape
    row_count = out_rows - stat_rows
    group_size = row_count // token_count
    token_tile = 64
    rows = token_tile * group_size
    stat_block = row_count // stat_rows
    query_heads = head_count * group_size

    def specs(size, index):
        flat = pl.BlockSpec((size, width), lambda step, place: (index(step), 0))
        whole = pl.BlockSpec((head_count, size, width), lambda step, place: (0, index(step), 0))
        return [flat] * len(parts) + [whole]

    return pl.pallas_call(
        functools.partial(merge_kernel, head_count, group_size, len(parts)),
        grid_spec=pltpu.PrefetchScalarGridSpec(
            num_scalar_prefetch=1,
            grid=(token_count // token_tile,),
            in_specs=specs(rows, lambda step: step)
            + specs(stat_rows, lambda step: stat_block)
            + [pl.BlockSpec(memory_space=pl.ANY)] * len(before),
            out_specs=pl.BlockSpec(
                (1, token_tile, query_heads, width), lambda step, place: (0, step, 0, 0)
            ),
            scratch_shapes=[pltpu.VMEM((token_tile, query_heads, width), jnp.float32)],
        ),
        out_shape=jax.ShapeDtypeStruct((1, token_count, query_heads, width), jnp.bfloat16),
        compiler_params=pltpu.CompilerParams(vmem_limit_bytes=vmem_bytes),
        cost_estimate=pl.CostEstimate(
            flops=4 * (len(parts) + head_count) * row_count * width,
            bytes_accessed=4 * (len(parts) + head_count) * row_count * width,
            transcendentals=0,
        ),
        name="merge_parts",
    )(place, *parts, own, *parts, own, *before)


def local(
    queries_one,
    keys_one,
    values_one,
    queries_two,
    keys_two,
    values_two,
    cache_keys,
    cache_values,
    paths,
    parents,
    positions,
):
    here_index = lax.axis_index("node")
    peer_count = lax.axis_size("node")
    block_count, token_count, head_count, width = cache_keys.shape
    per_peer = paths.shape[1] // peer_count
    copies = peer_count // head_count
    score_scale = width ** (-0.5)
    my_head = here_index % head_count
    my_group = here_index // head_count
    part_rows = per_peer * token_count
    places = [
        jnp.stack([my_head, lax.bitwise_xor(my_group, apart), here_index])
        for apart in range(copies)
    ]

    def swap(array, apart):
        return lax.ppermute(array, "node", [(node, node ^ apart) for node in range(peer_count)])

    cosine, sine_part = rotary_tables(positions[:, 0], width)
    send = turn_queries(queries_one, queries_two, cosine, sine_part, head_count, copies)
    got = lax.all_to_all(send, "node", split_axis=0, concat_axis=0, tiled=True)
    key_rot_one = rotary(keys_one[0], cosine[0], sine_part[0])
    key_rot_two = rotary(keys_two[0], cosine[1], sine_part[1])

    block_index = local_blocks(paths, here_index, block_count, per_peer).reshape(-1)
    chunks = []
    before = (send,)
    for apart in range(1, copies):
        packed = pack(
            cache_keys, cache_values, block_index, places[apart], (), per_peer, before
        )
        chunks.append([packed[0]] + [swap(packed[far], far) for far in range(1, head_count)])
        before = (packed[0],)
    packed = pack(
        cache_keys,
        cache_values,
        block_index,
        places[0],
        (key_rot_one, values_one[0]),
        per_peer,
        before,
    )
    further = [packed[0]] + [swap(packed[far], far) for far in range(1, head_count)]
    nearer = [packed[head_count]] + [
        swap(packed[head_count + far], far) for far in range(1, head_count)
    ]

    own_one = attend_own(
        send,
        0,
        jnp.moveaxis(key_rot_one, 1, 0),
        jnp.moveaxis(values_one[0], 1, 0),
        places[0],
        score_scale,
    )
    own_two = attend_own(
        send,
        1,
        jnp.moveaxis(key_rot_two, 1, 0),
        jnp.moveaxis(values_two[0], 1, 0),
        places[0],
        score_scale,
    )

    half = head_count // 2
    parts_one, parts_two = [None] * peer_count, [None] * peer_count

    def send_home(parts, tasks, rows):
        for task, row in zip(tasks, rows):
            parts[task] = swap(row, task) if task else row

    def first(sources, tasks, task_of, slot_of, before):
        rows, before = attend_first(
            got,
            sources,
            places[0],
            task_of,
            slot_of,
            len(tasks),
            part_rows,
            score_scale,
            before,
        )
        send_home(parts_one, tasks, rows)
        return before

    def second(tasks, task_of, before):
        rows, before = attend_second(
            got,
            further,
            nearer,
            chunks,
            parents,
            places[0],
            task_of,
            len(tasks),
            part_rows,
            score_scale,
            before,
        )
        send_home(parts_two, tasks, rows)
        return before

    def far_slot(task, place):
        return lax.bitwise_xor(task % head_count, place[0])

    before = (own_one, own_two)
    for apart in range(1, copies):
        base = apart * head_count
        before = first(chunks[apart - 1], [base], lambda step: base, far_slot, before)
        before = first(
            chunks[apart - 1],
            list(range(base + 1, base + head_count)),
            lambda step: base + 1 + step,
            far_slot,
            before,
        )
    before = first(
        further,
        list(range(half, head_count)),
        lambda step: half + step,
        lambda task, place: task - half,
        before,
    )
    for apart in range(1, copies):
        base = apart * head_count
        before = second([base], lambda step: base, before)
        before = (*before, *parts_one[base : base + 2])
        before = second(
            list(range(base + 1, base + head_count)), lambda step: base + 1 + step, before
        )
        before = (*before, *parts_one[base + 2 : base + head_count])
    before = first(
        nearer,
        list(range(1, half)) + [0],
        lambda step: (step + 1) % half,
        lambda task, place: task,
        (*before, *parts_one[half:head_count]),
    )
    before = second(
        list(range(1, head_count)),
        lambda step: step + 1,
        before,
    )
    before = second([0], lambda step: 0, before)
    before = (*before, *parts_two[head_count : head_count + 3])
    return (
        merge(parts_one, own_one, places[0], token_count, before),
        merge(parts_two, own_two, places[0], token_count),
    )


def solution(mesh):
    in_specs = (
        P(("group", "node"), None, "head", None),
        P(("group", "node"), None, "head", None),
        P(("group", "node"), None, "head", None),
        P(("group", "node"), None, "head", None),
        P(("group", "node"), None, "head", None),
        P(("group", "node"), None, "head", None),
        P(("group", "node"), None, "head", None),
        P(("group", "node"), None, "head", None),
        P("group", None),
        P("group"),
        P(None, ("group", "node"), None),
    )
    out_specs = (P(("group", "node"), None, "head", None), P(("group", "node"), None, "head", None))
    return jax.shard_map(
        local,
        mesh=mesh,
        in_specs=in_specs,
        out_specs=out_specs,
        check_vma=False,
    )
```

```python
import functools

import jax
import jax.numpy as jnp
from jax import lax
from jax.experimental import pallas as pl
from jax.experimental.pallas import tpu as pltpu
from jax.sharding import PartitionSpec as P

rope_theta = 500000.0
log2_e = 1.4426950408889634
stat_rows = 32
row_tile = 256
vmem_bytes = 56 * 1024 * 1024


def rotary_tables(positions, head_width):
    half_width = head_width // 2
    place = jnp.arange(head_width, dtype=jnp.int32)
    pair = (place % half_width).astype(jnp.float32)
    frequency = rope_theta ** (-(pair * 2.0) / head_width)
    angles = positions.astype(jnp.float32)[..., None] * frequency
    return jnp.cos(angles), jnp.where(place < half_width, -1.0, 1.0) * jnp.sin(angles)


def rotary(vector, cosine, signed_sine):
    widened = vector.astype(jnp.float32)
    swapped = jnp.roll(widened, widened.shape[-1] // 2, axis=-1)
    turned = widened * cosine[:, None, :] + swapped * signed_sine[:, None, :]
    return turned.astype(jnp.bfloat16)


def turn_kernel(head_count, copies, first_ref, second_ref, cosine_ref, sine_ref, out_ref):
    token_tile, query_heads, width = first_ref.shape[1:]
    group_size = query_heads // head_count
    rows = token_tile * group_size
    for depth, query_ref in enumerate((first_ref, second_ref)):
        widened = query_ref[0].astype(jnp.float32)
        swapped = pltpu.roll(widened.reshape(token_tile * query_heads, width), width // 2, 1)
        swapped = swapped.reshape(token_tile, query_heads, width)
        turned = widened * cosine_ref[depth][:, None, :] + swapped * sine_ref[depth][:, None, :]
        for head in range(head_count):
            turned_head = turned[:, head * group_size : (head + 1) * group_size, :]
            turned_head = turned_head.reshape(rows, width).astype(jnp.bfloat16)
            for copy in range(copies):
                out_ref[copy * head_count + head, depth] = turned_head


def turn_queries(queries_one, queries_two, cosine, sine_part, head_count, copies):
    _, token_count, query_heads, width = queries_one.shape
    token_tile = 64
    rows = token_tile * query_heads // head_count
    query_spec = pl.BlockSpec((1, token_tile, query_heads, width), lambda step: (0, step, 0, 0))
    table_spec = pl.BlockSpec((2, token_tile, width), lambda step: (0, step, 0))
    return pl.pallas_call(
        functools.partial(turn_kernel, head_count, copies),
        grid=(token_count // token_tile,),
        in_specs=[query_spec, query_spec, table_spec, table_spec],
        out_specs=pl.BlockSpec(
            (head_count * copies, 2, rows, width), lambda step: (0, 0, step, 0)
        ),
        out_shape=jax.ShapeDtypeStruct(
            (head_count * copies, 2, token_count * query_heads // head_count, width), jnp.bfloat16
        ),
        compiler_params=pltpu.CompilerParams(vmem_limit_bytes=vmem_bytes),
        cost_estimate=pl.CostEstimate(
            flops=8 * queries_one.size, bytes_accessed=12 * queries_one.size, transcendentals=0
        ),
        name="turn_queries",
    )(queries_one, queries_two, cosine, sine_part)


def local_blocks(paths, here_index, per_owner, per_peer):
    is_local = paths // per_owner == here_index
    slot_rank = jnp.cumsum(is_local.astype(jnp.int32), axis=1) - 1
    slot_range = jnp.arange(per_peer, dtype=jnp.int32)
    selected = jnp.logical_and(
        is_local[:, :, None], slot_rank[:, :, None] == slot_range[None, None, :]
    )
    return jnp.sum(jnp.where(selected, (paths % per_owner)[:, :, None], 0), axis=1)


def pack_kernel(per_peer, head_count, token_count, near, index_ref, place_ref, *refs):
    key_refs = refs[:per_peer]
    value_refs = refs[per_peer : 2 * per_peer]
    new_refs = refs[2 * per_peer : 2 * per_peer + 2] if near else ()
    out_refs, wide = refs[-1 - head_count * (2 if near else 1) : -1], refs[-1]
    step = pl.program_id(0)
    mine = place_ref[0]
    span_rows = 2 * per_peer * token_count
    half = head_count // 2

    def spread(rows, put):
        wide[...] = rows.astype(jnp.float32)
        for far in range(head_count):
            head = lax.bitwise_xor(mine, far)
            picked = wide[pl.ds(head, token_count, stride=head_count), :]
            put(far, head, picked.astype(jnp.bfloat16))

    for which, source_refs in enumerate((key_refs, value_refs)):
        for slot, source in enumerate(source_refs):
            offset = (which * per_peer + slot) * token_count

            def put(far, head, rows):
                if not near:
                    start = pl.multiple_of(step * span_rows + offset, token_count)
                    out_refs[far][pl.ds(start, token_count), :] = rows
                    return
                apart = lax.bitwise_xor(step, head)
                start = pl.multiple_of((apart % half) * span_rows + offset, token_count)

                @pl.when(apart >= half)
                def _():
                    out_refs[far][pl.ds(start, token_count), :] = rows

                @pl.when(apart < half)
                def _():
                    out_refs[head_count + far][pl.ds(start, token_count), :] = rows

            spread(source[0], put)
    if near:

        @pl.when(step == 0)
        def _():
            for which, source in enumerate(new_refs):
                start = half * span_rows + which * token_count

                def put(far, head, rows):
                    out_refs[far][start : start + token_count, :] = rows

                spread(source[...], put)


def pack(cache_keys, cache_values, block_index, place, new_rows, per_peer, before=()):
    block_count, token_count, head_count, width = cache_keys.shape
    flat_keys = cache_keys.reshape(block_count, token_count * head_count, width)
    flat_values = cache_values.reshape(block_count, token_count * head_count, width)
    span_rows = 2 * per_peer * token_count
    near = bool(new_rows)
    half_rows = head_count // 2 * span_rows
    out_rows = half_rows + 2 * token_count if near else head_count * span_rows
    shapes = [(out_rows, width)] * head_count
    if near:
        shapes += [(half_rows, width)] * head_count

    def block_spec(slot):
        return pl.BlockSpec(
            (1, token_count * head_count, width),
            lambda step, index, place: (
                index[(place[1] * head_count + step) * per_peer + slot],
                0,
                0,
            ),
        )

    def whole_spec(shape):
        return pl.BlockSpec(shape, lambda step, index, place: (0,) * len(shape))

    cache_specs = [block_spec(slot) for slot in range(per_peer)]
    new_spec = pl.BlockSpec((token_count * head_count, width), lambda step, index, place: (0, 0))
    operands = [flat_keys] * per_peer + [flat_values] * per_peer
    operands += [row.reshape(token_count * head_count, width) for row in new_rows]
    return pl.pallas_call(
        functools.partial(pack_kernel, per_peer, head_count, token_count, near),
        grid_spec=pltpu.PrefetchScalarGridSpec(
            num_scalar_prefetch=2,
            grid=(head_count,),
            in_specs=cache_specs
            + cache_specs
            + [new_spec] * len(new_rows)
            + [pl.BlockSpec(memory_space=pl.ANY)] * len(before),
            out_specs=[whole_spec(shape) for shape in shapes],
            scratch_shapes=[pltpu.VMEM((token_count * head_count, width), jnp.float32)],
        ),
        out_shape=[jax.ShapeDtypeStruct(shape, jnp.bfloat16) for shape in shapes],
        compiler_params=pltpu.CompilerParams(vmem_limit_bytes=vmem_bytes),
        cost_estimate=pl.CostEstimate(
            flops=0, bytes_accessed=4 * head_count * out_rows * width, transcendentals=0
        ),
        name="pack_rows",
    )(block_index, place, *operands, *before)


def eye(size):
    return lax.broadcasted_iota(jnp.int32, (size, size), 0) == lax.broadcasted_iota(
        jnp.int32, (size, size), 1
    )


def product(left, right):
    return lax.dot_general(
        left, right, (((1,), (1,)), ((), ())), preferred_element_type=jnp.float32
    )


def fold_lanes(array, width, operation):
    pieces = [array[:, start : start + width] for start in range(0, array.shape[1], width)]
    while len(pieces) > 1:
        pieces = [
            operation(*pieces[start : start + 2]) if start + 1 < len(pieces) else pieces[start]
            for start in range(0, len(pieces), 2)
        ]
    return pieces[0]


def attend_task(query_of, put, row_count, width, parts, mask_of, level_ref, score_ref, score_scale):
    tile_count = row_count // row_tile

    def make_scores(tile):
        query = query_of(tile)
        top, start = None, 0
        for place, (keys, _) in enumerate(parts):
            scores = product(query, keys())
            if mask_of is not None and place == len(parts) - 1:
                scores = jnp.where(mask_of(tile), scores, -1e30)
            size = scores.shape[1]
            score_ref[tile % 2, :, start : start + size] = scores
            start += size
            folded = fold_lanes(scores, width, jnp.maximum)
            top = folded if top is None else jnp.maximum(top, folded)
        return jnp.max(top, axis=-1, keepdims=True)

    picks = eye(width)
    row_max = make_scores(0)
    for tile in range(tile_count):
        next_max = make_scores(tile + 1) if tile + 1 < tile_count else None
        total, mixture, start = None, None, 0
        for _, values in parts:
            value_rows = values()
            size = value_rows.shape[0]
            scores = score_ref[tile % 2, :, start : start + size]
            start += size
            weights = jnp.exp2((scores - row_max) * (score_scale * log2_e))
            folded = fold_lanes(weights, width, jnp.add)
            total = folded if total is None else total + folded
            mixed = jnp.dot(
                weights.astype(jnp.bfloat16), value_rows, preferred_element_type=jnp.float32
            )
            mixture = mixed if mixture is None else mixture + mixed
        total = jnp.sum(total, axis=-1, keepdims=True)
        put(tile * row_tile, (mixture / total).astype(jnp.bfloat16))
        level = row_max * score_scale + jnp.log(total)
        for piece in range(row_tile // width):
            line = jnp.where(picks, level[piece * width : (piece + 1) * width], 0.0)
            row = tile * (row_tile // width) + piece
            level_ref[row : row + 1, :] = jnp.sum(line, axis=0, keepdims=True)
        row_max = next_max
    levels = level_ref[...]
    high = levels.astype(jnp.bfloat16).astype(jnp.float32)
    middle = (levels - high).astype(jnp.bfloat16).astype(jnp.float32)
    low = levels - high - middle
    stats = jnp.concatenate([high, middle, low, jnp.zeros_like(levels)], 0)
    put(row_count, stats.astype(jnp.bfloat16))


def putter(out_ref):
    def put(start, rows):
        out_ref[start : start + rows.shape[0], :] = rows

    return put


def hand_out(stage_ref, out_refs):
    for far, out_ref in enumerate(out_refs):

        @pl.when(pl.program_id(0) == far)
        def _():
            out_ref[...] = stage_ref[...]


def tile_reader(query_ref):
    return lambda tile: query_ref[0, tile * row_tile : (tile + 1) * row_tile, :]


def task_scratch(row_count, width, key_count):
    return [
        pltpu.VMEM((row_count // width, width), jnp.float32),
        pltpu.VMEM((2, row_tile, key_count), jnp.float32),
    ]


def task_cost(task_count, row_count, key_count, width):
    return pl.CostEstimate(
        flops=4 * task_count * row_count * key_count * width,
        bytes_accessed=4 * task_count * (row_count + key_count) * width,
        transcendentals=task_count * row_count * key_count,
    )


def first_kernel(source_count, task_count, part_rows, score_scale, place_ref, query_ref, *refs):
    source_refs = refs[:source_count]
    out_refs = refs[-4 - task_count : -4]
    mark_ref, level_ref, score_ref, stage_ref = refs[-4:]
    _, row_count, width = query_ref.shape
    mark_ref[...] = jnp.zeros_like(mark_ref)
    parts = [
        (
            functools.partial(lambda ref: ref[0:part_rows, :], ref),
            functools.partial(lambda ref: ref[part_rows : 2 * part_rows, :], ref),
        )
        for ref in source_refs
    ]
    attend_task(
        tile_reader(query_ref),
        putter(stage_ref),
        row_count,
        width,
        parts,
        None,
        level_ref,
        score_ref,
        score_scale,
    )
    hand_out(stage_ref, out_refs)


def attend_first(queries, sources, place, task_of, slot_of, task_count, part_rows, score_scale, before):
    _, _, row_count, width = queries.shape
    out_rows = row_count + stat_rows
    span_rows = 2 * part_rows
    source_spec = pl.BlockSpec(
        (span_rows, width), lambda step, place: (slot_of(task_of(step), place), 0)
    )
    outs = pl.pallas_call(
        functools.partial(first_kernel, len(sources), task_count, part_rows, score_scale),
        grid_spec=pltpu.PrefetchScalarGridSpec(
            num_scalar_prefetch=1,
            grid=(task_count,),
            in_specs=[
                pl.BlockSpec(
                    (1, None, row_count, width),
                    lambda step, place: (lax.bitwise_xor(place[2], task_of(step)), 0, 0, 0),
                )
            ]
            + [source_spec] * len(sources)
            + [pl.BlockSpec(memory_space=pl.ANY)] * len(before),
            out_specs=[pl.BlockSpec((out_rows, width), lambda step, place: (0, 0))] * task_count
            + [pl.BlockSpec((8, width), lambda step, place: (0, 0))],
            scratch_shapes=task_scratch(row_count, width, len(sources) * part_rows)
            + [pltpu.VMEM((out_rows, width), jnp.bfloat16)],
        ),
        out_shape=[jax.ShapeDtypeStruct((out_rows, width), jnp.bfloat16)] * task_count
        + [jax.ShapeDtypeStruct((8, width), jnp.float32)],
        compiler_params=pltpu.CompilerParams(vmem_limit_bytes=vmem_bytes),
        cost_estimate=task_cost(task_count, row_count, len(sources) * part_rows, width),
        name="attend_first",
    )(place, queries, *sources, *before)
    return outs[:-1], (outs[-1],)


def second_kernel(
    head_count, far_chunks, task_of, task_count, part_rows, score_scale, parent_ref, place_ref, query_ref, *refs
):
    further_refs = refs[:head_count]
    nearer_refs = refs[head_count : 2 * head_count]
    far_refs = refs[2 * head_count : (2 + far_chunks) * head_count]
    out_refs = refs[-8 - task_count : -8]
    mark_ref, level_ref, score_ref, stage_ref, held, fresh = refs[-8:-2]
    semaphores, fresh_semaphores = refs[-2:]
    _, row_count, width = query_ref.shape
    span_rows = 2 * part_rows
    token_count = fresh.shape[1] // 2
    half = head_count // 2
    step = pl.program_id(0)
    node = place_ref[2]
    mark_ref[...] = jnp.zeros_like(mark_ref)

    def parent_at(number):
        return parent_ref[lax.bitwise_xor(node, task_of(number))]

    def fetch(number):
        parent = parent_at(number)
        apart = lax.bitwise_xor(parent, node)

        def bring(chosen, source_refs, slot):
            @pl.when(chosen)
            def _():
                rows = pl.ds(pl.multiple_of(slot * span_rows, span_rows), span_rows)
                for source in range(head_count):
                    pltpu.make_async_copy(
                        source_refs[source].at[rows],
                        held.at[number % 2, source],
                        semaphores.at[number % 2, source],
                    ).start()

        bring(apart < half, nearer_refs, apart)
        bring(jnp.logical_and(apart >= half, apart < head_count), further_refs, apart - half)
        for chunk in range(far_chunks):
            bring(
                apart // head_count == chunk + 1,
                far_refs[chunk * head_count : (chunk + 1) * head_count],
                parent % head_count,
            )

    @pl.when(step == 0)
    def _():
        fetch(0)
        fresh_copies = [
            pltpu.make_async_copy(
                further_refs[source].at[pl.ds(half * span_rows, 2 * token_count)],
                fresh.at[source],
                fresh_semaphores.at[source],
            )
            for source in range(head_count)
        ]
        for copy in fresh_copies:
            copy.start()
        for copy in fresh_copies:
            copy.wait()

    @pl.when(step + 1 < task_count)
    def _():
        fetch(step + 1)

    slot = step % 2
    for source in range(head_count):
        pltpu.make_async_copy(
            further_refs[source].at[pl.ds(0, span_rows)],
            held.at[slot, source],
            semaphores.at[slot, source],
        ).wait()
    apart = lax.bitwise_xor(parent_at(step), node)
    place = jnp.where(apart < head_count, apart, 0)
    parts = [
        (
            functools.partial(lambda source: held[slot, source, 0:part_rows, :], source),
            functools.partial(lambda source: held[slot, source, part_rows:span_rows, :], source),
        )
        for source in range(head_count)
    ]
    parts.append(
        (
            lambda: fresh[place, 0:token_count, :],
            lambda: fresh[place, token_count : 2 * token_count, :],
        )
    )

    def mask_of(tile):
        return jnp.broadcast_to(apart < head_count, (row_tile, token_count))

    attend_task(
        tile_reader(query_ref),
        putter(stage_ref),
        row_count,
        width,
        parts,
        mask_of,
        level_ref,
        score_ref,
        score_scale,
    )
    hand_out(stage_ref, out_refs)


def attend_second(
    queries, further, nearer, far, parents, place, task_of, task_count, part_rows, score_scale, before
):
    _, _, row_count, width = queries.shape
    head_count = len(further)
    span_rows = 2 * part_rows
    fresh_rows = further[0].shape[0] - head_count // 2 * span_rows
    keys = head_count * part_rows + fresh_rows // 2
    out_rows = row_count + stat_rows
    operands = [row for rows in (further, nearer, *far) for row in rows] + [*before]
    outs = pl.pallas_call(
        functools.partial(
            second_kernel, head_count, len(far), task_of, task_count, part_rows, score_scale
        ),
        grid_spec=pltpu.PrefetchScalarGridSpec(
            num_scalar_prefetch=2,
            grid=(task_count,),
            in_specs=[
                pl.BlockSpec(
                    (1, None, row_count, width),
                    lambda step, parent, place: (lax.bitwise_xor(place[2], task_of(step)), 1, 0, 0),
                )
            ]
            + [pl.BlockSpec(memory_space=pl.ANY)] * len(operands),
            out_specs=[pl.BlockSpec((out_rows, width), lambda step, parent, place: (0, 0))]
            * task_count
            + [pl.BlockSpec((8, width), lambda step, parent, place: (0, 0))],
            scratch_shapes=task_scratch(row_count, width, keys)
            + [
                pltpu.VMEM((out_rows, width), jnp.bfloat16),
                pltpu.VMEM((2, head_count, span_rows, width), jnp.bfloat16),
                pltpu.VMEM((head_count, fresh_rows, width), jnp.bfloat16),
                pltpu.SemaphoreType.DMA((2, head_count)),
                pltpu.SemaphoreType.DMA((head_count,)),
            ],
        ),
        out_shape=[jax.ShapeDtypeStruct((out_rows, width), jnp.bfloat16)] * task_count
        + [jax.ShapeDtypeStruct((8, width), jnp.float32)],
        compiler_params=pltpu.CompilerParams(vmem_limit_bytes=vmem_bytes),
        cost_estimate=task_cost(task_count, row_count, keys, width),
        name="attend_second",
    )(parents, place, queries, *operands)
    return outs[:-1], (outs[-1],)


def own_kernel(
    group_size, score_scale, place_ref, query_ref, key_ref, value_ref, out_ref, level_ref, score_ref
):
    token_count = key_ref.shape[1]
    _, row_count, width = query_ref.shape

    def mask_of(tile):
        row = tile * row_tile + lax.broadcasted_iota(jnp.int32, (row_tile, token_count), 0)
        column = lax.broadcasted_iota(jnp.int32, (row_tile, token_count), 1)
        return column * group_size <= row

    attend_task(
        tile_reader(query_ref),
        putter(out_ref.at[0]),
        row_count,
        width,
        [(lambda: key_ref[0], lambda: value_ref[0])],
        mask_of,
        level_ref,
        score_ref,
        score_scale,
    )


def attend_own(queries, depth, keys, values, place, score_scale):
    head_count, token_count, width = keys.shape
    row_count = queries.shape[2]

    def head_spec(rows):
        return pl.BlockSpec(
            (1, rows, width), lambda step, place: (lax.bitwise_xor(place[0], step), 0, 0)
        )

    return pl.pallas_call(
        functools.partial(own_kernel, row_count // token_count, score_scale),
        grid_spec=pltpu.PrefetchScalarGridSpec(
            num_scalar_prefetch=1,
            grid=(head_count,),
            in_specs=[
                pl.BlockSpec(
                    (1, None, row_count, width),
                    lambda step, place: (lax.bitwise_xor(place[0], step), depth, 0, 0),
                ),
                head_spec(token_count),
                head_spec(token_count),
            ],
            out_specs=pl.BlockSpec(
                (1, row_count + stat_rows, width), lambda step, place: (step, 0, 0)
            ),
            scratch_shapes=task_scratch(row_count, width, token_count),
        ),
        out_shape=jax.ShapeDtypeStruct((head_count, row_count + stat_rows, width), jnp.bfloat16),
        compiler_params=pltpu.CompilerParams(vmem_limit_bytes=vmem_bytes),
        cost_estimate=task_cost(head_count, row_count, token_count, width),
        name="attend_own",
    )(place, queries, keys, values)


def merge_kernel(head_count, group_size, part_count, place_ref, *refs):
    part_refs, own_ref = refs[:part_count], refs[part_count]
    refs = refs[part_count + 1 :]
    stat_refs, own_stat_ref = refs[:part_count], refs[part_count]
    out_ref, mixed_ref = refs[-2:]
    token_tile, _, lanes = out_ref.shape[1:]
    stat_tile = token_tile * group_size // lanes
    step = pl.program_id(0)
    picks = eye(lanes)
    ones = jnp.ones((2 * lanes, lanes), jnp.bfloat16)
    span = stat_rows // 4

    for far in range(head_count):
        head = lax.bitwise_xor(place_ref[0], far)
        sources = [part_refs[place] for place in range(far, part_count, head_count)]
        sources.append(own_ref.at[far])
        stats = [stat_refs[place][...] for place in range(far, part_count, head_count)]
        stats.append(own_stat_ref[far])
        stats = [stat.astype(jnp.float32) for stat in stats]
        level = [
            stat[:span] + stat[span : 2 * span] + stat[2 * span : 3 * span] for stat in stats
        ]
        top = functools.reduce(jnp.maximum, level)
        shares = [jnp.exp(one - top) for one in level]
        total = functools.reduce(jnp.add, shares)
        shares = [one / total for one in shares]
        lines = []
        for share in shares:
            for piece in range(stat_tile):
                chosen = (
                    lax.broadcasted_iota(jnp.int32, share.shape, 0) == step * stat_tile + piece
                )
                lines.append(jnp.sum(jnp.where(chosen, share, 0.0), axis=0, keepdims=True))
        scales = []
        for line in lines:
            high = line.astype(jnp.bfloat16).astype(jnp.float32)
            scales.append(
                jnp.concatenate(
                    [
                        jnp.where(picks, portion, 0.0).astype(jnp.bfloat16)
                        for portion in (high, line - high)
                    ],
                    1,
                )
            )
        columns = jnp.dot(
            jnp.concatenate(scales, 0), ones, preferred_element_type=jnp.float32
        )
        mixed = None
        rows = stat_tile * lanes
        for place, source in enumerate(sources):
            block = source[...].astype(jnp.float32) * columns[place * rows : (place + 1) * rows]
            mixed = block if mixed is None else mixed + block
        mixed_ref[
            :, pl.ds(pl.multiple_of(head * group_size, group_size), group_size), :
        ] = mixed.reshape(token_tile, group_size, lanes)
    out_ref[0] = mixed_ref[...].astype(out_ref.dtype)


def merge(parts, own, place, token_count, before=()):
    head_count, out_rows, width = own.shape
    row_count = out_rows - stat_rows
    group_size = row_count // token_count
    token_tile = 64
    rows = token_tile * group_size
    stat_block = row_count // stat_rows
    query_heads = head_count * group_size

    def specs(size, index):
        flat = pl.BlockSpec((size, width), lambda step, place: (index(step), 0))
        whole = pl.BlockSpec((head_count, size, width), lambda step, place: (0, index(step), 0))
        return [flat] * len(parts) + [whole]

    return pl.pallas_call(
        functools.partial(merge_kernel, head_count, group_size, len(parts)),
        grid_spec=pltpu.PrefetchScalarGridSpec(
            num_scalar_prefetch=1,
            grid=(token_count // token_tile,),
            in_specs=specs(rows, lambda step: step)
            + specs(stat_rows, lambda step: stat_block)
            + [pl.BlockSpec(memory_space=pl.ANY)] * len(before),
            out_specs=pl.BlockSpec(
                (1, token_tile, query_heads, width), lambda step, place: (0, step, 0, 0)
            ),
            scratch_shapes=[pltpu.VMEM((token_tile, query_heads, width), jnp.float32)],
        ),
        out_shape=jax.ShapeDtypeStruct((1, token_count, query_heads, width), jnp.bfloat16),
        compiler_params=pltpu.CompilerParams(vmem_limit_bytes=vmem_bytes),
        cost_estimate=pl.CostEstimate(
            flops=4 * (len(parts) + head_count) * row_count * width,
            bytes_accessed=4 * (len(parts) + head_count) * row_count * width,
            transcendentals=0,
        ),
        name="merge_parts",
    )(place, *parts, own, *parts, own, *before)


def local(
    queries_one,
    keys_one,
    values_one,
    queries_two,
    keys_two,
    values_two,
    cache_keys,
    cache_values,
    paths,
    parents,
    positions,
):
    here_index = lax.axis_index("node")
    peer_count = lax.axis_size("node")
    block_count, token_count, head_count, width = cache_keys.shape
    per_peer = paths.shape[1] // peer_count
    copies = peer_count // head_count
    score_scale = width ** (-0.5)
    my_head = here_index % head_count
    my_group = here_index // head_count
    part_rows = per_peer * token_count
    places = [
        jnp.stack([my_head, lax.bitwise_xor(my_group, apart), here_index])
        for apart in range(copies)
    ]

    def swap(array, apart):
        return lax.ppermute(array, "node", [(node, node ^ apart) for node in range(peer_count)])

    cosine, sine_part = rotary_tables(positions[:, 0], width)
    send = turn_queries(queries_one, queries_two, cosine, sine_part, head_count, copies)
    got = lax.all_to_all(send, "node", split_axis=0, concat_axis=0, tiled=True)
    key_rot_one = rotary(keys_one[0], cosine[0], sine_part[0])
    key_rot_two = rotary(keys_two[0], cosine[1], sine_part[1])

    block_index = local_blocks(paths, here_index, block_count, per_peer).reshape(-1)
    chunks = []
    before = (send,)
    for apart in range(1, copies):
        packed = pack(
            cache_keys, cache_values, block_index, places[apart], (), per_peer, before
        )
        chunks.append([packed[0]] + [swap(packed[far], far) for far in range(1, head_count)])
        before = (packed[0],)
    packed = pack(
        cache_keys,
        cache_values,
        block_index,
        places[0],
        (key_rot_one, values_one[0]),
        per_peer,
        before,
    )
    further = [packed[0]] + [swap(packed[far], far) for far in range(1, head_count)]
    nearer = [packed[head_count]] + [
        swap(packed[head_count + far], far) for far in range(1, head_count)
    ]

    own_one = attend_own(
        send,
        0,
        jnp.moveaxis(key_rot_one, 1, 0),
        jnp.moveaxis(values_one[0], 1, 0),
        places[0],
        score_scale,
    )
    own_two = attend_own(
        send,
        1,
        jnp.moveaxis(key_rot_two, 1, 0),
        jnp.moveaxis(values_two[0], 1, 0),
        places[0],
        score_scale,
    )

    half = head_count // 2
    parts_one, parts_two = [None] * peer_count, [None] * peer_count

    def send_home(parts, tasks, rows):
        for task, row in zip(tasks, rows):
            parts[task] = swap(row, task) if task else row

    def first(sources, tasks, task_of, slot_of, before):
        rows, before = attend_first(
            got,
            sources,
            places[0],
            task_of,
            slot_of,
            len(tasks),
            part_rows,
            score_scale,
            before,
        )
        send_home(parts_one, tasks, rows)
        return before

    def second(tasks, task_of, before):
        rows, before = attend_second(
            got,
            further,
            nearer,
            chunks,
            parents,
            places[0],
            task_of,
            len(tasks),
            part_rows,
            score_scale,
            before,
        )
        send_home(parts_two, tasks, rows)
        return before

    def far_slot(task, place):
        return lax.bitwise_xor(task % head_count, place[0])

    before = (own_one, own_two)
    for apart in range(1, copies):
        base = apart * head_count
        before = first(chunks[apart - 1], [base], lambda step: base, far_slot, before)
        before = first(
            chunks[apart - 1],
            list(range(base + 1, base + head_count)),
            lambda step: base + 1 + step,
            far_slot,
            before,
        )
    before = first(
        further,
        list(range(half, head_count)),
        lambda step: half + step,
        lambda task, place: task - half,
        before,
    )
    for apart in range(1, copies):
        base = apart * head_count
        before = second(
            list(range(base, base + head_count)), lambda step: base + step, before
        )
        before = (*before, *parts_one[base : base + head_count])
    before = first(
        nearer,
        list(range(1, half)) + [0],
        lambda step: (step + 1) % half,
        lambda task, place: task,
        (*before, *parts_one[half:head_count]),
    )
    before = second(
        list(range(1, head_count)),
        lambda step: step + 1,
        before,
    )
    before = second([0], lambda step: 0, before)
    before = (*before, *parts_two[head_count : head_count + 3])
    return (
        merge(parts_one, own_one, places[0], token_count, before),
        merge(parts_two, own_two, places[0], token_count),
    )


def solution(mesh):
    in_specs = (
        P(("group", "node"), None, "head", None),
        P(("group", "node"), None, "head", None),
        P(("group", "node"), None, "head", None),
        P(("group", "node"), None, "head", None),
        P(("group", "node"), None, "head", None),
        P(("group", "node"), None, "head", None),
        P(("group", "node"), None, "head", None),
        P(("group", "node"), None, "head", None),
        P("group", None),
        P("group"),
        P(None, ("group", "node"), None),
    )
    out_specs = (P(("group", "node"), None, "head", None), P(("group", "node"), None, "head", None))
    return jax.shard_map(
        local,
        mesh=mesh,
        in_specs=in_specs,
        out_specs=out_specs,
        check_vma=False,
    )
```

```python
import functools

import jax
import jax.numpy as jnp
from jax import lax
from jax.experimental import pallas as pl
from jax.experimental.pallas import tpu as pltpu
from jax.sharding import PartitionSpec as P

rope_theta = 500000.0
log2_e = 1.4426950408889634
stat_rows = 32
row_tile = 256
vmem_bytes = 56 * 1024 * 1024


def rotary_tables(positions, head_width):
    half_width = head_width // 2
    place = jnp.arange(head_width, dtype=jnp.int32)
    pair = (place % half_width).astype(jnp.float32)
    frequency = rope_theta ** (-(pair * 2.0) / head_width)
    angles = positions.astype(jnp.float32)[..., None] * frequency
    return jnp.cos(angles), jnp.where(place < half_width, -1.0, 1.0) * jnp.sin(angles)


def rotary(vector, cosine, signed_sine):
    widened = vector.astype(jnp.float32)
    swapped = jnp.roll(widened, widened.shape[-1] // 2, axis=-1)
    turned = widened * cosine[:, None, :] + swapped * signed_sine[:, None, :]
    return turned.astype(jnp.bfloat16)


def turn_kernel(head_count, copies, first_ref, second_ref, cosine_ref, sine_ref, out_ref):
    token_tile, query_heads, width = first_ref.shape[1:]
    group_size = query_heads // head_count
    rows = token_tile * group_size
    for depth, query_ref in enumerate((first_ref, second_ref)):
        widened = query_ref[0].astype(jnp.float32)
        swapped = pltpu.roll(widened.reshape(token_tile * query_heads, width), width // 2, 1)
        swapped = swapped.reshape(token_tile, query_heads, width)
        turned = widened * cosine_ref[depth][:, None, :] + swapped * sine_ref[depth][:, None, :]
        for head in range(head_count):
            turned_head = turned[:, head * group_size : (head + 1) * group_size, :]
            turned_head = turned_head.reshape(rows, width).astype(jnp.bfloat16)
            for copy in range(copies):
                out_ref[copy * head_count + head, depth] = turned_head


def turn_queries(queries_one, queries_two, cosine, sine_part, head_count, copies):
    _, token_count, query_heads, width = queries_one.shape
    token_tile = 64
    rows = token_tile * query_heads // head_count
    query_spec = pl.BlockSpec((1, token_tile, query_heads, width), lambda step: (0, step, 0, 0))
    table_spec = pl.BlockSpec((2, token_tile, width), lambda step: (0, step, 0))
    return pl.pallas_call(
        functools.partial(turn_kernel, head_count, copies),
        grid=(token_count // token_tile,),
        in_specs=[query_spec, query_spec, table_spec, table_spec],
        out_specs=pl.BlockSpec(
            (head_count * copies, 2, rows, width), lambda step: (0, 0, step, 0)
        ),
        out_shape=jax.ShapeDtypeStruct(
            (head_count * copies, 2, token_count * query_heads // head_count, width), jnp.bfloat16
        ),
        compiler_params=pltpu.CompilerParams(vmem_limit_bytes=vmem_bytes),
        cost_estimate=pl.CostEstimate(
            flops=8 * queries_one.size, bytes_accessed=12 * queries_one.size, transcendentals=0
        ),
        name="turn_queries",
    )(queries_one, queries_two, cosine, sine_part)


def local_blocks(paths, here_index, per_owner, per_peer):
    is_local = paths // per_owner == here_index
    slot_rank = jnp.cumsum(is_local.astype(jnp.int32), axis=1) - 1
    slot_range = jnp.arange(per_peer, dtype=jnp.int32)
    selected = jnp.logical_and(
        is_local[:, :, None], slot_rank[:, :, None] == slot_range[None, None, :]
    )
    return jnp.sum(jnp.where(selected, (paths % per_owner)[:, :, None], 0), axis=1)


def pack_kernel(per_peer, head_count, token_count, near, index_ref, place_ref, *refs):
    key_refs = refs[:per_peer]
    value_refs = refs[per_peer : 2 * per_peer]
    new_refs = refs[2 * per_peer : 2 * per_peer + 2] if near else ()
    out_refs, wide = refs[-1 - head_count * (2 if near else 1) : -1], refs[-1]
    step = pl.program_id(0)
    mine = place_ref[0]
    span_rows = 2 * per_peer * token_count
    half = head_count // 2

    def spread(rows, put):
        wide[...] = rows.astype(jnp.float32)
        for far in range(head_count):
            head = lax.bitwise_xor(mine, far)
            picked = wide[pl.ds(head, token_count, stride=head_count), :]
            put(far, head, picked.astype(jnp.bfloat16))

    for which, source_refs in enumerate((key_refs, value_refs)):
        for slot, source in enumerate(source_refs):
            offset = (which * per_peer + slot) * token_count

            def put(far, head, rows):
                if not near:
                    start = pl.multiple_of(step * span_rows + offset, token_count)
                    out_refs[far][pl.ds(start, token_count), :] = rows
                    return
                apart = lax.bitwise_xor(step, head)
                start = pl.multiple_of((apart % half) * span_rows + offset, token_count)

                @pl.when(apart >= half)
                def _():
                    out_refs[far][pl.ds(start, token_count), :] = rows

                @pl.when(apart < half)
                def _():
                    out_refs[head_count + far][pl.ds(start, token_count), :] = rows

            spread(source[0], put)
    if near:

        @pl.when(step == 0)
        def _():
            for which, source in enumerate(new_refs):
                start = half * span_rows + which * token_count

                def put(far, head, rows):
                    out_refs[far][start : start + token_count, :] = rows

                spread(source[...], put)


def pack(cache_keys, cache_values, block_index, place, new_rows, per_peer, before=()):
    block_count, token_count, head_count, width = cache_keys.shape
    flat_keys = cache_keys.reshape(block_count, token_count * head_count, width)
    flat_values = cache_values.reshape(block_count, token_count * head_count, width)
    span_rows = 2 * per_peer * token_count
    near = bool(new_rows)
    half_rows = head_count // 2 * span_rows
    out_rows = half_rows + 2 * token_count if near else head_count * span_rows
    shapes = [(out_rows, width)] * head_count
    if near:
        shapes += [(half_rows, width)] * head_count

    def block_spec(slot):
        return pl.BlockSpec(
            (1, token_count * head_count, width),
            lambda step, index, place: (
                index[(place[1] * head_count + step) * per_peer + slot],
                0,
                0,
            ),
        )

    def whole_spec(shape):
        return pl.BlockSpec(shape, lambda step, index, place: (0,) * len(shape))

    cache_specs = [block_spec(slot) for slot in range(per_peer)]
    new_spec = pl.BlockSpec((token_count * head_count, width), lambda step, index, place: (0, 0))
    operands = [flat_keys] * per_peer + [flat_values] * per_peer
    operands += [row.reshape(token_count * head_count, width) for row in new_rows]
    return pl.pallas_call(
        functools.partial(pack_kernel, per_peer, head_count, token_count, near),
        grid_spec=pltpu.PrefetchScalarGridSpec(
            num_scalar_prefetch=2,
            grid=(head_count,),
            in_specs=cache_specs
            + cache_specs
            + [new_spec] * len(new_rows)
            + [pl.BlockSpec(memory_space=pl.ANY)] * len(before),
            out_specs=[whole_spec(shape) for shape in shapes],
            scratch_shapes=[pltpu.VMEM((token_count * head_count, width), jnp.float32)],
        ),
        out_shape=[jax.ShapeDtypeStruct(shape, jnp.bfloat16) for shape in shapes],
        compiler_params=pltpu.CompilerParams(vmem_limit_bytes=vmem_bytes),
        cost_estimate=pl.CostEstimate(
            flops=0, bytes_accessed=4 * head_count * out_rows * width, transcendentals=0
        ),
        name="pack_rows",
    )(block_index, place, *operands, *before)


def eye(size):
    return lax.broadcasted_iota(jnp.int32, (size, size), 0) == lax.broadcasted_iota(
        jnp.int32, (size, size), 1
    )


def product(left, right):
    return lax.dot_general(
        left, right, (((1,), (1,)), ((), ())), preferred_element_type=jnp.float32
    )


def fold_lanes(array, width, operation):
    pieces = [array[:, start : start + width] for start in range(0, array.shape[1], width)]
    while len(pieces) > 1:
        pieces = [
            operation(*pieces[start : start + 2]) if start + 1 < len(pieces) else pieces[start]
            for start in range(0, len(pieces), 2)
        ]
    return pieces[0]


def attend_task(query_of, put, row_count, width, parts, mask_of, level_ref, score_ref, score_scale):
    tile_count = row_count // row_tile

    def make_scores(tile):
        query = query_of(tile)
        top, start = None, 0
        for place, (keys, _) in enumerate(parts):
            scores = product(query, keys())
            if mask_of is not None and place == len(parts) - 1:
                scores = jnp.where(mask_of(tile), scores, -1e30)
            size = scores.shape[1]
            score_ref[tile % 2, :, start : start + size] = scores
            start += size
            folded = fold_lanes(scores, width, jnp.maximum)
            top = folded if top is None else jnp.maximum(top, folded)
        return jnp.max(top, axis=-1, keepdims=True)

    picks = eye(width)
    row_max = make_scores(0)
    for tile in range(tile_count):
        next_max = make_scores(tile + 1) if tile + 1 < tile_count else None
        total, mixture, start = None, None, 0
        for _, values in parts:
            value_rows = values()
            size = value_rows.shape[0]
            scores = score_ref[tile % 2, :, start : start + size]
            start += size
            weights = jnp.exp2((scores - row_max) * (score_scale * log2_e))
            folded = fold_lanes(weights, width, jnp.add)
            total = folded if total is None else total + folded
            mixed = jnp.dot(
                weights.astype(jnp.bfloat16), value_rows, preferred_element_type=jnp.float32
            )
            mixture = mixed if mixture is None else mixture + mixed
        total = jnp.sum(total, axis=-1, keepdims=True)
        put(tile * row_tile, (mixture / total).astype(jnp.bfloat16))
        level = row_max * score_scale + jnp.log(total)
        for piece in range(row_tile // width):
            line = jnp.where(picks, level[piece * width : (piece + 1) * width], 0.0)
            row = tile * (row_tile // width) + piece
            level_ref[row : row + 1, :] = jnp.sum(line, axis=0, keepdims=True)
        row_max = next_max
    levels = level_ref[...]
    high = levels.astype(jnp.bfloat16).astype(jnp.float32)
    middle = (levels - high).astype(jnp.bfloat16).astype(jnp.float32)
    low = levels - high - middle
    stats = jnp.concatenate([high, middle, low, jnp.zeros_like(levels)], 0)
    put(row_count, stats.astype(jnp.bfloat16))


def putter(out_ref):
    def put(start, rows):
        out_ref[start : start + rows.shape[0], :] = rows

    return put


def hand_out(stage_ref, out_refs):
    for far, out_ref in enumerate(out_refs):

        @pl.when(pl.program_id(0) == far)
        def _():
            out_ref[...] = stage_ref[...]


def tile_reader(query_ref):
    return lambda tile: query_ref[0, tile * row_tile : (tile + 1) * row_tile, :]


def task_scratch(row_count, width, key_count):
    return [
        pltpu.VMEM((row_count // width, width), jnp.float32),
        pltpu.VMEM((2, row_tile, key_count), jnp.float32),
    ]


def task_cost(task_count, row_count, key_count, width):
    return pl.CostEstimate(
        flops=4 * task_count * row_count * key_count * width,
        bytes_accessed=4 * task_count * (row_count + key_count) * width,
        transcendentals=task_count * row_count * key_count,
    )


def first_kernel(source_count, task_count, part_rows, score_scale, place_ref, query_ref, *refs):
    source_refs = refs[:source_count]
    out_refs = refs[-4 - task_count : -4]
    mark_ref, level_ref, score_ref, stage_ref = refs[-4:]
    _, row_count, width = query_ref.shape
    mark_ref[...] = jnp.zeros_like(mark_ref)
    parts = [
        (
            functools.partial(lambda ref: ref[0:part_rows, :], ref),
            functools.partial(lambda ref: ref[part_rows : 2 * part_rows, :], ref),
        )
        for ref in source_refs
    ]
    attend_task(
        tile_reader(query_ref),
        putter(stage_ref),
        row_count,
        width,
        parts,
        None,
        level_ref,
        score_ref,
        score_scale,
    )
    hand_out(stage_ref, out_refs)


def attend_first(queries, sources, place, task_of, slot_of, task_count, part_rows, score_scale, before):
    _, _, row_count, width = queries.shape
    out_rows = row_count + stat_rows
    span_rows = 2 * part_rows
    source_spec = pl.BlockSpec(
        (span_rows, width), lambda step, place: (slot_of(task_of(step), place), 0)
    )
    outs = pl.pallas_call(
        functools.partial(first_kernel, len(sources), task_count, part_rows, score_scale),
        grid_spec=pltpu.PrefetchScalarGridSpec(
            num_scalar_prefetch=1,
            grid=(task_count,),
            in_specs=[
                pl.BlockSpec(
                    (1, None, row_count, width),
                    lambda step, place: (lax.bitwise_xor(place[2], task_of(step)), 0, 0, 0),
                )
            ]
            + [source_spec] * len(sources)
            + [pl.BlockSpec(memory_space=pl.ANY)] * len(before),
            out_specs=[pl.BlockSpec((out_rows, width), lambda step, place: (0, 0))] * task_count
            + [pl.BlockSpec((8, width), lambda step, place: (0, 0))],
            scratch_shapes=task_scratch(row_count, width, len(sources) * part_rows)
            + [pltpu.VMEM((out_rows, width), jnp.bfloat16)],
        ),
        out_shape=[jax.ShapeDtypeStruct((out_rows, width), jnp.bfloat16)] * task_count
        + [jax.ShapeDtypeStruct((8, width), jnp.float32)],
        compiler_params=pltpu.CompilerParams(vmem_limit_bytes=vmem_bytes),
        cost_estimate=task_cost(task_count, row_count, len(sources) * part_rows, width),
        name="attend_first",
    )(place, queries, *sources, *before)
    return outs[:-1], (outs[-1],)


def second_kernel(
    head_count, far_chunks, task_of, task_count, part_rows, score_scale, parent_ref, place_ref, query_ref, *refs
):
    further_refs = refs[:head_count]
    nearer_refs = refs[head_count : 2 * head_count]
    far_refs = refs[2 * head_count : (2 + far_chunks) * head_count]
    out_refs = refs[-8 - task_count : -8]
    mark_ref, level_ref, score_ref, stage_ref, held, fresh = refs[-8:-2]
    semaphores, fresh_semaphores = refs[-2:]
    _, row_count, width = query_ref.shape
    span_rows = 2 * part_rows
    token_count = fresh.shape[1] // 2
    half = head_count // 2
    step = pl.program_id(0)
    node = place_ref[2]
    mark_ref[...] = jnp.zeros_like(mark_ref)

    def parent_at(number):
        return parent_ref[lax.bitwise_xor(node, task_of(number))]

    def fetch(number):
        parent = parent_at(number)
        apart = lax.bitwise_xor(parent, node)

        def bring(chosen, source_refs, slot):
            @pl.when(chosen)
            def _():
                rows = pl.ds(pl.multiple_of(slot * span_rows, span_rows), span_rows)
                for source in range(head_count):
                    pltpu.make_async_copy(
                        source_refs[source].at[rows],
                        held.at[number % 2, source],
                        semaphores.at[number % 2, source],
                    ).start()

        bring(apart < half, nearer_refs, apart)
        bring(jnp.logical_and(apart >= half, apart < head_count), further_refs, apart - half)
        for chunk in range(far_chunks):
            bring(
                apart // head_count == chunk + 1,
                far_refs[chunk * head_count : (chunk + 1) * head_count],
                parent % head_count,
            )

    @pl.when(step == 0)
    def _():
        fetch(0)
        fresh_copies = [
            pltpu.make_async_copy(
                further_refs[source].at[pl.ds(half * span_rows, 2 * token_count)],
                fresh.at[source],
                fresh_semaphores.at[source],
            )
            for source in range(head_count)
        ]
        for copy in fresh_copies:
            copy.start()
        for copy in fresh_copies:
            copy.wait()

    @pl.when(step + 1 < task_count)
    def _():
        fetch(step + 1)

    slot = step % 2
    for source in range(head_count):
        pltpu.make_async_copy(
            further_refs[source].at[pl.ds(0, span_rows)],
            held.at[slot, source],
            semaphores.at[slot, source],
        ).wait()
    apart = lax.bitwise_xor(parent_at(step), node)
    place = jnp.where(apart < head_count, apart, 0)
    parts = [
        (
            functools.partial(lambda source: held[slot, source, 0:part_rows, :], source),
            functools.partial(lambda source: held[slot, source, part_rows:span_rows, :], source),
        )
        for source in range(head_count)
    ]
    parts.append(
        (
            lambda: fresh[place, 0:token_count, :],
            lambda: fresh[place, token_count : 2 * token_count, :],
        )
    )

    def mask_of(tile):
        return jnp.broadcast_to(apart < head_count, (row_tile, token_count))

    attend_task(
        tile_reader(query_ref),
        putter(stage_ref),
        row_count,
        width,
        parts,
        mask_of,
        level_ref,
        score_ref,
        score_scale,
    )
    hand_out(stage_ref, out_refs)


def attend_second(
    queries, further, nearer, far, parents, place, task_of, task_count, part_rows, score_scale, before
):
    _, _, row_count, width = queries.shape
    head_count = len(further)
    span_rows = 2 * part_rows
    fresh_rows = further[0].shape[0] - head_count // 2 * span_rows
    keys = head_count * part_rows + fresh_rows // 2
    out_rows = row_count + stat_rows
    operands = [row for rows in (further, nearer, *far) for row in rows] + [*before]
    outs = pl.pallas_call(
        functools.partial(
            second_kernel, head_count, len(far), task_of, task_count, part_rows, score_scale
        ),
        grid_spec=pltpu.PrefetchScalarGridSpec(
            num_scalar_prefetch=2,
            grid=(task_count,),
            in_specs=[
                pl.BlockSpec(
                    (1, None, row_count, width),
                    lambda step, parent, place: (lax.bitwise_xor(place[2], task_of(step)), 1, 0, 0),
                )
            ]
            + [pl.BlockSpec(memory_space=pl.ANY)] * len(operands),
            out_specs=[pl.BlockSpec((out_rows, width), lambda step, parent, place: (0, 0))]
            * task_count
            + [pl.BlockSpec((8, width), lambda step, parent, place: (0, 0))],
            scratch_shapes=task_scratch(row_count, width, keys)
            + [
                pltpu.VMEM((out_rows, width), jnp.bfloat16),
                pltpu.VMEM((2, head_count, span_rows, width), jnp.bfloat16),
                pltpu.VMEM((head_count, fresh_rows, width), jnp.bfloat16),
                pltpu.SemaphoreType.DMA((2, head_count)),
                pltpu.SemaphoreType.DMA((head_count,)),
            ],
        ),
        out_shape=[jax.ShapeDtypeStruct((out_rows, width), jnp.bfloat16)] * task_count
        + [jax.ShapeDtypeStruct((8, width), jnp.float32)],
        compiler_params=pltpu.CompilerParams(vmem_limit_bytes=vmem_bytes),
        cost_estimate=task_cost(task_count, row_count, keys, width),
        name="attend_second",
    )(parents, place, queries, *operands)
    return outs[:-1], (outs[-1],)


def own_kernel(
    group_size, score_scale, place_ref, query_ref, key_ref, value_ref, out_ref, level_ref, score_ref
):
    token_count = key_ref.shape[1]
    _, row_count, width = query_ref.shape

    def mask_of(tile):
        row = tile * row_tile + lax.broadcasted_iota(jnp.int32, (row_tile, token_count), 0)
        column = lax.broadcasted_iota(jnp.int32, (row_tile, token_count), 1)
        return column * group_size <= row

    attend_task(
        tile_reader(query_ref),
        putter(out_ref.at[0]),
        row_count,
        width,
        [(lambda: key_ref[0], lambda: value_ref[0])],
        mask_of,
        level_ref,
        score_ref,
        score_scale,
    )


def attend_own(queries, depth, keys, values, place, score_scale):
    head_count, token_count, width = keys.shape
    row_count = queries.shape[2]

    def head_spec(rows):
        return pl.BlockSpec(
            (1, rows, width), lambda step, place: (lax.bitwise_xor(place[0], step), 0, 0)
        )

    return pl.pallas_call(
        functools.partial(own_kernel, row_count // token_count, score_scale),
        grid_spec=pltpu.PrefetchScalarGridSpec(
            num_scalar_prefetch=1,
            grid=(head_count,),
            in_specs=[
                pl.BlockSpec(
                    (1, None, row_count, width),
                    lambda step, place: (lax.bitwise_xor(place[0], step), depth, 0, 0),
                ),
                head_spec(token_count),
                head_spec(token_count),
            ],
            out_specs=pl.BlockSpec(
                (1, row_count + stat_rows, width), lambda step, place: (step, 0, 0)
            ),
            scratch_shapes=task_scratch(row_count, width, token_count),
        ),
        out_shape=jax.ShapeDtypeStruct((head_count, row_count + stat_rows, width), jnp.bfloat16),
        compiler_params=pltpu.CompilerParams(vmem_limit_bytes=vmem_bytes),
        cost_estimate=task_cost(head_count, row_count, token_count, width),
        name="attend_own",
    )(place, queries, keys, values)


def merge_kernel(head_count, group_size, part_count, place_ref, *refs):
    part_refs, own_ref = refs[:part_count], refs[part_count]
    refs = refs[part_count + 1 :]
    stat_refs, own_stat_ref = refs[:part_count], refs[part_count]
    out_ref, mixed_ref = refs[-2:]
    token_tile, _, lanes = out_ref.shape[1:]
    stat_tile = token_tile * group_size // lanes
    step = pl.program_id(0)
    picks = eye(lanes)
    ones = jnp.ones((2 * lanes, lanes), jnp.bfloat16)
    span = stat_rows // 4

    for far in range(head_count):
        head = lax.bitwise_xor(place_ref[0], far)
        sources = [part_refs[place] for place in range(far, part_count, head_count)]
        sources.append(own_ref.at[far])
        stats = [stat_refs[place][...] for place in range(far, part_count, head_count)]
        stats.append(own_stat_ref[far])
        stats = [stat.astype(jnp.float32) for stat in stats]
        level = [
            stat[:span] + stat[span : 2 * span] + stat[2 * span : 3 * span] for stat in stats
        ]
        top = functools.reduce(jnp.maximum, level)
        shares = [jnp.exp(one - top) for one in level]
        total = functools.reduce(jnp.add, shares)
        shares = [one / total for one in shares]
        lines = []
        for share in shares:
            for piece in range(stat_tile):
                chosen = (
                    lax.broadcasted_iota(jnp.int32, share.shape, 0) == step * stat_tile + piece
                )
                lines.append(jnp.sum(jnp.where(chosen, share, 0.0), axis=0, keepdims=True))
        scales = []
        for line in lines:
            high = line.astype(jnp.bfloat16).astype(jnp.float32)
            scales.append(
                jnp.concatenate(
                    [
                        jnp.where(picks, portion, 0.0).astype(jnp.bfloat16)
                        for portion in (high, line - high)
                    ],
                    1,
                )
            )
        columns = jnp.dot(
            jnp.concatenate(scales, 0), ones, preferred_element_type=jnp.float32
        )
        mixed = None
        rows = stat_tile * lanes
        for place, source in enumerate(sources):
            block = source[...].astype(jnp.float32) * columns[place * rows : (place + 1) * rows]
            mixed = block if mixed is None else mixed + block
        mixed_ref[
            :, pl.ds(pl.multiple_of(head * group_size, group_size), group_size), :
        ] = mixed.reshape(token_tile, group_size, lanes)
    out_ref[0] = mixed_ref[...].astype(out_ref.dtype)


def merge(parts, own, place, token_count, before=()):
    head_count, out_rows, width = own.shape
    row_count = out_rows - stat_rows
    group_size = row_count // token_count
    token_tile = 64
    rows = token_tile * group_size
    stat_block = row_count // stat_rows
    query_heads = head_count * group_size

    def specs(size, index):
        flat = pl.BlockSpec((size, width), lambda step, place: (index(step), 0))
        whole = pl.BlockSpec((head_count, size, width), lambda step, place: (0, index(step), 0))
        return [flat] * len(parts) + [whole]

    return pl.pallas_call(
        functools.partial(merge_kernel, head_count, group_size, len(parts)),
        grid_spec=pltpu.PrefetchScalarGridSpec(
            num_scalar_prefetch=1,
            grid=(token_count // token_tile,),
            in_specs=specs(rows, lambda step: step)
            + specs(stat_rows, lambda step: stat_block)
            + [pl.BlockSpec(memory_space=pl.ANY)] * len(before),
            out_specs=pl.BlockSpec(
                (1, token_tile, query_heads, width), lambda step, place: (0, step, 0, 0)
            ),
            scratch_shapes=[pltpu.VMEM((token_tile, query_heads, width), jnp.float32)],
        ),
        out_shape=jax.ShapeDtypeStruct((1, token_count, query_heads, width), jnp.bfloat16),
        compiler_params=pltpu.CompilerParams(vmem_limit_bytes=vmem_bytes),
        cost_estimate=pl.CostEstimate(
            flops=4 * (len(parts) + head_count) * row_count * width,
            bytes_accessed=4 * (len(parts) + head_count) * row_count * width,
            transcendentals=0,
        ),
        name="merge_parts",
    )(place, *parts, own, *parts, own, *before)


def local(
    queries_one,
    keys_one,
    values_one,
    queries_two,
    keys_two,
    values_two,
    cache_keys,
    cache_values,
    paths,
    parents,
    positions,
):
    here_index = lax.axis_index("node")
    peer_count = lax.axis_size("node")
    block_count, token_count, head_count, width = cache_keys.shape
    per_peer = paths.shape[1] // peer_count
    copies = peer_count // head_count
    score_scale = width ** (-0.5)
    my_head = here_index % head_count
    my_group = here_index // head_count
    part_rows = per_peer * token_count
    places = [
        jnp.stack([my_head, lax.bitwise_xor(my_group, apart), here_index])
        for apart in range(copies)
    ]

    def swap(array, apart):
        return lax.ppermute(array, "node", [(node, node ^ apart) for node in range(peer_count)])

    cosine, sine_part = rotary_tables(positions[:, 0], width)
    send = turn_queries(queries_one, queries_two, cosine, sine_part, head_count, copies)
    got = lax.all_to_all(send, "node", split_axis=0, concat_axis=0, tiled=True)
    key_rot_one = rotary(keys_one[0], cosine[0], sine_part[0])
    key_rot_two = rotary(keys_two[0], cosine[1], sine_part[1])

    block_index = local_blocks(paths, here_index, block_count, per_peer).reshape(-1)
    chunks = []
    before = (send,)
    for apart in range(1, copies):
        packed = pack(
            cache_keys, cache_values, block_index, places[apart], (), per_peer, before
        )
        chunks.append([packed[0]] + [swap(packed[far], far) for far in range(1, head_count)])
        before = (packed[0],)
    packed = pack(
        cache_keys,
        cache_values,
        block_index,
        places[0],
        (key_rot_one, values_one[0]),
        per_peer,
        before,
    )
    further = [packed[0]] + [swap(packed[far], far) for far in range(1, head_count)]
    nearer = [packed[head_count]] + [
        swap(packed[head_count + far], far) for far in range(1, head_count)
    ]

    own_one = attend_own(
        send,
        0,
        jnp.moveaxis(key_rot_one, 1, 0),
        jnp.moveaxis(values_one[0], 1, 0),
        places[0],
        score_scale,
    )
    own_two = attend_own(
        send,
        1,
        jnp.moveaxis(key_rot_two, 1, 0),
        jnp.moveaxis(values_two[0], 1, 0),
        places[0],
        score_scale,
    )

    half = head_count // 2
    parts_one, parts_two = [None] * peer_count, [None] * peer_count

    def send_home(parts, tasks, rows):
        for task, row in zip(tasks, rows):
            parts[task] = swap(row, task) if task else row

    def first(sources, tasks, task_of, slot_of, before):
        rows, before = attend_first(
            got,
            sources,
            places[0],
            task_of,
            slot_of,
            len(tasks),
            part_rows,
            score_scale,
            before,
        )
        send_home(parts_one, tasks, rows)
        return before

    def second(tasks, task_of, before):
        rows, before = attend_second(
            got,
            further,
            nearer,
            chunks,
            parents,
            places[0],
            task_of,
            len(tasks),
            part_rows,
            score_scale,
            before,
        )
        send_home(parts_two, tasks, rows)
        return before

    def far_slot(task, place):
        return lax.bitwise_xor(task % head_count, place[0])

    before = (own_one, own_two)
    for apart in range(1, copies):
        base = apart * head_count
        before = first(chunks[apart - 1], [base], lambda step: base, far_slot, before)
        before = first(
            chunks[apart - 1],
            list(range(base + 1, base + head_count)),
            lambda step: base + 1 + step,
            far_slot,
            before,
        )
    before = first(
        further,
        list(range(half, head_count)),
        lambda step: half + step,
        lambda task, place: task - half,
        before,
    )
    for apart in range(1, copies):
        base = apart * head_count
        before = second(
            list(range(base, base + head_count)), lambda step: base + step, before
        )
        before = (*before, *parts_one[base : base + head_count])
    before = second(list(range(1, head_count)), lambda step: step + 1, before)
    before = first(
        nearer,
        list(range(1, half)) + [0],
        lambda step: (step + 1) % half,
        lambda task, place: task,
        (*before, *parts_one[half:head_count]),
    )
    before = second([0], lambda step: 0, before)
    before = (*before, *parts_two[head_count : head_count + 3])
    return (
        merge(parts_one, own_one, places[0], token_count, before),
        merge(parts_two, own_two, places[0], token_count),
    )


def solution(mesh):
    in_specs = (
        P(("group", "node"), None, "head", None),
        P(("group", "node"), None, "head", None),
        P(("group", "node"), None, "head", None),
        P(("group", "node"), None, "head", None),
        P(("group", "node"), None, "head", None),
        P(("group", "node"), None, "head", None),
        P(("group", "node"), None, "head", None),
        P(("group", "node"), None, "head", None),
        P("group", None),
        P("group"),
        P(None, ("group", "node"), None),
    )
    out_specs = (P(("group", "node"), None, "head", None), P(("group", "node"), None, "head", None))
    return jax.shard_map(
        local,
        mesh=mesh,
        in_specs=in_specs,
        out_specs=out_specs,
        check_vma=False,
    )
```
